256 devices in a mesh: gx: 16 (over x_lo, y, core), gy: 16 (over z, x_hi).
Axes of the slice: x: 4 (x_hi: 2, x_lo: 2; x = x_hi * 2 + x_lo), y: 4, z: 8, core: 2. Of those that a mesh axis runs over, the one named last changes fastest.
Arguments:
- offsets: float32 [3, 32, 32, 4, 128], P(None, 'gx', 'gy'), may hold values from 0 to 1
- charges: float32 [32, 32, 4, 128], P('gx', 'gy'), may hold values from -0.12 to 0.12
- counts: int32 [32, 32, 4], P('gx', 'gy'), may hold values from 16 to 128, as said below
- c2e_leaf_up: float32 [256, 256], replicated, may hold values from -0.09375 to 0.09375
- c2e_leaf_down: float32 [256, 256], replicated, may hold values from -0.09375 to 0.09375
- c2e_top_up: float32 [256, 256], replicated, may hold values from -0.046875 to 0.046875
- c2e_top_down: float32 [256, 256], replicated, may hold values from -0.046875 to 0.046875
Outputs:
- potential: float32 [32, 32, 4, 128], P('gx', 'gy')
The draws below stay inside these ranges and needn't reach their ends.
Inputs may be any that keep to these rules, and one draw needn't show every extreme that they name: The first counts slots of a leaf box hold its particles, the rest are padding.
All inputs are finite; a program needn't handle non-finite values.
Results may differ from the reference program's by a relative error of at most 0.0003.
Values sent between devices are 32-bit elements; how exact they have to be, the bound alone decides.
A program may use at most 64 MiB of HBM per device.

```python
import jax
import jax.numpy as jnp
from jax import lax

S = 128
NE = 256
BZ = 4
PZ = 2
NBX = 32
NBY = 32
N_GX = 16
N_GY = 16


def draw_counts(key, part):
    raw_counts = jax.random.randint(key, (NBX, NBY, BZ), S // 8, 2 * S)
    return jnp.minimum(raw_counts, S).astype(jnp.int32)


def level_of(key, dims, cuts, least, largest):
    level = 1.0
    for dim, blocks in cuts:
        heights = jax.random.uniform(jax.random.fold_in(jax.random.fold_in(key, 6), dim), (blocks,), jnp.float32, least / len(cuts), largest / len(cuts))
        level = level * jnp.repeat(jnp.exp(heights), dims[dim] // blocks).reshape((-1,) + (1,) * (len(dims) - 1 - dim))
    return level


def normal_values(key, extent, scale, reach, split=(), kind=jnp.bfloat16):
    factor_of = level_of(key, extent, split, -0.22, 0.18) if split else 1.0
    drawn = jax.random.normal(key, extent, jnp.float32) * scale * factor_of
    return jnp.minimum(jnp.maximum(drawn, -reach), reach).astype(kind)


def setup_inputs(seed: int = 0) -> dict:
    splits = jax.random.split(jax.random.key(seed), 8)
    return {
        "offsets": jnp.clip(1.0 * jax.random.uniform(splits[0], (3, NBX, NBY, BZ, S), jnp.float32) ** level_of(splits[0], (3, NBX, NBY, BZ, S), ((1, 16), (2, 16)), -0.2, 0.2), 0.0, 1.0),
        "charges": normal_values(splits[1], (NBX, NBY, BZ, S), 0.02, 0.12, ((0, 16), (1, 16)), jnp.float32),
        "counts": draw_counts(jax.random.fold_in(splits[7], 71), 0),
        "c2e_leaf_up": normal_values(splits[3], (NE, NE), (16 * NE) ** -0.5, 0.09375, (), jnp.float32),
        "c2e_leaf_down": normal_values(splits[4], (NE, NE), (16 * NE) ** -0.5, 0.09375, (), jnp.float32),
        "c2e_top_up": normal_values(splits[5], (NE, NE), (64 * NE) ** -0.5, 0.046875, (), jnp.float32),
        "c2e_top_down": normal_values(splits[6], (NE, NE), (64 * NE) ** -0.5, 0.046875, (), jnp.float32),
    }


softening_sq = 0.0004
golden_turn = 2.399963229728653
highest = lax.Precision.HIGHEST

def sphere(point_count):
    middle = jnp.arange(point_count).astype(jnp.float32) + 0.5
    height = 1.0 - 2.0 * middle / point_count
    radial = jnp.sqrt(jnp.maximum(1.0 - height * height, 0.0))
    angle_turn = middle * golden_turn
    return jnp.stack([radial * jnp.cos(angle_turn), radial * jnp.sin(angle_turn), height])

def point_sum(targets, sources, weights):
    delta_x = targets[0][..., :, None] - sources[0][..., None, :]
    delta_y = targets[1][..., :, None] - sources[1][..., None, :]
    delta_z = targets[2][..., :, None] - sources[2][..., None, :]
    kernel = lax.rsqrt(delta_x * delta_x + delta_y * delta_y + delta_z * delta_z + softening_sq)
    return lax.optimization_barrier(jnp.sum(kernel * weights[..., None, :], axis=-1))

def translation(unit_sphere, shift_x, shift_y, shift_z, radius):
    delta_x = radius * (unit_sphere[0][:, None] - unit_sphere[0][None, :]) - shift_x[..., None, None]
    delta_y = radius * (unit_sphere[1][:, None] - unit_sphere[1][None, :]) - shift_y[..., None, None]
    delta_z = radius * (unit_sphere[2][:, None] - unit_sphere[2][None, :]) - shift_z[..., None, None]
    return lax.rsqrt(delta_x * delta_x + delta_y * delta_y + delta_z * delta_z + softening_sq)

def child_points(unit_sphere):
    centre = jnp.arange(2).astype(jnp.float32) + 0.5
    point_count = unit_sphere.shape[1]
    box_shape = (2, 2, 2, point_count)
    along_x = jnp.broadcast_to(centre[:, None, None, None] + 0.9 * unit_sphere[0], box_shape)
    along_y = jnp.broadcast_to(centre[None, :, None, None] + 0.9 * unit_sphere[1], box_shape)
    along_z = jnp.broadcast_to(centre[None, None, :, None] + 0.9 * unit_sphere[2], box_shape)
    return jnp.stack([along_x, along_y, along_z]).reshape(3, 8 * point_count)

def reference(offsets, charges, counts, c2e_leaf_up, c2e_leaf_down, c2e_top_up, c2e_top_down):
    unit_sphere = sphere(NE)
    slot_index = jnp.arange(S)
    weights = jnp.where(slot_index < counts[..., None], charges, 0.0)
    packed = jnp.concatenate([offsets, weights[None]], axis=0)
    leaf_check_pts = 0.5 + 1.8 * unit_sphere

    def leaf_up_row(column):
        row_block = lax.dynamic_index_in_dim(packed, column, 1, keepdims=False)
        return point_sum(leaf_check_pts[:, None, None, :], row_block[:3], row_block[3])
    leaf_check = lax.map(leaf_up_row, jnp.arange(NBX))
    leaf_eq = jnp.einsum('ec,xyzc->xyze', c2e_leaf_up, leaf_check, precision=highest)
    children = child_points(unit_sphere)
    grouped = leaf_eq.reshape(N_GX, 2, N_GY, 2, PZ, 2, NE).transpose(0, 2, 4, 1, 3, 5, 6).reshape(N_GX, N_GY, PZ, 8 * NE)
    parent_check_pts = 1.0 + 3.6 * unit_sphere

    def parent_up_row(block_row):
        return point_sum(parent_check_pts[:, None, None, :], children[:, None, None, :], block_row)
    parent_check = lax.map(parent_up_row, grouped)
    parent_eq = jnp.einsum('ec,xymc->xyme', c2e_top_up, parent_check, precision=highest)
    layer_float = jnp.arange(PZ).astype(jnp.float32)
    depth_pairs = 2.0 * (layer_float[None, :] - layer_float[:, None])
    pair_ones = jnp.ones((PZ, PZ), jnp.float32)

    def far_step(running, combo):
        off_x = combo // N_GY - N_GX // 2
        off_y = combo % N_GY - N_GY // 2
        moved = jnp.roll(parent_eq, (-off_x, -off_y), axis=(0, 1))
        keep = ((jnp.abs(off_x) > 1) | (jnp.abs(off_y) > 1)).astype(jnp.float32)
        matrices = translation(unit_sphere, 2.0 * off_x.astype(jnp.float32) * pair_ones, 2.0 * off_y.astype(jnp.float32) * pair_ones, depth_pairs, 1.8)
        term = jnp.einsum('tsce,xyse->xytc', matrices, moved, precision=highest)
        return (running + keep * term, None)
    far_check, _ = lax.scan(far_step, jnp.zeros((N_GX, N_GY, PZ, NE), jnp.float32), jnp.arange(N_GX * N_GY))
    parent_local = jnp.einsum('ec,xymc->xyme', c2e_top_down, far_check, precision=highest)
    framed = jnp.pad(leaf_eq, ((0, 0), (0, 0), (3, 3), (0, 0)))
    parity_x = jnp.arange(NBX) % 2
    parity_y = jnp.arange(NBY) % 2
    layer_index = jnp.arange(BZ)
    depth_shift = jnp.arange(7) - 3
    seven_ones = jnp.ones((7,), jnp.float32)

    def list_step(running, combo):
        shift_x = combo // 7 - 3
        shift_y = combo % 7 - 3
        moved = jnp.roll(framed, (-shift_x, -shift_y), axis=(0, 1))
        stacked = jnp.stack([moved[:, :, depth:depth + BZ] for depth in range(7)])
        valid_x = (parity_x + shift_x >= -2) & (parity_x + shift_x <= 3)
        valid_y = (parity_y + shift_y >= -2) & (parity_y + shift_y <= 3)
        valid_z = (layer_index[None, :] + depth_shift[:, None] >= 0) & (layer_index[None, :] + depth_shift[:, None] <= BZ - 1)
        far_enough = (jnp.abs(shift_x) > 1) | (jnp.abs(shift_y) > 1) | (jnp.abs(depth_shift) > 1)
        keep = valid_x[None, :, None, None] & valid_y[None, None, :, None] & valid_z[:, None, None, :] & far_enough[:, None, None, None]
        matrices = translation(unit_sphere, shift_x.astype(jnp.float32) * seven_ones, shift_y.astype(jnp.float32) * seven_ones, depth_shift.astype(jnp.float32), 0.9)
        sources = jnp.where(keep[..., None], stacked, 0.0)
        return (running + jnp.einsum('zce,zxyke->xykc', matrices, sources, precision=highest), None)
    leaf_down_check, _ = lax.scan(list_step, jnp.zeros((NBX, NBY, BZ, NE), jnp.float32), jnp.arange(49))
    leaf_local = jnp.einsum('ec,xyzc->xyze', c2e_leaf_down, leaf_down_check, precision=highest)
    spread_local = jnp.repeat(jnp.repeat(jnp.repeat(parent_local, 2, axis=0), 2, axis=1), 2, axis=2)
    beside_all = jnp.pad(packed, ((0, 0), (1, 1), (1, 1), (0, 0), (0, 0)), mode='wrap')
    beside_all = jnp.pad(beside_all, ((0, 0), (0, 0), (0, 0), (1, 1), (0, 0)))
    diagonal = jnp.arange(S)[:, None] == jnp.arange(S)[None, :]
    leaf_down_pts = 0.5 + 1.8 * unit_sphere
    parent_down_pts = 1.0 + 3.6 * unit_sphere
    float_parity_y = (jnp.arange(NBY) % 2).astype(jnp.float32)
    float_parity_z = (jnp.arange(BZ) % 2).astype(jnp.float32)

    def finish_row(column):
        own_block = lax.dynamic_index_in_dim(packed, column, 1, keepdims=False)
        near = jnp.zeros((NBY, BZ, S), jnp.float32)
        for stencil in range(27):
            move_x = stencil // 9 - 1
            move_y = stencil // 3 % 3 - 1
            move_z = stencil % 3 - 1
            slab_row = lax.dynamic_index_in_dim(beside_all, column + 1 + move_x, 1, keepdims=False)
            source = slab_row[:, 1 + move_y:1 + move_y + NBY, 1 + move_z:1 + move_z + BZ]
            delta_x = own_block[0][..., :, None] - source[0][..., None, :] - float(move_x)
            delta_y = own_block[1][..., :, None] - source[1][..., None, :] - float(move_y)
            delta_z = own_block[2][..., :, None] - source[2][..., None, :] - float(move_z)
            kernel = lax.rsqrt(delta_x * delta_x + delta_y * delta_y + delta_z * delta_z + softening_sq)
            if stencil == 13:
                kernel = jnp.where(diagonal, 0.0, kernel)
            near = near + lax.optimization_barrier(jnp.sum(kernel * source[3][..., None, :], axis=-1))
        local_leaf = lax.dynamic_index_in_dim(leaf_local, column, 0, keepdims=False)
        local_parent = lax.dynamic_index_in_dim(spread_local, column, 0, keepdims=False)
        leaf_far = point_sum(own_block[:3], leaf_down_pts[:, None, None, :], local_leaf)
        column_parity = (column % 2).astype(jnp.float32)
        in_parent = jnp.stack([column_parity + own_block[0], float_parity_y[:, None, None] + own_block[1], float_parity_z[None, :, None] + own_block[2]])
        parent_far = point_sum(in_parent, parent_down_pts[:, None, None, :], local_parent)
        return near + leaf_far + parent_far
    total = lax.map(finish_row, jnp.arange(NBX))
    return jnp.where(slot_index < counts[..., None], total, 0.0)
```

```python
import functools

import jax
import jax.numpy as jnp
import numpy as np
from jax import lax
from jax.experimental import pallas as pl
from jax.experimental.pallas import tpu as pltpu
from jax.sharding import PartitionSpec as P

SOFT = 0.0004
F32 = jnp.float32
BF16 = jnp.bfloat16
HIGHEST = lax.Precision.HIGHEST
MESH = pl.DeviceIdType.MESH


def sphere_points(count):
    middle = np.arange(count).astype(np.float32) + np.float32(0.5)
    height = (np.float32(1.0) - np.float32(2.0) * middle / np.float32(count)).astype(np.float32)
    radial = np.sqrt(np.maximum(np.float32(1.0) - height * height, np.float32(0.0)))
    turn = (middle * np.float32(2.399963229728653)).astype(np.float32)
    cos = np.cos(turn.astype(np.float64)).astype(np.float32)
    sin = np.sin(turn.astype(np.float64)).astype(np.float32)
    return np.stack([radial * cos, radial * sin, height]).astype(np.float32)


def split(value):
    high = value.astype(BF16)
    low = (value - high.astype(F32)).astype(BF16)
    return high, low


def bdot(a, b):
    return jnp.dot(a, b, preferred_element_type=F32)


def dot_t(a, b):
    return lax.dot_general(
        a, b, (((1,), (1,)), ((), ())), precision=HIGHEST, preferred_element_type=F32
    )


def leaf_task(a):
    return a // 2 - 3, a % 2


def body(
    nx,
    ny,
    counts_ref,
    off_ref,
    chg_ref,
    u_ref,
    ut_ref,
    cl_up,
    cl_down,
    ct_up,
    ct_down,
    out_ref,
    halo,
    tables,
    k_leaf,
    k_parent,
    up_hi,
    up_lo,
    leaf_send,
    leaf_recv,
    par_send,
    par_recv,
    rs_send,
    rs_recv,
    shifted,
    par_ring,
    m_hi,
    m_lo,
    l_hi,
    l_lo,
    near_acc,
    turned_ref,
    halo_ssem,
    halo_rsem,
    leaf_ssem,
    leaf_rsem,
    par_ssem,
    par_rsem,
    rs_ssem,
    rs_rsem,
):
    a = lax.axis_index("gx")
    b = lax.axis_index("gy")
    lane128 = lax.broadcasted_iota(jnp.int32, (4, 128), 1)

    for px in range(2):
        for py in range(2):
            cell = halo.at[1 + px, 1 + py]
            for comp in range(3):
                cell[4 * comp : 4 * comp + 4, :] = off_ref[comp, px, py]
            for k in range(4):
                row = chg_ref[px, py, k : k + 1, :]
                cell[12 + k : 13 + k, :] = jnp.where(
                    lane128[0:1] < counts_ref[px, py, k], row, 0.0
                )

    sides = [(sx, sy) for sx in (-1, 0, 1) for sy in (-1, 0, 1) if (sx, sy) != (0, 0)]

    def halo_copy(index):
        sx, sy = sides[index]
        src_x = pl.ds(1, 2) if sx == 0 else pl.ds(2 if sx == 1 else 1, 1)
        src_y = pl.ds(1, 2) if sy == 0 else pl.ds(2 if sy == 1 else 1, 1)
        dst_x = pl.ds(1, 2) if sx == 0 else pl.ds(0 if sx == 1 else 3, 1)
        dst_y = pl.ds(1, 2) if sy == 0 else pl.ds(0 if sy == 1 else 3, 1)
        return pltpu.make_async_remote_copy(
            src_ref=halo.at[src_x, src_y],
            dst_ref=halo.at[dst_x, dst_y],
            send_sem=halo_ssem.at[index],
            recv_sem=halo_rsem.at[index],
            device_id=(lax.rem(a + sx + nx, nx), lax.rem(b + sy + ny, ny)),
            device_id_type=MESH,
        )

    for index in range(8):
        halo_copy(index).start()

    for chunk in range(8):
        rows = pl.ds(32 * chunk, 32)
        total = jnp.zeros((32, 256), F32)
        for comp in range(3):
            diff = 0.9 * (u_ref[comp : comp + 1, :] - ut_ref[rows, comp : comp + 1])
            tables[1 + comp, rows, :] = -2.0 * diff
            total = total + diff * diff
        tables[0, rows, :] = total

    def child_chunk(chunk, carry):
        rows = pl.ds(pl.multiple_of(32 * chunk, 32), 32)
        base = jnp.full((32, 256), 0.1875 + SOFT / 4, F32)
        half = []
        for comp in range(3):
            diff = 1.8 * u_ref[comp : comp + 1, :] - 0.45 * ut_ref[rows, comp : comp + 1]
            base = base + diff * diff
            half.append(0.5 * diff)
        for child in range(8):
            value = base
            for comp, bit in enumerate((child // 4, child // 2 % 2, child % 2)):
                value = value + half[comp] if bit == 0 else value - half[comp]
            high, low = split(lax.rsqrt(value))
            up_hi[child, rows, :] = high
            up_lo[child, rows, :] = low
        return carry

    lax.fori_loop(0, 8, child_chunk, 0)

    centre = [0.5 + 1.8 * u_ref[comp : comp + 1, :] for comp in range(3)]
    checks = []
    for px in range(2):
        for py in range(2):
            turned = jnp.transpose(halo[1 + px, 1 + py])
            for k in range(4):
                box = (px * 2 + py) * 4 + k
                total = jnp.full((128, 256), SOFT, F32)
                for comp in range(3):
                    diff = centre[comp] - turned[:, 4 * comp + k : 4 * comp + k + 1]
                    total = total + diff * diff
                kernel = lax.rsqrt(total)
                k_leaf[box] = kernel
                weight = turned[:, 12 + k : 13 + k]
                checks.append(jnp.sum(kernel * weight, axis=0, keepdims=True))
    leaf_check = jnp.concatenate(checks, axis=0)
    leaf_eq = dot_t(leaf_check, cl_up[...])
    for px in range(2):
        for py in range(2):
            first = (px * 2 + py) * 4
            leaf_send[py, 4 * px : 4 * px + 4, :] = leaf_eq[first : first + 4, :]

    def leaf_route(target, py):
        dy, _ = leaf_task(target)
        src = py + dy
        valid = (target < 14) & (src >= -2) & (src <= 3)
        row = (src + 4) // 2 - 2
        return valid, row, (src + 4) % 2

    def leaf_copy(target, py):
        valid, row, src_py = leaf_route(target, py)
        to_b = lax.rem(b - row + ny, ny)
        copy = pltpu.make_async_remote_copy(
            src_ref=leaf_send.at[src_py],
            dst_ref=leaf_recv.at[a, py],
            send_sem=leaf_ssem.at[target, py],
            recv_sem=leaf_rsem.at[a, py],
            device_id=(target, to_b),
            device_id_type=MESH,
        )
        self_copy = (target == a) & (to_b == b)
        return valid, self_copy, src_py, copy

    def leaf_start(target, carry):
        for py in range(2):
            valid, self_copy, src_py, copy = leaf_copy(target, py)

            @pl.when(valid & jnp.logical_not(self_copy))
            def _():
                copy.start()

            @pl.when(valid & self_copy)
            def _():
                leaf_recv[a, py] = leaf_send[src_py]

        return carry

    lax.fori_loop(0, nx, leaf_start, 0)

    eq_hi, eq_lo = split(leaf_eq)
    both = jnp.concatenate([eq_hi, eq_lo], axis=0)
    row16 = lax.broadcasted_iota(jnp.int32, (16, 256), 0)
    rows_sum = jnp.zeros((16, 256), F32)
    for child in range(8):
        first = bdot(both, up_hi[child])
        term = first[:16] + first[16:] + bdot(eq_hi, up_lo[child])
        mine = ((row16 // 4) == (child // 2)) & ((row16 % 2) == (child % 2))
        rows_sum = jnp.where(mine, term, rows_sum)
    upper = (row16 % 4) >= 2
    check0 = 0.5 * jnp.sum(jnp.where(upper, 0.0, rows_sum), axis=0, keepdims=True)
    check1 = 0.5 * jnp.sum(jnp.where(upper, rows_sum, 0.0), axis=0, keepdims=True)
    row8 = lax.broadcasted_iota(jnp.int32, (8, 256), 0)
    parent_check = jnp.where(row8 == 0, check0, jnp.where(row8 == 1, check1, 0.0))
    par_send[...] = dot_t(parent_check, ct_up[...])

    def par_copy(target):
        to_b = lax.rem(b - target + nx // 2 + ny, ny)
        copy = pltpu.make_async_remote_copy(
            src_ref=par_send,
            dst_ref=par_recv.at[a],
            send_sem=par_ssem.at[target],
            recv_sem=par_rsem.at[a],
            device_id=(target, to_b),
            device_id_type=MESH,
        )
        return (target == a) & (to_b == b), copy

    def par_start(target, carry):
        self_copy, copy = par_copy(target)

        @pl.when(jnp.logical_not(self_copy))
        def _():
            copy.start()

        @pl.when(self_copy)
        def _():
            par_recv[a] = par_send[...]

        return carry

    lax.fori_loop(0, nx, par_start, 0)

    sub8 = lax.broadcasted_iota(jnp.int32, (8, 128), 0)
    lane8 = lax.broadcasted_iota(jnp.int32, (8, 128), 1)

    def near_column(fx, fy):
        turned_ref[...] = jnp.transpose(halo[fx, fy])
        columns = [
            (px, py)
            for px in range(2)
            for py in range(2)
            if abs(px + 1 - fx) <= 1 and abs(py + 1 - fy) <= 1
        ]
        pairs = [(px, py, k) for px, py in columns for k in range(4)]

        def tile(t, carry):
            sums = list(carry)
            block = turned_ref[pl.ds(pl.multiple_of(8 * t, 8), 8), :]
            for ks in range(4):
                source = [
                    jnp.broadcast_to(block[:, 4 * comp + ks : 4 * comp + ks + 1], (8, 128))
                    for comp in range(4)
                ]
                for slot, (px, py, k) in enumerate(pairs):
                    if abs(k - ks) > 1:
                        continue
                    shift = (px + 1 - fx, py + 1 - fy, k - ks)
                    total = None
                    for comp in range(3):
                        row = halo[1 + px, 1 + py, 4 * comp + k : 4 * comp + k + 1, :]
                        if shift[comp]:
                            row = row + float(shift[comp])
                        diff = row - source[comp]
                        total = diff * diff + SOFT if total is None else total + diff * diff
                    kernel = lax.rsqrt(total)
                    if shift == (0, 0, 0):
                        kernel = jnp.where(lane8 == sub8 + 8 * t, 0.0, kernel)
                    sums[slot] = sums[slot] + kernel * source[3]
            return tuple(sums)

        start = tuple(near_acc[(px * 2 + py) * 4 + k] for px, py, k in pairs)
        done = lax.fori_loop(0, 16, tile, start)
        for slot, (px, py, k) in enumerate(pairs):
            near_acc[(px * 2 + py) * 4 + k] = done[slot]

    near_acc[...] = jnp.zeros_like(near_acc)
    for fx in (1, 2):
        for fy in (1, 2):
            near_column(fx, fy)

    for px in range(2):
        for py in range(2):
            turned = jnp.transpose(halo[1 + px, 1 + py])
            for k in range(4):
                box = (px * 2 + py) * 4 + k
                total = jnp.full((128, 256), SOFT / 4, F32)
                for comp, bit in enumerate((px, py, k % 2)):
                    place = 0.5 * turned[:, 4 * comp + k : 4 * comp + k + 1] + 0.5 * bit
                    diff = centre[comp] - place
                    total = total + diff * diff
                k_parent[box] = lax.rsqrt(total)

    def par_wait(source, carry):
        from_b = lax.rem(b + a - nx // 2 + ny, ny)
        self_copy = (source == a) & (from_b == b)
        arrived = pltpu.make_async_remote_copy(
            src_ref=par_send,
            dst_ref=par_recv.at[source],
            send_sem=par_ssem.at[source],
            recv_sem=par_rsem.at[source],
            device_id=(lax.rem(a + 1, nx), b),
            device_id_type=MESH,
        )

        @pl.when(jnp.logical_not(self_copy))
        def _():
            arrived.wait_recv()

        return carry

    lax.fori_loop(0, nx, par_wait, 0)
    for source in range(nx):
        for layer in range(2):
            par_ring[layer, source : source + 1, :] = par_recv[source, layer : layer + 1, :]

    oy = a - nx // 2
    oy_f = oy.astype(F32)

    def far_step(index, carry):
        acc0, acc1 = carry
        ox = index - nx // 2
        ox_f = ox.astype(F32)
        keep = (ox > 1) | (ox < -1) | (oy > 1) | (oy < -1)
        const = ox_f * ox_f + oy_f * oy_f + SOFT / 4
        for chunk in range(8):
            rows = pl.ds(32 * chunk, 32)
            flat = tables[0, rows, :] + ox_f * tables[1, rows, :] + oy_f * tables[2, rows, :]
            flat = flat + const
            lift = tables[3, rows, :]
            for slot, value in enumerate((flat + 1.0 - lift, flat, flat + 1.0 + lift)):
                high, low = split(jnp.where(keep, lax.rsqrt(value), 0.0))
                m_hi[slot, rows, :] = high
                m_lo[slot, rows, :] = low
        turn = lax.rem(nx + nx // 2 - index, nx)
        p0h, p0l = split(pltpu.roll(par_ring[0], turn, 0))
        p1h, p1l = split(pltpu.roll(par_ring[1], turn, 0))
        same = bdot(jnp.concatenate([p0h, p1h, p0l, p1l], axis=0), m_hi[1])
        same2 = bdot(jnp.concatenate([p0h, p1h], axis=0), m_lo[1])
        up = bdot(jnp.concatenate([p1h, p1l], axis=0), m_hi[2])
        up2 = bdot(p1h, m_lo[2])
        down = bdot(jnp.concatenate([p0h, p0l], axis=0), m_hi[0])
        down2 = bdot(p0h, m_lo[0])
        acc0 = acc0 + ((same[0:16] + up[0:16]) + (same[32:48] + same2[0:16] + up[16:32] + up2))
        acc1 = acc1 + (
            (same[16:32] + down[0:16]) + (same[48:64] + same2[16:32] + down[16:32] + down2)
        )
        return acc0, acc1

    zero16 = jnp.zeros((16, 256), F32)
    far0, far1 = lax.fori_loop(0, nx, far_step, (zero16, zero16))
    for target in range(nx):
        rs_send[target, 2] = jnp.where(
            row8 == 0,
            0.5 * far0[target : target + 1, :],
            jnp.where(row8 == 1, 0.5 * far1[target : target + 1, :], 0.0),
        )

    dy, half_z = leaf_task(a)

    def leaf_wait(source, carry):
        for py in range(2):
            valid, row, src_py = leaf_route(a, py)
            self_copy = (source == a) & (row == 0)
            arrived = pltpu.make_async_remote_copy(
                src_ref=leaf_send.at[0],
                dst_ref=leaf_recv.at[source, py],
                send_sem=leaf_ssem.at[source, py],
                recv_sem=leaf_rsem.at[source, py],
                device_id=(lax.rem(a + 1, nx), b),
                device_id_type=MESH,
            )

            @pl.when(valid & jnp.logical_not(self_copy))
            def _():
                arrived.wait_recv()

        return carry

    lax.fori_loop(0, nx, leaf_wait, 0)

    @pl.when(dy == 3)
    def _():
        leaf_recv[:, 1] = jnp.zeros((nx, 8, 256), F32)

    @pl.when(dy == -3)
    def _():
        leaf_recv[:, 0] = jnp.zeros((nx, 8, 256), F32)

    for target in range(nx):
        rs_send[target, 0] = jnp.zeros((8, 256), F32)
        rs_send[target, 1] = jnp.zeros((8, 256), F32)

    @pl.when(a < 14)
    def _():
        for source in range(nx):
            low_py = leaf_recv[source, 0]
            high_py = leaf_recv[source, 1]
            first = row8 < 4
            shifted[0, 8 * source : 8 * source + 8, :] = jnp.where(
                first, low_py, pltpu.roll(high_py, 4, 0)
            )
            shifted[1, 8 * source : 8 * source + 8, :] = jnp.where(
                first, pltpu.roll(low_py, 4, 0), high_py
            )
        dy_f = dy.astype(F32)
        row128 = lax.broadcasted_iota(jnp.int32, (128, 256), 0) % 4

        def leaf_step(step, carry):
            dz = jnp.where(half_z == 0, step - 3, step + 1)

            @pl.when(dz <= 3)
            def _():
                dz_f = dz.astype(F32)
                beside = (dy >= -1) & (dy <= 1) & (dz >= -1) & (dz <= 1)
                const = dy_f * dy_f + dz_f * dz_f + SOFT
                for chunk in range(8):
                    rows = pl.ds(32 * chunk, 32)
                    base = tables[0, rows, :] + dy_f * tables[2, rows, :]
                    base = base + dz_f * tables[3, rows, :] + const
                    along = tables[1, rows, :]
                    for slot in range(7):
                        dx = slot - 3
                        value = base + (float(dx) * along + float(dx * dx)) if dx else base
                        kernel = lax.rsqrt(value)
                        if abs(dx) <= 1:
                            kernel = jnp.where(beside, 0.0, kernel)
                        high, low = split(kernel)
                        m_hi[slot, rows, :] = high
                        m_lo[slot, rows, :] = low
                inside = (row128 + dz >= 0) & (row128 + dz <= 3)
                turn = lax.rem(128 - dz, 128)
                for sx in range(2):
                    moved = jnp.where(inside, pltpu.roll(shifted[sx], turn, 0), 0.0)
                    for block in (-1, 0, 1):
                        if block == -1:
                            placed = jnp.concatenate([moved[120:], moved[:120]], axis=0)
                        elif block == 1:
                            placed = jnp.concatenate([moved[8:], moved[:8]], axis=0)
                        else:
                            placed = moved
                        slot = 2 * block + sx + 2
                        high, low = split(placed)
                        l_hi[slot] = high
                        l_lo[slot] = low
                for px in range(2):
                    total = jnp.zeros((128, 256), F32)
                    for slot in range(6):
                        matrix = slot + 1 - px
                        total = total + (
                            bdot(l_hi[slot], m_hi[matrix])
                            + (bdot(l_lo[slot], m_hi[matrix]) + bdot(l_hi[slot], m_lo[matrix]))
                        )
                    rs_send[:, px] = rs_send[:, px] + total.reshape(nx, 8, 256)

            return carry

        lax.fori_loop(0, 4, leaf_step, 0)

    def rs_copy(target):
        return pltpu.make_async_remote_copy(
            src_ref=rs_send.at[target],
            dst_ref=rs_recv.at[a],
            send_sem=rs_ssem.at[target],
            recv_sem=rs_rsem.at[a],
            device_id=(target, b),
            device_id_type=MESH,
        )

    def rs_start(step, carry):
        rs_copy(lax.rem(a + step, nx)).start()
        return carry

    lax.fori_loop(1, nx, rs_start, 0)
    rs_recv[a] = rs_send[a]

    for index in range(8):
        halo_copy(7 - index).wait_recv()
    for fx in range(4):
        for fy in range(4):
            if fx in (0, 3) or fy in (0, 3):
                near_column(fx, fy)

    def rs_wait(step, carry):
        source = lax.rem(a + step, nx)
        pltpu.make_async_remote_copy(
            src_ref=rs_send.at[source],
            dst_ref=rs_recv.at[source],
            send_sem=rs_ssem.at[source],
            recv_sem=rs_rsem.at[source],
            device_id=(source, b),
            device_id_type=MESH,
        ).wait_recv()
        return carry

    lax.fori_loop(1, nx, rs_wait, 0)
    sums = [jnp.zeros((8, 256), F32) for _ in range(3)]
    for source in range(nx):
        for part in range(3):
            sums[part] = sums[part] + rs_recv[source, part]

    leaf_local = dot_t(jnp.concatenate([sums[0], sums[1]], axis=0), cl_down[...])
    parent_local = 0.5 * dot_t(sums[2], ct_down[...])
    lanes = lax.broadcasted_iota(jnp.int32, (128, 128), 1)
    columns = jnp.zeros((128, 128), F32)
    for box in range(16):
        layer = (box % 4) // 2
        value = k_leaf[box] * leaf_local[box : box + 1, :]
        value = value + k_parent[box] * parent_local[layer : layer + 1, :]
        column = jnp.sum(value, axis=1, keepdims=True)
        columns = jnp.where(lanes == box, column, columns)
    flipped = jnp.transpose(columns)
    for px in range(2):
        for py in range(2):
            for k in range(4):
                box = (px * 2 + py) * 4 + k
                row = flipped[box : box + 1, :] + jnp.sum(near_acc[box], axis=0, keepdims=True)
                out_ref[px, py, k : k + 1, :] = jnp.where(
                    lane128[0:1] < counts_ref[px, py, k], row, 0.0
                )

    for index in range(8):
        halo_copy(index).wait_send()

    def drain(target, carry):
        for py in range(2):
            valid, self_copy, _, copy = leaf_copy(target, py)

            @pl.when(valid & jnp.logical_not(self_copy))
            def _():
                copy.wait_send()

        own, copy = par_copy(target)

        @pl.when(jnp.logical_not(own))
        def _():
            copy.wait_send()

        @pl.when(target != a)
        def _():
            rs_copy(target).wait_send()

        return carry

    lax.fori_loop(0, nx, drain, 0)


def shards(offsets, charges, counts, cl_up, cl_down, ct_up, ct_down):
    nx = lax.axis_size("gx")
    ny = lax.axis_size("gy")
    points = sphere_points(256)
    unit = np.zeros((8, 256), np.float32)
    unit[:3] = points
    unit_t = np.zeros((256, 8), np.float32)
    unit_t[:, :3] = points.T
    vmem = pl.BlockSpec(memory_space=pltpu.VMEM)
    dma = pltpu.SemaphoreType.DMA
    return pl.pallas_call(
        functools.partial(body, nx, ny),
        out_shape=jax.ShapeDtypeStruct(charges.shape, F32),
        in_specs=[pl.BlockSpec(memory_space=pltpu.SMEM)] + [vmem] * 8,
        out_specs=vmem,
        scratch_shapes=[
            pltpu.VMEM((4, 4, 16, 128), F32),
            pltpu.VMEM((4, 256, 256), F32),
            pltpu.VMEM((16, 128, 256), F32),
            pltpu.VMEM((16, 128, 256), F32),
            pltpu.VMEM((8, 256, 256), BF16),
            pltpu.VMEM((8, 256, 256), BF16),
            pltpu.VMEM((2, 8, 256), F32),
            pltpu.VMEM((nx, 2, 8, 256), F32),
            pltpu.VMEM((8, 256), F32),
            pltpu.VMEM((nx, 8, 256), F32),
            pltpu.VMEM((nx, 3, 8, 256), F32),
            pltpu.VMEM((nx, 3, 8, 256), F32),
            pltpu.VMEM((2, 8 * nx, 256), F32),
            pltpu.VMEM((2, nx, 256), F32),
            pltpu.VMEM((7, 256, 256), BF16),
            pltpu.VMEM((7, 256, 256), BF16),
            pltpu.VMEM((6, 8 * nx, 256), BF16),
            pltpu.VMEM((6, 8 * nx, 256), BF16),
            pltpu.VMEM((16, 8, 128), F32),
            pltpu.VMEM((128, 16), F32),
            dma((8,)),
            dma((8,)),
            dma((nx, 2)),
            dma((nx, 2)),
            dma((nx,)),
            dma((nx,)),
            dma((nx,)),
            dma((nx,)),
        ],
        compiler_params=pltpu.CompilerParams(
            has_side_effects=True, vmem_limit_bytes=48 * 1024 * 1024
        ),
        name="multipole",
    )(counts, offsets, charges, jnp.asarray(unit), jnp.asarray(unit_t), cl_up, cl_down, ct_up, ct_down)


def solution(mesh):
    return jax.shard_map(
        shards,
        mesh=mesh,
        in_specs=(
            P(None, "gx", "gy", None, None),
            P("gx", "gy", None, None),
            P("gx", "gy", None),
            P(),
            P(),
            P(),
            P(),
        ),
        out_specs=P("gx", "gy", None, None),
        check_vma=False,
    )
```

```python
import functools

import jax
import jax.numpy as jnp
import numpy as np
from jax import lax
from jax.experimental import pallas as pl
from jax.experimental.pallas import tpu as pltpu
from jax.sharding import PartitionSpec as P

SOFT = 0.0004
F32 = jnp.float32
BF16 = jnp.bfloat16
HIGHEST = lax.Precision.HIGHEST
MESH = pl.DeviceIdType.MESH
SIDES = [(sx, sy) for sx in (-1, 0, 1) for sy in (-1, 0, 1) if (sx, sy) != (0, 0)]


def sphere_points(count):
    middle = np.arange(count).astype(np.float32) + np.float32(0.5)
    height = (np.float32(1.0) - np.float32(2.0) * middle / np.float32(count)).astype(np.float32)
    radial = np.sqrt(np.maximum(np.float32(1.0) - height * height, np.float32(0.0)))
    turn = (middle * np.float32(2.399963229728653)).astype(np.float32)
    cos = np.cos(turn.astype(np.float64)).astype(np.float32)
    sin = np.sin(turn.astype(np.float64)).astype(np.float32)
    return np.stack([radial * cos, radial * sin, height]).astype(np.float32)


def split(value):
    high = value.astype(BF16)
    low = (value - high.astype(F32)).astype(BF16)
    return high, low


def bdot(a, b):
    return jnp.dot(a, b, preferred_element_type=F32)


def dot_t(a, b):
    return lax.dot_general(
        a, b, (((1,), (1,)), ((), ())), precision=HIGHEST, preferred_element_type=F32
    )


def leaf_task(a):
    return a // 2 - 3, a % 2


def body(
    nx,
    ny,
    counts_hbm,
    off_hbm,
    chg_hbm,
    u_hbm,
    ut_hbm,
    cl_up_hbm,
    cl_down_hbm,
    ct_up_hbm,
    ct_down_hbm,
    out_ref,
    counts_ref,
    off_ref,
    chg_ref,
    u_ref,
    ut_ref,
    cl_up,
    cl_down,
    ct_up,
    ct_down,
    in_sem,
    halo,
    tables,
    k_leaf,
    k_parent,
    up_hi,
    up_lo,
    leaf_send,
    leaf_recv,
    par_send,
    par_recv,
    rs_send,
    rs_recv,
    shifted,
    par_ring,
    m_hi,
    m_lo,
    l_hi,
    l_lo,
    near_acc,
    turned_ref,
    halo_ssem,
    halo_rsem,
    leaf_ssem,
    leaf_rsem,
    par_ssem,
    par_rsem,
    rs_ssem,
    rs_rsem,
):
    a = lax.axis_index("gx")
    b = lax.axis_index("gy")
    lane128 = lax.broadcasted_iota(jnp.int32, (4, 128), 1)

    fetches = [
        pltpu.make_async_copy(src, dst, in_sem.at[index])
        for index, (src, dst) in enumerate(
            (
                (counts_hbm, counts_ref),
                (off_hbm, off_ref),
                (chg_hbm, chg_ref),
                (u_hbm, u_ref),
                (ut_hbm, ut_ref),
                (cl_up_hbm, cl_up),
                (ct_up_hbm, ct_up),
                (cl_down_hbm, cl_down),
                (ct_down_hbm, ct_down),
            )
        )
    ]
    for fetch in fetches:
        fetch.start()

    barrier = pltpu.get_barrier_semaphore()

    def hello(to_a, to_b):
        pl.semaphore_signal(barrier, inc=1, device_id=(to_a, to_b), device_id_type=MESH)

    def hello_row(step, carry):
        hello(lax.rem(a + step, nx), b)
        return carry

    lax.fori_loop(1, nx, hello_row, 0)
    for sx, sy in SIDES:
        hello(lax.rem(a + sx + nx, nx), lax.rem(b + sy + ny, ny))
    task_dy, _ = leaf_task(a)
    leaf_row = jnp.where(task_dy > 0, 1, -1)
    far_b = lax.rem(b + a - nx // 2 + ny, ny)

    def hello_far(step, carry):
        to_a = lax.rem(a + step, nx)

        @pl.when((a < 14) & (task_dy != 0))
        def _():
            hello(to_a, lax.rem(b + leaf_row + ny, ny))

        @pl.when((to_a != a) | (far_b != b))
        def _():
            hello(to_a, far_b)

        return carry

    lax.fori_loop(0, nx, hello_far, 0)
    for fetch in fetches[:5]:
        fetch.wait()

    for px in range(2):
        for py in range(2):
            cell = halo.at[1 + px, 1 + py]
            for comp in range(3):
                cell[4 * comp : 4 * comp + 4, :] = off_ref[comp, px, py]
            for k in range(4):
                row = chg_ref[px, py, k : k + 1, :]
                cell[12 + k : 13 + k, :] = jnp.where(
                    lane128[0:1] < counts_ref[px, py, k], row, 0.0
                )

    def halo_copy(index):
        sx, sy = SIDES[index]
        src_x = pl.ds(1, 2) if sx == 0 else pl.ds(2 if sx == 1 else 1, 1)
        src_y = pl.ds(1, 2) if sy == 0 else pl.ds(2 if sy == 1 else 1, 1)
        dst_x = pl.ds(1, 2) if sx == 0 else pl.ds(0 if sx == 1 else 3, 1)
        dst_y = pl.ds(1, 2) if sy == 0 else pl.ds(0 if sy == 1 else 3, 1)
        return pltpu.make_async_remote_copy(
            src_ref=halo.at[src_x, src_y],
            dst_ref=halo.at[dst_x, dst_y],
            send_sem=halo_ssem.at[index],
            recv_sem=halo_rsem.at[index],
            device_id=(lax.rem(a + sx + nx, nx), lax.rem(b + sy + ny, ny)),
            device_id_type=MESH,
        )

    for chunk in range(8):
        rows = pl.ds(32 * chunk, 32)
        total = jnp.zeros((32, 256), F32)
        for comp in range(3):
            diff = 0.9 * (u_ref[comp : comp + 1, :] - ut_ref[rows, comp : comp + 1])
            tables[1 + comp, rows, :] = -2.0 * diff
            total = total + diff * diff
        tables[0, rows, :] = total

    def child_chunk(chunk, carry):
        rows = pl.ds(pl.multiple_of(32 * chunk, 32), 32)
        base = jnp.full((32, 256), 0.1875 + SOFT / 4, F32)
        half = []
        for comp in range(3):
            diff = 1.8 * u_ref[comp : comp + 1, :] - 0.45 * ut_ref[rows, comp : comp + 1]
            base = base + diff * diff
            half.append(0.5 * diff)
        for child in range(8):
            value = base
            for comp, bit in enumerate((child // 4, child // 2 % 2, child % 2)):
                value = value + half[comp] if bit == 0 else value - half[comp]
            high, low = split(lax.rsqrt(value))
            up_hi[child, rows, :] = high
            up_lo[child, rows, :] = low
        return carry

    lax.fori_loop(0, 8, child_chunk, 0)

    centre = [0.5 + 1.8 * u_ref[comp : comp + 1, :] for comp in range(3)]
    checks = []
    for px in range(2):
        for py in range(2):
            turned = jnp.transpose(halo[1 + px, 1 + py])
            for k in range(4):
                box = (px * 2 + py) * 4 + k
                total = jnp.full((128, 256), SOFT, F32)
                for comp in range(3):
                    diff = centre[comp] - turned[:, 4 * comp + k : 4 * comp + k + 1]
                    total = total + diff * diff
                kernel = lax.rsqrt(total)
                k_leaf[box] = kernel
                weight = turned[:, 12 + k : 13 + k]
                checks.append(jnp.sum(kernel * weight, axis=0, keepdims=True))
    leaf_check = jnp.concatenate(checks, axis=0)
    fetches[5].wait()
    leaf_eq = dot_t(leaf_check, cl_up[...])
    for px in range(2):
        for py in range(2):
            first = (px * 2 + py) * 4
            leaf_send[py, 4 * px : 4 * px + 4, :] = leaf_eq[first : first + 4, :]

    def leaf_route(target, py):
        dy, _ = leaf_task(target)
        src = py + dy
        valid = (target < 14) & (src >= -2) & (src <= 3)
        row = (src + 4) // 2 - 2
        return valid, row, (src + 4) % 2

    def leaf_copy(target, py):
        valid, row, src_py = leaf_route(target, py)
        to_b = lax.rem(b - row + ny, ny)
        copy = pltpu.make_async_remote_copy(
            src_ref=leaf_send.at[src_py],
            dst_ref=leaf_recv.at[a, py],
            send_sem=leaf_ssem.at[target, py],
            recv_sem=leaf_rsem.at[a, py],
            device_id=(target, to_b),
            device_id_type=MESH,
        )
        self_copy = (target == a) & (to_b == b)
        return valid, self_copy, src_py, copy

    def leaf_start(target, carry):
        for py in range(2):
            valid, self_copy, src_py, copy = leaf_copy(target, py)

            @pl.when(valid & jnp.logical_not(self_copy))
            def _():
                copy.start()

            @pl.when(valid & self_copy)
            def _():
                leaf_recv[a, py] = leaf_send[src_py]

        return carry

    pl.semaphore_wait(barrier, (nx - 1) + 8 + 12 + jnp.where(a == nx // 2, nx - 1, nx))
    lax.fori_loop(0, nx, leaf_start, 0)
    for index in range(8):
        halo_copy(index).start()

    eq_hi, eq_lo = split(leaf_eq)
    both = jnp.concatenate([eq_hi, eq_lo], axis=0)
    row16 = lax.broadcasted_iota(jnp.int32, (16, 256), 0)
    rows_sum = jnp.zeros((16, 256), F32)
    for child in range(8):
        first = bdot(both, up_hi[child])
        term = first[:16] + first[16:] + bdot(eq_hi, up_lo[child])
        mine = ((row16 // 4) == (child // 2)) & ((row16 % 2) == (child % 2))
        rows_sum = jnp.where(mine, term, rows_sum)
    upper = (row16 % 4) >= 2
    check0 = 0.5 * jnp.sum(jnp.where(upper, 0.0, rows_sum), axis=0, keepdims=True)
    check1 = 0.5 * jnp.sum(jnp.where(upper, rows_sum, 0.0), axis=0, keepdims=True)
    row8 = lax.broadcasted_iota(jnp.int32, (8, 256), 0)
    parent_check = jnp.where(row8 == 0, check0, jnp.where(row8 == 1, check1, 0.0))
    fetches[6].wait()
    par_send[...] = dot_t(parent_check, ct_up[...])

    def par_copy(target):
        to_b = lax.rem(b - target + nx // 2 + ny, ny)
        copy = pltpu.make_async_remote_copy(
            src_ref=par_send,
            dst_ref=par_recv.at[a],
            send_sem=par_ssem.at[target],
            recv_sem=par_rsem.at[a],
            device_id=(target, to_b),
            device_id_type=MESH,
        )
        return (target == a) & (to_b == b), copy

    def par_start(target, carry):
        self_copy, copy = par_copy(target)

        @pl.when(jnp.logical_not(self_copy))
        def _():
            copy.start()

        @pl.when(self_copy)
        def _():
            par_recv[a] = par_send[...]

        return carry

    lax.fori_loop(0, nx, par_start, 0)

    sub8 = lax.broadcasted_iota(jnp.int32, (8, 128), 0)
    lane8 = lax.broadcasted_iota(jnp.int32, (8, 128), 1)

    def near_column(fx, fy):
        turned_ref[...] = jnp.transpose(halo[fx, fy])
        columns = [
            (px, py)
            for px in range(2)
            for py in range(2)
            if abs(px + 1 - fx) <= 1 and abs(py + 1 - fy) <= 1
        ]
        pairs = [(px, py, k) for px, py in columns for k in range(4)]

        def tile(t, carry):
            sums = list(carry)
            block = turned_ref[pl.ds(pl.multiple_of(8 * t, 8), 8), :]
            for ks in range(4):
                source = [
                    jnp.broadcast_to(block[:, 4 * comp + ks : 4 * comp + ks + 1], (8, 128))
                    for comp in range(4)
                ]
                for slot, (px, py, k) in enumerate(pairs):
                    if abs(k - ks) > 1:
                        continue
                    shift = (px + 1 - fx, py + 1 - fy, k - ks)
                    total = None
                    for comp in range(3):
                        row = halo[1 + px, 1 + py, 4 * comp + k : 4 * comp + k + 1, :]
                        if shift[comp]:
                            row = row + float(shift[comp])
                        diff = row - source[comp]
                        total = diff * diff + SOFT if total is None else total + diff * diff
                    kernel = lax.rsqrt(total)
                    if shift == (0, 0, 0):
                        kernel = jnp.where(lane8 == sub8 + 8 * t, 0.0, kernel)
                    sums[slot] = sums[slot] + kernel * source[3]
            return tuple(sums)

        start = tuple(near_acc[(px * 2 + py) * 4 + k] for px, py, k in pairs)
        done = lax.fori_loop(0, 16, tile, start)
        for slot, (px, py, k) in enumerate(pairs):
            near_acc[(px * 2 + py) * 4 + k] = done[slot]

    near_acc[...] = jnp.zeros_like(near_acc)
    for fx in (1, 2):
        for fy in (1, 2):
            near_column(fx, fy)

    for px in range(2):
        for py in range(2):
            turned = jnp.transpose(halo[1 + px, 1 + py])
            for k in range(4):
                box = (px * 2 + py) * 4 + k
                total = jnp.full((128, 256), SOFT / 4, F32)
                for comp, bit in enumerate((px, py, k % 2)):
                    place = 0.5 * turned[:, 4 * comp + k : 4 * comp + k + 1] + 0.5 * bit
                    diff = centre[comp] - place
                    total = total + diff * diff
                k_parent[box] = lax.rsqrt(total)

    def par_wait(source, carry):
        from_b = lax.rem(b + a - nx // 2 + ny, ny)
        self_copy = (source == a) & (from_b == b)
        arrived = pltpu.make_async_remote_copy(
            src_ref=par_send,
            dst_ref=par_recv.at[source],
            send_sem=par_ssem.at[source],
            recv_sem=par_rsem.at[source],
            device_id=(lax.rem(a + 1, nx), b),
            device_id_type=MESH,
        )

        @pl.when(jnp.logical_not(self_copy))
        def _():
            arrived.wait_recv()

        return carry

    lax.fori_loop(0, nx, par_wait, 0)
    for source in range(nx):
        for layer in range(2):
            par_ring[layer, source : source + 1, :] = par_recv[source, layer : layer + 1, :]

    oy = a - nx // 2
    oy_f = oy.astype(F32)

    def far_step(index, carry):
        acc0, acc1 = carry
        ox = index - nx // 2
        ox_f = ox.astype(F32)
        keep = (ox > 1) | (ox < -1) | (oy > 1) | (oy < -1)
        const = ox_f * ox_f + oy_f * oy_f + SOFT / 4
        for chunk in range(8):
            rows = pl.ds(32 * chunk, 32)
            flat = tables[0, rows, :] + ox_f * tables[1, rows, :] + oy_f * tables[2, rows, :]
            flat = flat + const
            lift = tables[3, rows, :]
            for slot, value in enumerate((flat + 1.0 - lift, flat, flat + 1.0 + lift)):
                high, low = split(jnp.where(keep, lax.rsqrt(value), 0.0))
                m_hi[slot, rows, :] = high
                m_lo[slot, rows, :] = low
        turn = lax.rem(nx + nx // 2 - index, nx)
        p0h, p0l = split(pltpu.roll(par_ring[0], turn, 0))
        p1h, p1l = split(pltpu.roll(par_ring[1], turn, 0))
        same = bdot(jnp.concatenate([p0h, p1h, p0l, p1l], axis=0), m_hi[1])
        same2 = bdot(jnp.concatenate([p0h, p1h], axis=0), m_lo[1])
        up = bdot(jnp.concatenate([p1h, p1l], axis=0), m_hi[2])
        up2 = bdot(p1h, m_lo[2])
        down = bdot(jnp.concatenate([p0h, p0l], axis=0), m_hi[0])
        down2 = bdot(p0h, m_lo[0])
        acc0 = acc0 + ((same[0:16] + up[0:16]) + (same[32:48] + same2[0:16] + up[16:32] + up2))
        acc1 = acc1 + (
            (same[16:32] + down[0:16]) + (same[48:64] + same2[16:32] + down[16:32] + down2)
        )
        return acc0, acc1

    zero16 = jnp.zeros((16, 256), F32)
    far0, far1 = lax.fori_loop(0, nx, far_step, (zero16, zero16))
    for target in range(nx):
        rs_send[target, 2] = jnp.where(
            row8 == 0,
            0.5 * far0[target : target + 1, :],
            jnp.where(row8 == 1, 0.5 * far1[target : target + 1, :], 0.0),
        )

    dy, half_z = leaf_task(a)

    def leaf_wait(source, carry):
        for py in range(2):
            valid, row, src_py = leaf_route(a, py)
            self_copy = (source == a) & (row == 0)
            arrived = pltpu.make_async_remote_copy(
                src_ref=leaf_send.at[0],
                dst_ref=leaf_recv.at[source, py],
                send_sem=leaf_ssem.at[source, py],
                recv_sem=leaf_rsem.at[source, py],
                device_id=(lax.rem(a + 1, nx), b),
                device_id_type=MESH,
            )

            @pl.when(valid & jnp.logical_not(self_copy))
            def _():
                arrived.wait_recv()

        return carry

    lax.fori_loop(0, nx, leaf_wait, 0)

    @pl.when(dy == 3)
    def _():
        leaf_recv[:, 1] = jnp.zeros((nx, 8, 256), F32)

    @pl.when(dy == -3)
    def _():
        leaf_recv[:, 0] = jnp.zeros((nx, 8, 256), F32)

    for target in range(nx):
        rs_send[target, 0] = jnp.zeros((8, 256), F32)
        rs_send[target, 1] = jnp.zeros((8, 256), F32)

    @pl.when(a < 14)
    def _():
        for source in range(nx):
            low_py = leaf_recv[source, 0]
            high_py = leaf_recv[source, 1]
            first = row8 < 4
            shifted[0, 8 * source : 8 * source + 8, :] = jnp.where(
                first, low_py, pltpu.roll(high_py, 4, 0)
            )
            shifted[1, 8 * source : 8 * source + 8, :] = jnp.where(
                first, pltpu.roll(low_py, 4, 0), high_py
            )
        dy_f = dy.astype(F32)
        row128 = lax.broadcasted_iota(jnp.int32, (128, 256), 0) % 4

        def leaf_step(step, carry):
            dz = jnp.where(half_z == 0, step - 3, step + 1)

            @pl.when(dz <= 3)
            def _():
                dz_f = dz.astype(F32)
                beside = (dy >= -1) & (dy <= 1) & (dz >= -1) & (dz <= 1)
                const = dy_f * dy_f + dz_f * dz_f + SOFT
                for chunk in range(8):
                    rows = pl.ds(32 * chunk, 32)
                    base = tables[0, rows, :] + dy_f * tables[2, rows, :]
                    base = base + dz_f * tables[3, rows, :] + const
                    along = tables[1, rows, :]
                    for slot in range(7):
                        dx = slot - 3
                        value = base + (float(dx) * along + float(dx * dx)) if dx else base
                        kernel = lax.rsqrt(value)
                        if abs(dx) <= 1:
                            kernel = jnp.where(beside, 0.0, kernel)
                        high, low = split(kernel)
                        m_hi[slot, rows, :] = high
                        m_lo[slot, rows, :] = low
                inside = (row128 + dz >= 0) & (row128 + dz <= 3)
                turn = lax.rem(128 - dz, 128)
                for sx in range(2):
                    moved = jnp.where(inside, pltpu.roll(shifted[sx], turn, 0), 0.0)
                    for block in (-1, 0, 1):
                        if block == -1:
                            placed = jnp.concatenate([moved[120:], moved[:120]], axis=0)
                        elif block == 1:
                            placed = jnp.concatenate([moved[8:], moved[:8]], axis=0)
                        else:
                            placed = moved
                        slot = 2 * block + sx + 2
                        high, low = split(placed)
                        l_hi[slot] = high
                        l_lo[slot] = low
                for px in range(2):
                    total = jnp.zeros((128, 256), F32)
                    for slot in range(6):
                        matrix = slot + 1 - px
                        total = total + (
                            bdot(l_hi[slot], m_hi[matrix])
                            + (bdot(l_lo[slot], m_hi[matrix]) + bdot(l_hi[slot], m_lo[matrix]))
                        )
                    rs_send[:, px] = rs_send[:, px] + total.reshape(nx, 8, 256)

            return carry

        lax.fori_loop(0, 4, leaf_step, 0)

    def rs_copy(target):
        return pltpu.make_async_remote_copy(
            src_ref=rs_send.at[target],
            dst_ref=rs_recv.at[a],
            send_sem=rs_ssem.at[target],
            recv_sem=rs_rsem.at[a],
            device_id=(target, b),
            device_id_type=MESH,
        )

    def rs_start(step, carry):
        rs_copy(lax.rem(a + step, nx)).start()
        return carry

    lax.fori_loop(1, nx, rs_start, 0)
    rs_recv[a] = rs_send[a]

    for index in range(8):
        halo_copy(7 - index).wait_recv()
    for fx in range(4):
        for fy in range(4):
            if fx in (0, 3) or fy in (0, 3):
                near_column(fx, fy)

    def rs_wait(step, carry):
        source = lax.rem(a + step, nx)
        pltpu.make_async_remote_copy(
            src_ref=rs_send.at[source],
            dst_ref=rs_recv.at[source],
            send_sem=rs_ssem.at[source],
            recv_sem=rs_rsem.at[source],
            device_id=(source, b),
            device_id_type=MESH,
        ).wait_recv()
        return carry

    lax.fori_loop(1, nx, rs_wait, 0)
    sums = [jnp.zeros((8, 256), F32) for _ in range(3)]
    for source in range(nx):
        for part in range(3):
            sums[part] = sums[part] + rs_recv[source, part]

    fetches[7].wait()
    fetches[8].wait()
    leaf_local = dot_t(jnp.concatenate([sums[0], sums[1]], axis=0), cl_down[...])
    parent_local = 0.5 * dot_t(sums[2], ct_down[...])
    lanes = lax.broadcasted_iota(jnp.int32, (128, 128), 1)
    columns = jnp.zeros((128, 128), F32)
    for box in range(16):
        layer = (box % 4) // 2
        value = k_leaf[box] * leaf_local[box : box + 1, :]
        value = value + k_parent[box] * parent_local[layer : layer + 1, :]
        column = jnp.sum(value, axis=1, keepdims=True)
        columns = jnp.where(lanes == box, column, columns)
    flipped = jnp.transpose(columns)
    for px in range(2):
        for py in range(2):
            for k in range(4):
                box = (px * 2 + py) * 4 + k
                row = flipped[box : box + 1, :] + jnp.sum(near_acc[box], axis=0, keepdims=True)
                out_ref[px, py, k : k + 1, :] = jnp.where(
                    lane128[0:1] < counts_ref[px, py, k], row, 0.0
                )

    for index in range(8):
        halo_copy(index).wait_send()

    def drain(target, carry):
        for py in range(2):
            valid, self_copy, _, copy = leaf_copy(target, py)

            @pl.when(valid & jnp.logical_not(self_copy))
            def _():
                copy.wait_send()

        own, copy = par_copy(target)

        @pl.when(jnp.logical_not(own))
        def _():
            copy.wait_send()

        @pl.when(target != a)
        def _():
            rs_copy(target).wait_send()

        return carry

    lax.fori_loop(0, nx, drain, 0)


def shards(offsets, charges, counts, cl_up, cl_down, ct_up, ct_down):
    nx = lax.axis_size("gx")
    ny = lax.axis_size("gy")
    points = sphere_points(256)
    unit = np.zeros((8, 256), np.float32)
    unit[:3] = points
    unit_t = np.zeros((256, 8), np.float32)
    unit_t[:, :3] = points.T
    vmem = pl.BlockSpec(memory_space=pltpu.VMEM)
    dma = pltpu.SemaphoreType.DMA
    return pl.pallas_call(
        functools.partial(body, nx, ny),
        out_shape=jax.ShapeDtypeStruct(charges.shape, F32),
        in_specs=[pl.BlockSpec(memory_space=pl.ANY)] * 9,
        out_specs=vmem,
        scratch_shapes=[
            pltpu.SMEM(counts.shape, jnp.int32),
            pltpu.VMEM(offsets.shape, F32),
            pltpu.VMEM(charges.shape, F32),
            pltpu.VMEM(unit.shape, F32),
            pltpu.VMEM(unit_t.shape, F32),
            pltpu.VMEM((256, 256), F32),
            pltpu.VMEM((256, 256), F32),
            pltpu.VMEM((256, 256), F32),
            pltpu.VMEM((256, 256), F32),
            dma((9,)),
            pltpu.VMEM((4, 4, 16, 128), F32),
            pltpu.VMEM((4, 256, 256), F32),
            pltpu.VMEM((16, 128, 256), F32),
            pltpu.VMEM((16, 128, 256), F32),
            pltpu.VMEM((8, 256, 256), BF16),
            pltpu.VMEM((8, 256, 256), BF16),
            pltpu.VMEM((2, 8, 256), F32),
            pltpu.VMEM((nx, 2, 8, 256), F32),
            pltpu.VMEM((8, 256), F32),
            pltpu.VMEM((nx, 8, 256), F32),
            pltpu.VMEM((nx, 3, 8, 256), F32),
            pltpu.VMEM((nx, 3, 8, 256), F32),
            pltpu.VMEM((2, 8 * nx, 256), F32),
            pltpu.VMEM((2, nx, 256), F32),
            pltpu.VMEM((7, 256, 256), BF16),
            pltpu.VMEM((7, 256, 256), BF16),
            pltpu.VMEM((6, 8 * nx, 256), BF16),
            pltpu.VMEM((6, 8 * nx, 256), BF16),
            pltpu.VMEM((16, 8, 128), F32),
            pltpu.VMEM((128, 16), F32),
            dma((8,)),
            dma((8,)),
            dma((nx, 2)),
            dma((nx, 2)),
            dma((nx,)),
            dma((nx,)),
            dma((nx,)),
            dma((nx,)),
        ],
        compiler_params=pltpu.CompilerParams(
            has_side_effects=True, collective_id=0, vmem_limit_bytes=56 * 1024 * 1024
        ),
        name="multipole",
    )(counts, offsets, charges, jnp.asarray(unit), jnp.asarray(unit_t), cl_up, cl_down, ct_up, ct_down)


def solution(mesh):
    return jax.shard_map(
        shards,
        mesh=mesh,
        in_specs=(
            P(None, "gx", "gy", None, None),
            P("gx", "gy", None, None),
            P("gx", "gy", None),
            P(),
            P(),
            P(),
            P(),
        ),
        out_specs=P("gx", "gy", None, None),
        check_vma=False,
    )
```

```python
import functools

import jax
import jax.numpy as jnp
import numpy as np
from jax import lax
from jax.experimental import pallas as pl
from jax.experimental.pallas import tpu as pltpu
from jax.sharding import PartitionSpec as P

SOFT = 0.0004
F32 = jnp.float32
BF16 = jnp.bfloat16
HIGHEST = lax.Precision.HIGHEST
MESH = pl.DeviceIdType.MESH
SIDES = [(sx, sy) for sx in (-1, 0, 1) for sy in (-1, 0, 1) if (sx, sy) != (0, 0)]


def sphere_points(count):
    middle = np.arange(count).astype(np.float32) + np.float32(0.5)
    height = (np.float32(1.0) - np.float32(2.0) * middle / np.float32(count)).astype(np.float32)
    radial = np.sqrt(np.maximum(np.float32(1.0) - height * height, np.float32(0.0)))
    turn = (middle * np.float32(2.399963229728653)).astype(np.float32)
    cos = np.cos(turn.astype(np.float64)).astype(np.float32)
    sin = np.sin(turn.astype(np.float64)).astype(np.float32)
    return np.stack([radial * cos, radial * sin, height]).astype(np.float32)


def split(value):
    high = value.astype(BF16)
    low = (value - high.astype(F32)).astype(BF16)
    return high, low


def pieces(value):
    first = value.astype(BF16).astype(F32)
    rest = value - first
    second = rest.astype(BF16).astype(F32)
    return first, second, rest - second


def bdot(a, b):
    return jnp.dot(a, b, preferred_element_type=F32)


def dot_t(a, b):
    return lax.dot_general(
        a, b, (((1,), (1,)), ((), ())), precision=HIGHEST, preferred_element_type=F32
    )


def leaf_task(a):
    return a // 2 - 3, a % 2


def body(
    nx,
    ny,
    counts_hbm,
    off_hbm,
    chg_hbm,
    u_hbm,
    ut_hbm,
    cl_up_hbm,
    cl_down_hbm,
    ct_up_hbm,
    ct_down_hbm,
    out_ref,
    counts_ref,
    off_ref,
    chg_ref,
    u_ref,
    ut_ref,
    cl_up,
    cl_down,
    ct_up,
    ct_down,
    in_sem,
    halo,
    tables,
    k_leaf,
    k_parent,
    up_hi,
    up_lo,
    leaf_send,
    leaf_recv,
    par_send,
    par_recv,
    rs_send,
    rs_recv,
    shifted,
    par_ring,
    m_hi,
    m_lo,
    l_hi,
    l_lo,
    near_acc,
    near_lhs,
    feat,
    bank_own,
    bank_x,
    bank_y,
    w_own,
    w_x,
    w_y,
    halo_ssem,
    halo_rsem,
    leaf_ssem,
    leaf_rsem,
    par_ssem,
    par_rsem,
    rs_ssem,
    rs_rsem,
):
    a = lax.axis_index("gx")
    b = lax.axis_index("gy")
    lane128 = lax.broadcasted_iota(jnp.int32, (4, 128), 1)

    fetches = [
        pltpu.make_async_copy(src, dst, in_sem.at[index])
        for index, (src, dst) in enumerate(
            (
                (counts_hbm, counts_ref),
                (off_hbm, off_ref),
                (chg_hbm, chg_ref),
                (u_hbm, u_ref),
                (ut_hbm, ut_ref),
                (cl_up_hbm, cl_up),
                (ct_up_hbm, ct_up),
                (cl_down_hbm, cl_down),
                (ct_down_hbm, ct_down),
            )
        )
    ]
    for fetch in fetches:
        fetch.start()

    barrier = pltpu.get_barrier_semaphore()

    def hello(to_a, to_b):
        pl.semaphore_signal(barrier, inc=1, device_id=(to_a, to_b), device_id_type=MESH)

    def hello_row(step, carry):
        hello(lax.rem(a + step, nx), b)
        return carry

    lax.fori_loop(1, nx, hello_row, 0)
    for sx, sy in SIDES:
        hello(lax.rem(a + sx + nx, nx), lax.rem(b + sy + ny, ny))
    task_dy, _ = leaf_task(a)
    leaf_row = jnp.where(task_dy > 0, 1, -1)
    far_b = lax.rem(b + a - nx // 2 + ny, ny)

    def hello_far(step, carry):
        to_a = lax.rem(a + step, nx)

        @pl.when((a < 14) & (task_dy != 0))
        def _():
            hello(to_a, lax.rem(b + leaf_row + ny, ny))

        @pl.when((to_a != a) | (far_b != b))
        def _():
            hello(to_a, far_b)

        return carry

    lax.fori_loop(0, nx, hello_far, 0)
    for fetch in fetches[:5]:
        fetch.wait()

    for px in range(2):
        for py in range(2):
            cell = halo.at[1 + px, 1 + py]
            for comp in range(3):
                cell[4 * comp : 4 * comp + 4, :] = off_ref[comp, px, py]
            for k in range(4):
                row = chg_ref[px, py, k : k + 1, :]
                cell[12 + k : 13 + k, :] = jnp.where(
                    lane128[0:1] < counts_ref[px, py, k], row, 0.0
                )

    def halo_copy(index):
        sx, sy = SIDES[index]
        src_x = pl.ds(1, 2) if sx == 0 else pl.ds(2 if sx == 1 else 1, 1)
        src_y = pl.ds(1, 2) if sy == 0 else pl.ds(2 if sy == 1 else 1, 1)
        dst_x = pl.ds(1, 2) if sx == 0 else pl.ds(0 if sx == 1 else 3, 1)
        dst_y = pl.ds(1, 2) if sy == 0 else pl.ds(0 if sy == 1 else 3, 1)
        return pltpu.make_async_remote_copy(
            src_ref=halo.at[src_x, src_y],
            dst_ref=halo.at[dst_x, dst_y],
            send_sem=halo_ssem.at[index],
            recv_sem=halo_rsem.at[index],
            device_id=(lax.rem(a + sx + nx, nx), lax.rem(b + sy + ny, ny)),
            device_id_type=MESH,
        )

    for chunk in range(8):
        rows = pl.ds(32 * chunk, 32)
        total = jnp.zeros((32, 256), F32)
        for comp in range(3):
            diff = 0.9 * (u_ref[comp : comp + 1, :] - ut_ref[rows, comp : comp + 1])
            tables[1 + comp, rows, :] = -2.0 * diff
            total = total + diff * diff
        tables[0, rows, :] = total

    def child_chunk(chunk, carry):
        rows = pl.ds(pl.multiple_of(32 * chunk, 32), 32)
        base = jnp.full((32, 256), 0.1875 + SOFT / 4, F32)
        half = []
        for comp in range(3):
            diff = 1.8 * u_ref[comp : comp + 1, :] - 0.45 * ut_ref[rows, comp : comp + 1]
            base = base + diff * diff
            half.append(0.5 * diff)
        for child in range(8):
            value = base
            for comp, bit in enumerate((child // 4, child // 2 % 2, child % 2)):
                value = value + half[comp] if bit == 0 else value - half[comp]
            high, low = split(lax.rsqrt(value))
            up_hi[child, rows, :] = high
            up_lo[child, rows, :] = low
        return carry

    lax.fori_loop(0, 8, child_chunk, 0)

    centre = [0.5 + 1.8 * u_ref[comp : comp + 1, :] for comp in range(3)]
    checks = []
    for px in range(2):
        for py in range(2):
            turned = jnp.transpose(halo[1 + px, 1 + py])
            for k in range(4):
                box = (px * 2 + py) * 4 + k
                total = jnp.full((128, 256), SOFT, F32)
                for comp in range(3):
                    diff = centre[comp] - turned[:, 4 * comp + k : 4 * comp + k + 1]
                    total = total + diff * diff
                kernel = lax.rsqrt(total)
                k_leaf[box] = kernel
                weight = turned[:, 12 + k : 13 + k]
                checks.append(jnp.sum(kernel * weight, axis=0, keepdims=True))
    leaf_check = jnp.concatenate(checks, axis=0)
    fetches[5].wait()
    leaf_eq = dot_t(leaf_check, cl_up[...])
    for px in range(2):
        for py in range(2):
            first = (px * 2 + py) * 4
            leaf_send[py, 4 * px : 4 * px + 4, :] = leaf_eq[first : first + 4, :]

    eq_hi, eq_lo = split(leaf_eq)
    both = jnp.concatenate([eq_hi, eq_lo], axis=0)
    row16 = lax.broadcasted_iota(jnp.int32, (16, 256), 0)
    rows_sum = jnp.zeros((16, 256), F32)
    for child in range(8):
        first = bdot(both, up_hi[child])
        term = first[:16] + first[16:] + bdot(eq_hi, up_lo[child])
        mine = ((row16 // 4) == (child // 2)) & ((row16 % 2) == (child % 2))
        rows_sum = jnp.where(mine, term, rows_sum)
    upper = (row16 % 4) >= 2
    check0 = 0.5 * jnp.sum(jnp.where(upper, 0.0, rows_sum), axis=0, keepdims=True)
    check1 = 0.5 * jnp.sum(jnp.where(upper, rows_sum, 0.0), axis=0, keepdims=True)
    row8 = lax.broadcasted_iota(jnp.int32, (8, 256), 0)
    parent_check = jnp.where(row8 == 0, check0, jnp.where(row8 == 1, check1, 0.0))
    fetches[6].wait()
    par_send[...] = dot_t(parent_check, ct_up[...])

    def source_rows(x, y, z):
        rows = []
        for value in (x, y, z):
            q1, q2, q3 = pieces(value)
            rows += [q1, q2, q1, q2, q3, q1]
        n1, n2, n3 = pieces((x * x + y * y) + (z * z + SOFT))
        one = jnp.ones_like(x)
        return rows + [n1, n2, n3, one, one, one]

    def target_rows(x, y, z):
        rows = []
        for value in (x, y, z):
            p1, p2, p3 = [-2.0 * part for part in pieces(value)]
            rows += [p1, p1, p2, p2, p1, p3]
        one = jnp.ones_like(x)
        n1, n2, n3 = pieces((x * x + y * y) + z * z)
        return rows + [one, one, one, n1, n2, n3]

    box_row = lax.broadcasted_iota(jnp.int32, (16, 128), 0)
    own_x, own_y, own_z, own_w = [
        jnp.concatenate(
            [halo[1 + px, 1 + py, 4 * comp : 4 * comp + 4, :] for px in (0, 1) for py in (0, 1)],
            axis=0,
        )
        for comp in range(4)
    ]
    own_x = own_x + ((box_row // 8) - 1).astype(F32)
    own_y = own_y + ((box_row // 4 % 2) - 1).astype(F32)
    own_z = own_z - 0.5
    feat[pl.ds(384, 128), :] = jnp.zeros((128, 128), F32)
    for index, value in enumerate(source_rows(own_x, own_y, own_z)):
        feat[16 * index : 16 * index + 16, :] = value
    for column in range(4):
        for layer in range(4):
            block = feat[pl.ds(4 * column + layer, 32, stride=16), :]
            bank_own[layer, :, 128 * column : 128 * column + 128] = block.astype(BF16)
            row = own_w[4 * column + layer : 4 * column + layer + 1, :]
            w_own[layer, 0:1, 128 * column : 128 * column + 128] = row
    for turn in range(3):
        for index, value in enumerate(target_rows(own_x, own_y, own_z - float(turn - 1))):
            feat[16 * index : 16 * index + 16, :] = value
        for box in range(16):
            block = feat[pl.ds(box, 32, stride=16), :]
            near_lhs[turn, box] = jnp.transpose(block).astype(BF16)

    lane512 = lax.broadcasted_iota(jnp.int32, (128, 512), 1)
    row512 = lax.broadcasted_iota(jnp.int32, (128, 512), 0)

    def fold(value):
        total = value[:, 0:128]
        for first in range(128, value.shape[1], 128):
            total = total + value[:, first : first + 128]
        return total

    def near_own(turn):
        low = max(0, 1 - turn)
        count = 4 - abs(turn - 1)

        def step(index, carry):
            column = index // count
            layer = index % count + low
            box = 4 * column + layer
            source = layer + turn - 1
            kernel = lax.rsqrt(bdot(near_lhs[turn, box], bank_own[source]))
            if turn == 1:
                kernel = jnp.where(lane512 == row512 + 128 * column, 0.0, kernel)
            value = fold(kernel * w_own[source, 0:1, :])
            near_acc[box] = value if turn == 1 else near_acc[box] + value
            return carry

        lax.fori_loop(0, 4 * count, step, 0)

    def near_halo(turn):
        low = max(0, 1 - turn)
        count = 4 - abs(turn - 1)

        def step(index, carry):
            column = index // count
            layer = index % count + low
            box = 4 * column + layer
            source = layer + turn - 1
            px = column // 2
            py = column % 2
            lanes = pl.ds(pl.multiple_of(128 * py, 128), 384)
            lhs = near_lhs[turn, box]
            value = lax.rsqrt(bdot(lhs, bank_x[source, px, :, lanes]))
            value = fold(value * w_x[source, px, 0:1, lanes])
            other = lax.rsqrt(bdot(lhs, bank_y[source, py]))
            other = fold(other * w_y[source, py, 0:1, :])
            near_acc[box] = near_acc[box] + (value + other)
            return carry

        lax.fori_loop(0, 4 * count, step, 0)

    for turn in (1, 0, 2):
        near_own(turn)

    def leaf_route(target, py):
        dy, _ = leaf_task(target)
        src = py + dy
        valid = (target < 14) & (src >= -2) & (src <= 3)
        row = (src + 4) // 2 - 2
        return valid, row, (src + 4) % 2

    def leaf_copy(target, py):
        valid, row, src_py = leaf_route(target, py)
        to_b = lax.rem(b - row + ny, ny)
        copy = pltpu.make_async_remote_copy(
            src_ref=leaf_send.at[src_py],
            dst_ref=leaf_recv.at[a, py],
            send_sem=leaf_ssem.at[target, py],
            recv_sem=leaf_rsem.at[a, py],
            device_id=(target, to_b),
            device_id_type=MESH,
        )
        self_copy = (target == a) & (to_b == b)
        return valid, self_copy, src_py, copy

    def leaf_start(target, carry):
        for py in range(2):
            valid, self_copy, src_py, copy = leaf_copy(target, py)

            @pl.when(valid & jnp.logical_not(self_copy))
            def _():
                copy.start()

            @pl.when(valid & self_copy)
            def _():
                leaf_recv[a, py] = leaf_send[src_py]

        return carry

    def par_copy(target):
        to_b = lax.rem(b - target + nx // 2 + ny, ny)
        copy = pltpu.make_async_remote_copy(
            src_ref=par_send,
            dst_ref=par_recv.at[a],
            send_sem=par_ssem.at[target],
            recv_sem=par_rsem.at[a],
            device_id=(target, to_b),
            device_id_type=MESH,
        )
        return (target == a) & (to_b == b), copy

    def par_start(target, carry):
        self_copy, copy = par_copy(target)

        @pl.when(jnp.logical_not(self_copy))
        def _():
            copy.start()

        @pl.when(self_copy)
        def _():
            par_recv[a] = par_send[...]

        return carry

    pl.semaphore_wait(barrier, (nx - 1) + 8 + 12 + jnp.where(a == nx // 2, nx - 1, nx))
    lax.fori_loop(0, nx, leaf_start, 0)
    for index in range(8):
        halo_copy(index).start()

    lax.fori_loop(0, nx, par_start, 0)

    for px in range(2):
        for py in range(2):
            turned = jnp.transpose(halo[1 + px, 1 + py])
            for k in range(4):
                box = (px * 2 + py) * 4 + k
                total = jnp.full((128, 256), SOFT / 4, F32)
                for comp, bit in enumerate((px, py, k % 2)):
                    place = 0.5 * turned[:, 4 * comp + k : 4 * comp + k + 1] + 0.5 * bit
                    diff = centre[comp] - place
                    total = total + diff * diff
                k_parent[box] = lax.rsqrt(total)

    def par_wait(source, carry):
        from_b = lax.rem(b + a - nx // 2 + ny, ny)
        self_copy = (source == a) & (from_b == b)
        arrived = pltpu.make_async_remote_copy(
            src_ref=par_send,
            dst_ref=par_recv.at[source],
            send_sem=par_ssem.at[source],
            recv_sem=par_rsem.at[source],
            device_id=(lax.rem(a + 1, nx), b),
            device_id_type=MESH,
        )

        @pl.when(jnp.logical_not(self_copy))
        def _():
            arrived.wait_recv()

        return carry

    lax.fori_loop(0, nx, par_wait, 0)
    for source in range(nx):
        for layer in range(2):
            par_ring[layer, source : source + 1, :] = par_recv[source, layer : layer + 1, :]

    oy = a - nx // 2
    oy_f = oy.astype(F32)

    def far_step(index, carry):
        acc0, acc1 = carry
        ox = index - nx // 2
        ox_f = ox.astype(F32)
        keep = (ox > 1) | (ox < -1) | (oy > 1) | (oy < -1)
        const = ox_f * ox_f + oy_f * oy_f + SOFT / 4
        for chunk in range(8):
            rows = pl.ds(32 * chunk, 32)
            flat = tables[0, rows, :] + ox_f * tables[1, rows, :] + oy_f * tables[2, rows, :]
            flat = flat + const
            lift = tables[3, rows, :]
            for slot, value in enumerate((flat + 1.0 - lift, flat, flat + 1.0 + lift)):
                high, low = split(jnp.where(keep, lax.rsqrt(value), 0.0))
                m_hi[slot, rows, :] = high
                m_lo[slot, rows, :] = low
        turn = lax.rem(nx + nx // 2 - index, nx)
        p0h, p0l = split(pltpu.roll(par_ring[0], turn, 0))
        p1h, p1l = split(pltpu.roll(par_ring[1], turn, 0))
        same = bdot(jnp.concatenate([p0h, p1h, p0l, p1l], axis=0), m_hi[1])
        same2 = bdot(jnp.concatenate([p0h, p1h], axis=0), m_lo[1])
        up = bdot(jnp.concatenate([p1h, p1l], axis=0), m_hi[2])
        up2 = bdot(p1h, m_lo[2])
        down = bdot(jnp.concatenate([p0h, p0l], axis=0), m_hi[0])
        down2 = bdot(p0h, m_lo[0])
        acc0 = acc0 + ((same[0:16] + up[0:16]) + (same[32:48] + same2[0:16] + up[16:32] + up2))
        acc1 = acc1 + (
            (same[16:32] + down[0:16]) + (same[48:64] + same2[16:32] + down[16:32] + down2)
        )
        return acc0, acc1

    zero16 = jnp.zeros((16, 256), F32)
    far0, far1 = lax.fori_loop(0, nx, far_step, (zero16, zero16))
    for target in range(nx):
        rs_send[target, 2] = jnp.where(
            row8 == 0,
            0.5 * far0[target : target + 1, :],
            jnp.where(row8 == 1, 0.5 * far1[target : target + 1, :], 0.0),
        )

    dy, half_z = leaf_task(a)

    def leaf_wait(source, carry):
        for py in range(2):
            valid, row, src_py = leaf_route(a, py)
            self_copy = (source == a) & (row == 0)
            arrived = pltpu.make_async_remote_copy(
                src_ref=leaf_send.at[0],
                dst_ref=leaf_recv.at[source, py],
                send_sem=leaf_ssem.at[source, py],
                recv_sem=leaf_rsem.at[source, py],
                device_id=(lax.rem(a + 1, nx), b),
                device_id_type=MESH,
            )

            @pl.when(valid & jnp.logical_not(self_copy))
            def _():
                arrived.wait_recv()

        return carry

    lax.fori_loop(0, nx, leaf_wait, 0)

    @pl.when(dy == 3)
    def _():
        leaf_recv[:, 1] = jnp.zeros((nx, 8, 256), F32)

    @pl.when(dy == -3)
    def _():
        leaf_recv[:, 0] = jnp.zeros((nx, 8, 256), F32)

    for target in range(nx):
        rs_send[target, 0] = jnp.zeros((8, 256), F32)
        rs_send[target, 1] = jnp.zeros((8, 256), F32)

    @pl.when(a < 14)
    def _():
        for source in range(nx):
            low_py = leaf_recv[source, 0]
            high_py = leaf_recv[source, 1]
            first = row8 < 4
            shifted[0, 8 * source : 8 * source + 8, :] = jnp.where(
                first, low_py, pltpu.roll(high_py, 4, 0)
            )
            shifted[1, 8 * source : 8 * source + 8, :] = jnp.where(
                first, pltpu.roll(low_py, 4, 0), high_py
            )
        dy_f = dy.astype(F32)
        row128 = lax.broadcasted_iota(jnp.int32, (128, 256), 0) % 4

        def leaf_step(step, carry):
            dz = jnp.where(half_z == 0, step - 3, step + 1)

            @pl.when(dz <= 3)
            def _():
                dz_f = dz.astype(F32)
                beside = (dy >= -1) & (dy <= 1) & (dz >= -1) & (dz <= 1)
                const = dy_f * dy_f + dz_f * dz_f + SOFT
                for chunk in range(8):
                    rows = pl.ds(32 * chunk, 32)
                    base = tables[0, rows, :] + dy_f * tables[2, rows, :]
                    base = base + dz_f * tables[3, rows, :] + const
                    along = tables[1, rows, :]
                    for slot in range(7):
                        dx = slot - 3
                        value = base + (float(dx) * along + float(dx * dx)) if dx else base
                        kernel = lax.rsqrt(value)
                        if abs(dx) <= 1:
                            kernel = jnp.where(beside, 0.0, kernel)
                        high, low = split(kernel)
                        m_hi[slot, rows, :] = high
                        m_lo[slot, rows, :] = low
                inside = (row128 + dz >= 0) & (row128 + dz <= 3)
                turn = lax.rem(128 - dz, 128)
                for sx in range(2):
                    moved = jnp.where(inside, pltpu.roll(shifted[sx], turn, 0), 0.0)
                    for block in (-1, 0, 1):
                        if block == -1:
                            placed = jnp.concatenate([moved[120:], moved[:120]], axis=0)
                        elif block == 1:
                            placed = jnp.concatenate([moved[8:], moved[:8]], axis=0)
                        else:
                            placed = moved
                        slot = 2 * block + sx + 2
                        high, low = split(placed)
                        l_hi[slot] = high
                        l_lo[slot] = low
                for px in range(2):
                    total = jnp.zeros((128, 256), F32)
                    for slot in range(6):
                        matrix = slot + 1 - px
                        total = total + (
                            bdot(l_hi[slot], m_hi[matrix])
                            + (bdot(l_lo[slot], m_hi[matrix]) + bdot(l_hi[slot], m_lo[matrix]))
                        )
                    rs_send[:, px] = rs_send[:, px] + total.reshape(nx, 8, 256)

            return carry

        lax.fori_loop(0, 4, leaf_step, 0)

    def rs_copy(target):
        return pltpu.make_async_remote_copy(
            src_ref=rs_send.at[target],
            dst_ref=rs_recv.at[a],
            send_sem=rs_ssem.at[target],
            recv_sem=rs_rsem.at[a],
            device_id=(target, b),
            device_id_type=MESH,
        )

    def rs_start(step, carry):
        rs_copy(lax.rem(a + step, nx)).start()
        return carry

    lax.fori_loop(1, nx, rs_start, 0)
    rs_recv[a] = rs_send[a]

    for index in range(8):
        halo_copy(7 - index).wait_recv()
    for strip in range(4):
        if strip < 2:
            cells = [(3 * strip, fy) for fy in range(4)]
        else:
            cells = [(1, 3 * (strip - 2)), (2, 3 * (strip - 2))]
        side_x, side_y, side_z, side_w = [
            jnp.concatenate(
                [halo[fx, fy, 4 * comp : 4 * comp + 4, :] for fx, fy in cells], axis=0
            )
            for comp in range(4)
        ]
        size = 4 * len(cells)
        place = lax.broadcasted_iota(jnp.int32, (size, 128), 0) // 4
        if strip < 2:
            side_x = side_x + float(3 * strip - 2)
            side_y = side_y + (place - 2).astype(F32)
        else:
            side_x = side_x + (place - 1).astype(F32)
            side_y = side_y + float(3 * (strip - 2) - 2)
        for index, value in enumerate(source_rows(side_x, side_y, side_z - 0.5)):
            feat[size * index : size * index + size, :] = value
        feat[pl.ds(24 * size, 8 * size), :] = jnp.zeros((8 * size, 128), F32)
        for cell in range(len(cells)):
            for layer in range(4):
                block = feat[pl.ds(4 * cell + layer, 32, stride=size), :].astype(BF16)
                row = side_w[4 * cell + layer : 4 * cell + layer + 1, :]
                if strip < 2:
                    bank_x[layer, strip, :, 128 * cell : 128 * cell + 128] = block
                    w_x[layer, strip, 0:1, 128 * cell : 128 * cell + 128] = row
                else:
                    bank_y[layer, strip - 2, :, 128 * cell : 128 * cell + 128] = block
                    w_y[layer, strip - 2, 0:1, 128 * cell : 128 * cell + 128] = row
    for turn in (1, 0, 2):
        near_halo(turn)

    def rs_wait(step, carry):
        source = lax.rem(a + step, nx)
        pltpu.make_async_remote_copy(
            src_ref=rs_send.at[source],
            dst_ref=rs_recv.at[source],
            send_sem=rs_ssem.at[source],
            recv_sem=rs_rsem.at[source],
            device_id=(source, b),
            device_id_type=MESH,
        ).wait_recv()
        return carry

    lax.fori_loop(1, nx, rs_wait, 0)
    sums = [jnp.zeros((8, 256), F32) for _ in range(3)]
    for source in range(nx):
        for part in range(3):
            sums[part] = sums[part] + rs_recv[source, part]

    fetches[7].wait()
    fetches[8].wait()
    leaf_local = dot_t(jnp.concatenate([sums[0], sums[1]], axis=0), cl_down[...])
    parent_local = 0.5 * dot_t(sums[2], ct_down[...])
    lanes = lax.broadcasted_iota(jnp.int32, (128, 128), 1)
    columns = jnp.zeros((128, 128), F32)
    for box in range(16):
        layer = (box % 4) // 2
        value = k_leaf[box] * leaf_local[box : box + 1, :]
        value = value + k_parent[box] * parent_local[layer : layer + 1, :]
        value = value[:, :128] + value[:, 128:] + near_acc[box]
        column = jnp.sum(value, axis=1, keepdims=True)
        columns = jnp.where(lanes == box, column, columns)
    flipped = jnp.transpose(columns)
    for px in range(2):
        for py in range(2):
            for k in range(4):
                box = (px * 2 + py) * 4 + k
                row = flipped[box : box + 1, :]
                out_ref[px, py, k : k + 1, :] = jnp.where(
                    lane128[0:1] < counts_ref[px, py, k], row, 0.0
                )

    for index in range(8):
        halo_copy(index).wait_send()

    def drain(target, carry):
        for py in range(2):
            valid, self_copy, _, copy = leaf_copy(target, py)

            @pl.when(valid & jnp.logical_not(self_copy))
            def _():
                copy.wait_send()

        own, copy = par_copy(target)

        @pl.when(jnp.logical_not(own))
        def _():
            copy.wait_send()

        @pl.when(target != a)
        def _():
            rs_copy(target).wait_send()

        return carry

    lax.fori_loop(0, nx, drain, 0)


def shards(offsets, charges, counts, cl_up, cl_down, ct_up, ct_down):
    nx = lax.axis_size("gx")
    ny = lax.axis_size("gy")
    points = sphere_points(256)
    unit = np.zeros((8, 256), np.float32)
    unit[:3] = points
    unit_t = np.zeros((256, 8), np.float32)
    unit_t[:, :3] = points.T
    vmem = pl.BlockSpec(memory_space=pltpu.VMEM)
    dma = pltpu.SemaphoreType.DMA
    return pl.pallas_call(
        functools.partial(body, nx, ny),
        out_shape=jax.ShapeDtypeStruct(charges.shape, F32),
        in_specs=[pl.BlockSpec(memory_space=pl.ANY)] * 9,
        out_specs=vmem,
        scratch_shapes=[
            pltpu.SMEM(counts.shape, jnp.int32),
            pltpu.VMEM(offsets.shape, F32),
            pltpu.VMEM(charges.shape, F32),
            pltpu.VMEM(unit.shape, F32),
            pltpu.VMEM(unit_t.shape, F32),
            pltpu.VMEM((256, 256), F32),
            pltpu.VMEM((256, 256), F32),
            pltpu.VMEM((256, 256), F32),
            pltpu.VMEM((256, 256), F32),
            dma((9,)),
            pltpu.VMEM((4, 4, 16, 128), F32),
            pltpu.VMEM((4, 256, 256), F32),
            pltpu.VMEM((16, 128, 256), F32),
            pltpu.VMEM((16, 128, 256), F32),
            pltpu.VMEM((8, 256, 256), BF16),
            pltpu.VMEM((8, 256, 256), BF16),
            pltpu.VMEM((2, 8, 256), F32),
            pltpu.VMEM((nx, 2, 8, 256), F32),
            pltpu.VMEM((8, 256), F32),
            pltpu.VMEM((nx, 8, 256), F32),
            pltpu.VMEM((nx, 3, 8, 256), F32),
            pltpu.VMEM((nx, 3, 8, 256), F32),
            pltpu.VMEM((2, 8 * nx, 256), F32),
            pltpu.VMEM((2, nx, 256), F32),
            pltpu.VMEM((7, 256, 256), BF16),
            pltpu.VMEM((7, 256, 256), BF16),
            pltpu.VMEM((6, 8 * nx, 256), BF16),
            pltpu.VMEM((6, 8 * nx, 256), BF16),
            pltpu.VMEM((16, 128, 128), F32),
            pltpu.VMEM((3, 16, 128, 32), BF16),
            pltpu.VMEM((512, 128), F32),
            pltpu.VMEM((4, 32, 512), BF16),
            pltpu.VMEM((4, 2, 32, 512), BF16),
            pltpu.VMEM((4, 2, 32, 256), BF16),
            pltpu.VMEM((4, 8, 512), F32),
            pltpu.VMEM((4, 2, 8, 512), F32),
            pltpu.VMEM((4, 2, 8, 256), F32),
            dma((8,)),
            dma((8,)),
            dma((nx, 2)),
            dma((nx, 2)),
            dma((nx,)),
            dma((nx,)),
            dma((nx,)),
            dma((nx,)),
        ],
        compiler_params=pltpu.CompilerParams(
            has_side_effects=True, collective_id=0, vmem_limit_bytes=56 * 1024 * 1024
        ),
        name="multipole",
    )(counts, offsets, charges, jnp.asarray(unit), jnp.asarray(unit_t), cl_up, cl_down, ct_up, ct_down)


def solution(mesh):
    return jax.shard_map(
        shards,
        mesh=mesh,
        in_specs=(
            P(None, "gx", "gy", None, None),
            P("gx", "gy", None, None),
            P("gx", "gy", None),
            P(),
            P(),
            P(),
            P(),
        ),
        out_specs=P("gx", "gy", None, None),
        check_vma=False,
    )
```

```python
import functools

import jax
import jax.numpy as jnp
import numpy as np
from jax import lax
from jax.experimental import pallas as pl
from jax.experimental.pallas import tpu as pltpu
from jax.sharding import PartitionSpec as P

SOFT = 0.0004
F32 = jnp.float32
BF16 = jnp.bfloat16
HIGHEST = lax.Precision.HIGHEST
MESH = pl.DeviceIdType.MESH
SIDES = [(sx, sy) for sx in (-1, 0, 1) for sy in (-1, 0, 1) if (sx, sy) != (0, 0)]


def sphere_points(count):
    middle = np.arange(count).astype(np.float32) + np.float32(0.5)
    height = (np.float32(1.0) - np.float32(2.0) * middle / np.float32(count)).astype(np.float32)
    radial = np.sqrt(np.maximum(np.float32(1.0) - height * height, np.float32(0.0)))
    turn = (middle * np.float32(2.399963229728653)).astype(np.float32)
    cos = np.cos(turn.astype(np.float64)).astype(np.float32)
    sin = np.sin(turn.astype(np.float64)).astype(np.float32)
    return np.stack([radial * cos, radial * sin, height]).astype(np.float32)


def split(value):
    high = value.astype(BF16)
    low = (value - high.astype(F32)).astype(BF16)
    return high, low


def pieces(value):
    first = value.astype(BF16).astype(F32)
    rest = value - first
    second = rest.astype(BF16).astype(F32)
    return first, second, rest - second


def bdot(a, b):
    return jnp.dot(a, b, preferred_element_type=F32)


def dot_t(a, b):
    return lax.dot_general(
        a, b, (((1,), (1,)), ((), ())), precision=HIGHEST, preferred_element_type=F32
    )


def leaf_task(a):
    return a // 2 - 3, a % 2


def body(
    nx,
    ny,
    counts_hbm,
    off_hbm,
    chg_hbm,
    u_hbm,
    ut_hbm,
    cl_up_hbm,
    cl_down_hbm,
    ct_up_hbm,
    ct_down_hbm,
    out_ref,
    counts_ref,
    off_ref,
    chg_ref,
    u_ref,
    ut_ref,
    cl_up,
    cl_down,
    ct_up,
    ct_down,
    in_sem,
    halo,
    tables,
    k_leaf,
    k_parent,
    up_hi,
    up_lo,
    leaf_send,
    leaf_recv,
    par_send,
    par_recv,
    rs_send,
    rs_recv,
    shifted,
    par_ring,
    m_hi,
    m_lo,
    l_hi,
    l_lo,
    near_acc,
    near_lhs,
    feat,
    bank_own,
    bank_x,
    bank_y,
    w_own,
    w_x,
    w_y,
    halo_ssem,
    halo_rsem,
    leaf_ssem,
    leaf_rsem,
    par_ssem,
    par_rsem,
    rs_ssem,
    rs_rsem,
):
    a = lax.axis_index("gx")
    b = lax.axis_index("gy")
    lane128 = lax.broadcasted_iota(jnp.int32, (4, 128), 1)

    fetches = [
        pltpu.make_async_copy(src, dst, in_sem.at[index])
        for index, (src, dst) in enumerate(
            (
                (counts_hbm, counts_ref),
                (off_hbm, off_ref),
                (chg_hbm, chg_ref),
                (u_hbm, u_ref),
                (ut_hbm, ut_ref),
                (cl_up_hbm, cl_up),
                (ct_up_hbm, ct_up),
                (cl_down_hbm, cl_down),
                (ct_down_hbm, ct_down),
            )
        )
    ]
    for fetch in fetches:
        fetch.start()

    barrier = pltpu.get_barrier_semaphore()

    def hello(to_a, to_b):
        pl.semaphore_signal(barrier, inc=1, device_id=(to_a, to_b), device_id_type=MESH)

    def hello_row(step, carry):
        hello(lax.rem(a + step, nx), b)
        return carry

    lax.fori_loop(1, nx, hello_row, 0)
    for sx, sy in SIDES:
        hello(lax.rem(a + sx + nx, nx), lax.rem(b + sy + ny, ny))
    task_dy, _ = leaf_task(a)
    leaf_row = jnp.where(task_dy > 0, 1, -1)
    far_b = lax.rem(b + a - nx // 2 + ny, ny)

    def hello_far(step, carry):
        to_a = lax.rem(a + step, nx)

        @pl.when((a < 14) & (task_dy != 0))
        def _():
            hello(to_a, lax.rem(b + leaf_row + ny, ny))

        @pl.when((to_a != a) | (far_b != b))
        def _():
            hello(to_a, far_b)

        return carry

    lax.fori_loop(0, nx, hello_far, 0)
    for fetch in fetches[:5]:
        fetch.wait()

    for px in range(2):
        for py in range(2):
            cell = halo.at[1 + px, 1 + py]
            for comp in range(3):
                cell[4 * comp : 4 * comp + 4, :] = off_ref[comp, px, py]
            for k in range(4):
                row = chg_ref[px, py, k : k + 1, :]
                cell[12 + k : 13 + k, :] = jnp.where(
                    lane128[0:1] < counts_ref[px, py, k], row, 0.0
                )

    def halo_copy(index):
        sx, sy = SIDES[index]
        src_x = pl.ds(1, 2) if sx == 0 else pl.ds(2 if sx == 1 else 1, 1)
        src_y = pl.ds(1, 2) if sy == 0 else pl.ds(2 if sy == 1 else 1, 1)
        dst_x = pl.ds(1, 2) if sx == 0 else pl.ds(0 if sx == 1 else 3, 1)
        dst_y = pl.ds(1, 2) if sy == 0 else pl.ds(0 if sy == 1 else 3, 1)
        return pltpu.make_async_remote_copy(
            src_ref=halo.at[src_x, src_y],
            dst_ref=halo.at[dst_x, dst_y],
            send_sem=halo_ssem.at[index],
            recv_sem=halo_rsem.at[index],
            device_id=(lax.rem(a + sx + nx, nx), lax.rem(b + sy + ny, ny)),
            device_id_type=MESH,
        )

    for chunk in range(8):
        rows = pl.ds(32 * chunk, 32)
        total = jnp.zeros((32, 256), F32)
        for comp in range(3):
            diff = 0.9 * (u_ref[comp : comp + 1, :] - ut_ref[rows, comp : comp + 1])
            tables[1 + comp, rows, :] = -2.0 * diff
            total = total + diff * diff
        tables[0, rows, :] = total

    def child_chunk(chunk, carry):
        rows = pl.ds(pl.multiple_of(32 * chunk, 32), 32)
        base = jnp.full((32, 256), 0.1875 + SOFT / 4, F32)
        half = []
        for comp in range(3):
            diff = 1.8 * u_ref[comp : comp + 1, :] - 0.45 * ut_ref[rows, comp : comp + 1]
            base = base + diff * diff
            half.append(0.5 * diff)
        for child in range(8):
            value = base
            for comp, bit in enumerate((child // 4, child // 2 % 2, child % 2)):
                value = value + half[comp] if bit == 0 else value - half[comp]
            high, low = split(lax.rsqrt(value))
            up_hi[child, rows, :] = high
            up_lo[child, rows, :] = low
        return carry

    lax.fori_loop(0, 8, child_chunk, 0)

    centre = [0.5 + 1.8 * u_ref[comp : comp + 1, :] for comp in range(3)]
    checks = []
    for px in range(2):
        for py in range(2):
            turned = jnp.transpose(halo[1 + px, 1 + py])
            for k in range(4):
                box = (px * 2 + py) * 4 + k
                total = jnp.full((128, 256), SOFT, F32)
                for comp in range(3):
                    diff = centre[comp] - turned[:, 4 * comp + k : 4 * comp + k + 1]
                    total = total + diff * diff
                kernel = lax.rsqrt(total)
                k_leaf[box] = kernel
                weight = turned[:, 12 + k : 13 + k]
                checks.append(jnp.sum(kernel * weight, axis=0, keepdims=True))
    leaf_check = jnp.concatenate(checks, axis=0)
    fetches[5].wait()
    leaf_eq = dot_t(leaf_check, cl_up[...])
    for px in range(2):
        for py in range(2):
            first = (px * 2 + py) * 4
            leaf_send[py, 4 * px : 4 * px + 4, :] = leaf_eq[first : first + 4, :]

    eq_hi, eq_lo = split(leaf_eq)
    both = jnp.concatenate([eq_hi, eq_lo], axis=0)
    row16 = lax.broadcasted_iota(jnp.int32, (16, 256), 0)
    rows_sum = jnp.zeros((16, 256), F32)
    for child in range(8):
        first = bdot(both, up_hi[child])
        term = first[:16] + first[16:] + bdot(eq_hi, up_lo[child])
        mine = ((row16 // 4) == (child // 2)) & ((row16 % 2) == (child % 2))
        rows_sum = jnp.where(mine, term, rows_sum)
    upper = (row16 % 4) >= 2
    check0 = 0.5 * jnp.sum(jnp.where(upper, 0.0, rows_sum), axis=0, keepdims=True)
    check1 = 0.5 * jnp.sum(jnp.where(upper, rows_sum, 0.0), axis=0, keepdims=True)
    row8 = lax.broadcasted_iota(jnp.int32, (8, 256), 0)
    parent_check = jnp.where(row8 == 0, check0, jnp.where(row8 == 1, check1, 0.0))
    fetches[6].wait()
    par_send[...] = dot_t(parent_check, ct_up[...])[0:2]

    def source_rows(x, y, z):
        rows = []
        for value in (x, y, z):
            q1, q2, q3 = pieces(value)
            rows += [q1, q2, q1, q2, q3, q1]
        n1, n2, n3 = pieces((x * x + y * y) + (z * z + SOFT))
        one = jnp.ones_like(x)
        return rows + [n1, n2, n3, one, one, one]

    def target_rows(x, y, z):
        rows = []
        for value in (x, y, z):
            p1, p2, p3 = [-2.0 * part for part in pieces(value)]
            rows += [p1, p1, p2, p2, p1, p3]
        one = jnp.ones_like(x)
        n1, n2, n3 = pieces((x * x + y * y) + z * z)
        return rows + [one, one, one, n1, n2, n3]

    box_row = lax.broadcasted_iota(jnp.int32, (16, 128), 0)
    own_x, own_y, own_z, own_w = [
        jnp.concatenate(
            [halo[1 + px, 1 + py, 4 * comp : 4 * comp + 4, :] for px in (0, 1) for py in (0, 1)],
            axis=0,
        )
        for comp in range(4)
    ]
    own_x = own_x + ((box_row // 8) - 1).astype(F32)
    own_y = own_y + ((box_row // 4 % 2) - 1).astype(F32)
    own_z = own_z - 0.5
    feat[pl.ds(384, 128), :] = jnp.zeros((128, 128), F32)
    for index, value in enumerate(source_rows(own_x, own_y, own_z)):
        feat[16 * index : 16 * index + 16, :] = value
    for column in range(4):
        for layer in range(4):
            block = feat[pl.ds(4 * column + layer, 32, stride=16), :]
            bank_own[layer, :, 128 * column : 128 * column + 128] = block.astype(BF16)
            row = own_w[4 * column + layer : 4 * column + layer + 1, :]
            w_own[layer, 0:1, 128 * column : 128 * column + 128] = row
    for turn in range(3):
        for index, value in enumerate(target_rows(own_x, own_y, own_z - float(turn - 1))):
            feat[16 * index : 16 * index + 16, :] = value
        for box in range(16):
            block = feat[pl.ds(box, 32, stride=16), :]
            near_lhs[turn, box] = jnp.transpose(block).astype(BF16)

    lane512 = lax.broadcasted_iota(jnp.int32, (128, 512), 1)
    row512 = lax.broadcasted_iota(jnp.int32, (128, 512), 0)

    def fold(value):
        total = value[:, 0:128]
        for first in range(128, value.shape[1], 128):
            total = total + value[:, first : first + 128]
        return total

    def near_own(turn):
        low = max(0, 1 - turn)
        count = 4 - abs(turn - 1)

        def step(index, carry):
            column = index // count
            layer = index % count + low
            box = 4 * column + layer
            source = layer + turn - 1
            kernel = lax.rsqrt(bdot(near_lhs[turn, box], bank_own[source]))
            if turn == 1:
                kernel = jnp.where(lane512 == row512 + 128 * column, 0.0, kernel)
            value = fold(kernel * w_own[source, 0:1, :])
            near_acc[box] = value if turn == 1 else near_acc[box] + value
            return carry

        lax.fori_loop(0, 4 * count, step, 0)

    def near_halo(turn):
        low = max(0, 1 - turn)
        count = 4 - abs(turn - 1)

        def step(index, carry):
            column = index // count
            layer = index % count + low
            box = 4 * column + layer
            source = layer + turn - 1
            px = column // 2
            py = column % 2
            lanes = pl.ds(pl.multiple_of(128 * py, 128), 384)
            lhs = near_lhs[turn, box]
            value = lax.rsqrt(bdot(lhs, bank_x[source, px, :, lanes]))
            value = fold(value * w_x[source, px, 0:1, lanes])
            other = lax.rsqrt(bdot(lhs, bank_y[source, py]))
            other = fold(other * w_y[source, py, 0:1, :])
            near_acc[box] = near_acc[box] + (value + other)
            return carry

        lax.fori_loop(0, 4 * count, step, 0)

    def leaf_route(target, py):
        dy, _ = leaf_task(target)
        src = py + dy
        valid = (target < 14) & (src >= -2) & (src <= 3)
        row = (src + 4) // 2 - 2
        return valid, row, (src + 4) % 2

    def leaf_copy(target, py):
        valid, row, src_py = leaf_route(target, py)
        to_b = lax.rem(b - row + ny, ny)
        copy = pltpu.make_async_remote_copy(
            src_ref=leaf_send.at[src_py],
            dst_ref=leaf_recv.at[a, py],
            send_sem=leaf_ssem.at[target, py],
            recv_sem=leaf_rsem.at[a, py],
            device_id=(target, to_b),
            device_id_type=MESH,
        )
        self_copy = (target == a) & (to_b == b)
        return valid, self_copy, src_py, copy

    def leaf_start(target, carry):
        for py in range(2):
            valid, self_copy, src_py, copy = leaf_copy(target, py)

            @pl.when(valid & jnp.logical_not(self_copy))
            def _():
                copy.start()

            @pl.when(valid & self_copy)
            def _():
                leaf_recv[a, py] = leaf_send[src_py]

        return carry

    def par_copy(target):
        to_b = lax.rem(b - target + nx // 2 + ny, ny)
        copy = pltpu.make_async_remote_copy(
            src_ref=par_send,
            dst_ref=par_recv.at[a],
            send_sem=par_ssem.at[target],
            recv_sem=par_rsem.at[a],
            device_id=(target, to_b),
            device_id_type=MESH,
        )
        return (target == a) & (to_b == b), copy

    def par_start(target, carry):
        self_copy, copy = par_copy(target)

        @pl.when(jnp.logical_not(self_copy))
        def _():
            copy.start()

        @pl.when(self_copy)
        def _():
            par_recv[a] = par_send[...]

        return carry

    for px in range(2):
        for py in range(2):
            turned = jnp.transpose(halo[1 + px, 1 + py])
            for k in range(4):
                box = (px * 2 + py) * 4 + k
                total = jnp.full((128, 256), SOFT / 4, F32)
                for comp, bit in enumerate((px, py, k % 2)):
                    place = 0.5 * turned[:, 4 * comp + k : 4 * comp + k + 1] + 0.5 * bit
                    diff = centre[comp] - place
                    total = total + diff * diff
                k_parent[box] = lax.rsqrt(total)

    pl.semaphore_wait(barrier, (nx - 1) + 8 + 12 + jnp.where(a == nx // 2, nx - 1, nx))
    lax.fori_loop(0, nx, par_start, 0)
    lax.fori_loop(0, nx, leaf_start, 0)
    for index in range(8):
        halo_copy(index).start()

    for turn in (1, 0, 2):
        near_own(turn)

    def par_wait(source, carry):
        from_b = lax.rem(b + a - nx // 2 + ny, ny)
        self_copy = (source == a) & (from_b == b)
        arrived = pltpu.make_async_remote_copy(
            src_ref=par_send,
            dst_ref=par_recv.at[source],
            send_sem=par_ssem.at[source],
            recv_sem=par_rsem.at[source],
            device_id=(lax.rem(a + 1, nx), b),
            device_id_type=MESH,
        )

        @pl.when(jnp.logical_not(self_copy))
        def _():
            arrived.wait_recv()

        return carry

    lax.fori_loop(0, nx, par_wait, 0)
    for source in range(nx):
        for layer in range(2):
            par_ring[layer, source : source + 1, :] = par_recv[source, layer : layer + 1, :]

    oy = a - nx // 2
    oy_f = oy.astype(F32)

    def far_step(index, carry):
        acc0, acc1 = carry
        ox = index - nx // 2
        ox_f = ox.astype(F32)
        keep = (ox > 1) | (ox < -1) | (oy > 1) | (oy < -1)
        const = ox_f * ox_f + oy_f * oy_f + SOFT / 4
        for chunk in range(8):
            rows = pl.ds(32 * chunk, 32)
            flat = tables[0, rows, :] + ox_f * tables[1, rows, :] + oy_f * tables[2, rows, :]
            flat = flat + const
            lift = tables[3, rows, :]
            for slot, value in enumerate((flat + 1.0 - lift, flat, flat + 1.0 + lift)):
                high, low = split(jnp.where(keep, lax.rsqrt(value), 0.0))
                m_hi[slot, rows, :] = high
                m_lo[slot, rows, :] = low
        turn = lax.rem(nx + nx // 2 - index, nx)
        p0h, p0l = split(pltpu.roll(par_ring[0], turn, 0))
        p1h, p1l = split(pltpu.roll(par_ring[1], turn, 0))
        same = bdot(jnp.concatenate([p0h, p1h, p0l, p1l], axis=0), m_hi[1])
        same2 = bdot(jnp.concatenate([p0h, p1h], axis=0), m_lo[1])
        up = bdot(jnp.concatenate([p1h, p1l], axis=0), m_hi[2])
        up2 = bdot(p1h, m_lo[2])
        down = bdot(jnp.concatenate([p0h, p0l], axis=0), m_hi[0])
        down2 = bdot(p0h, m_lo[0])
        acc0 = acc0 + ((same[0:16] + up[0:16]) + (same[32:48] + same2[0:16] + up[16:32] + up2))
        acc1 = acc1 + (
            (same[16:32] + down[0:16]) + (same[48:64] + same2[16:32] + down[16:32] + down2)
        )
        return acc0, acc1

    zero16 = jnp.zeros((16, 256), F32)
    far0, far1 = lax.fori_loop(0, nx, far_step, (zero16, zero16))
    for target in range(nx):
        rs_send[target, 2] = jnp.where(
            row8 == 0,
            0.5 * far0[target : target + 1, :],
            jnp.where(row8 == 1, 0.5 * far1[target : target + 1, :], 0.0),
        )

    dy, half_z = leaf_task(a)

    def leaf_wait(source, carry):
        for py in range(2):
            valid, row, src_py = leaf_route(a, py)
            self_copy = (source == a) & (row == 0)
            arrived = pltpu.make_async_remote_copy(
                src_ref=leaf_send.at[0],
                dst_ref=leaf_recv.at[source, py],
                send_sem=leaf_ssem.at[source, py],
                recv_sem=leaf_rsem.at[source, py],
                device_id=(lax.rem(a + 1, nx), b),
                device_id_type=MESH,
            )

            @pl.when(valid & jnp.logical_not(self_copy))
            def _():
                arrived.wait_recv()

        return carry

    lax.fori_loop(0, nx, leaf_wait, 0)

    @pl.when(dy == 3)
    def _():
        leaf_recv[:, 1] = jnp.zeros((nx, 8, 256), F32)

    @pl.when(dy == -3)
    def _():
        leaf_recv[:, 0] = jnp.zeros((nx, 8, 256), F32)

    for target in range(nx):
        rs_send[target, 0] = jnp.zeros((8, 256), F32)
        rs_send[target, 1] = jnp.zeros((8, 256), F32)

    @pl.when(a < 14)
    def _():
        for source in range(nx):
            low_py = leaf_recv[source, 0]
            high_py = leaf_recv[source, 1]
            first = row8 < 4
            shifted[0, 8 * source : 8 * source + 8, :] = jnp.where(
                first, low_py, pltpu.roll(high_py, 4, 0)
            )
            shifted[1, 8 * source : 8 * source + 8, :] = jnp.where(
                first, pltpu.roll(low_py, 4, 0), high_py
            )
        dy_f = dy.astype(F32)
        row128 = lax.broadcasted_iota(jnp.int32, (128, 256), 0) % 4

        def leaf_step(step, carry):
            dz = jnp.where(half_z == 0, step - 3, step + 1)

            @pl.when(dz <= 3)
            def _():
                dz_f = dz.astype(F32)
                beside = (dy >= -1) & (dy <= 1) & (dz >= -1) & (dz <= 1)
                const = dy_f * dy_f + dz_f * dz_f + SOFT
                for chunk in range(8):
                    rows = pl.ds(32 * chunk, 32)
                    base = tables[0, rows, :] + dy_f * tables[2, rows, :]
                    base = base + dz_f * tables[3, rows, :] + const
                    along = tables[1, rows, :]
                    for slot in range(7):
                        dx = slot - 3
                        value = base + (float(dx) * along + float(dx * dx)) if dx else base
                        kernel = lax.rsqrt(value)
                        if abs(dx) <= 1:
                            kernel = jnp.where(beside, 0.0, kernel)
                        high, low = split(kernel)
                        m_hi[slot, rows, :] = high
                        m_lo[slot, rows, :] = low
                inside = (row128 + dz >= 0) & (row128 + dz <= 3)
                turn = lax.rem(128 - dz, 128)
                for sx in range(2):
                    moved = jnp.where(inside, pltpu.roll(shifted[sx], turn, 0), 0.0)
                    for block in (-1, 0, 1):
                        if block == -1:
                            placed = jnp.concatenate([moved[120:], moved[:120]], axis=0)
                        elif block == 1:
                            placed = jnp.concatenate([moved[8:], moved[:8]], axis=0)
                        else:
                            placed = moved
                        slot = 2 * block + sx + 2
                        high, low = split(placed)
                        l_hi[slot] = high
                        l_lo[slot] = low
                for px in range(2):
                    total = jnp.zeros((128, 256), F32)
                    for slot in range(6):
                        matrix = slot + 1 - px
                        total = total + (
                            bdot(l_hi[slot], m_hi[matrix])
                            + (bdot(l_lo[slot], m_hi[matrix]) + bdot(l_hi[slot], m_lo[matrix]))
                        )
                    rs_send[:, px] = rs_send[:, px] + total.reshape(nx, 8, 256)

            return carry

        lax.fori_loop(0, 4, leaf_step, 0)

    def rs_copy(target):
        return pltpu.make_async_remote_copy(
            src_ref=rs_send.at[target],
            dst_ref=rs_recv.at[a],
            send_sem=rs_ssem.at[target],
            recv_sem=rs_rsem.at[a],
            device_id=(target, b),
            device_id_type=MESH,
        )

    def rs_start(step, carry):
        rs_copy(lax.rem(a + step, nx)).start()
        return carry

    lax.fori_loop(1, nx, rs_start, 0)
    rs_recv[a] = rs_send[a]

    for index in range(8):
        halo_copy(7 - index).wait_recv()
    for strip in range(4):
        if strip < 2:
            cells = [(3 * strip, fy) for fy in range(4)]
        else:
            cells = [(1, 3 * (strip - 2)), (2, 3 * (strip - 2))]
        side_x, side_y, side_z, side_w = [
            jnp.concatenate(
                [halo[fx, fy, 4 * comp : 4 * comp + 4, :] for fx, fy in cells], axis=0
            )
            for comp in range(4)
        ]
        size = 4 * len(cells)
        place = lax.broadcasted_iota(jnp.int32, (size, 128), 0) // 4
        if strip < 2:
            side_x = side_x + float(3 * strip - 2)
            side_y = side_y + (place - 2).astype(F32)
        else:
            side_x = side_x + (place - 1).astype(F32)
            side_y = side_y + float(3 * (strip - 2) - 2)
        for index, value in enumerate(source_rows(side_x, side_y, side_z - 0.5)):
            feat[size * index : size * index + size, :] = value
        feat[pl.ds(24 * size, 8 * size), :] = jnp.zeros((8 * size, 128), F32)
        for cell in range(len(cells)):
            for layer in range(4):
                block = feat[pl.ds(4 * cell + layer, 32, stride=size), :].astype(BF16)
                row = side_w[4 * cell + layer : 4 * cell + layer + 1, :]
                if strip < 2:
                    bank_x[layer, strip, :, 128 * cell : 128 * cell + 128] = block
                    w_x[layer, strip, 0:1, 128 * cell : 128 * cell + 128] = row
                else:
                    bank_y[layer, strip - 2, :, 128 * cell : 128 * cell + 128] = block
                    w_y[layer, strip - 2, 0:1, 128 * cell : 128 * cell + 128] = row
    for turn in (1, 0, 2):
        near_halo(turn)

    def rs_wait(step, carry):
        source = lax.rem(a + step, nx)
        pltpu.make_async_remote_copy(
            src_ref=rs_send.at[source],
            dst_ref=rs_recv.at[source],
            send_sem=rs_ssem.at[source],
            recv_sem=rs_rsem.at[source],
            device_id=(source, b),
            device_id_type=MESH,
        ).wait_recv()
        return carry

    lax.fori_loop(1, nx, rs_wait, 0)
    sums = [jnp.zeros((8, 256), F32) for _ in range(3)]
    for source in range(nx):
        for part in range(3):
            sums[part] = sums[part] + rs_recv[source, part]

    fetches[7].wait()
    fetches[8].wait()
    leaf_local = dot_t(jnp.concatenate([sums[0], sums[1]], axis=0), cl_down[...])
    parent_local = 0.5 * dot_t(sums[2], ct_down[...])
    lanes = lax.broadcasted_iota(jnp.int32, (128, 128), 1)
    columns = jnp.zeros((128, 128), F32)
    for box in range(16):
        layer = (box % 4) // 2
        value = k_leaf[box] * leaf_local[box : box + 1, :]
        value = value + k_parent[box] * parent_local[layer : layer + 1, :]
        value = value[:, :128] + value[:, 128:] + near_acc[box]
        column = jnp.sum(value, axis=1, keepdims=True)
        columns = jnp.where(lanes == box, column, columns)
    flipped = jnp.transpose(columns)
    for px in range(2):
        for py in range(2):
            for k in range(4):
                box = (px * 2 + py) * 4 + k
                row = flipped[box : box + 1, :]
                out_ref[px, py, k : k + 1, :] = jnp.where(
                    lane128[0:1] < counts_ref[px, py, k], row, 0.0
                )

    for index in range(8):
        halo_copy(index).wait_send()

    def drain(target, carry):
        for py in range(2):
            valid, self_copy, _, copy = leaf_copy(target, py)

            @pl.when(valid & jnp.logical_not(self_copy))
            def _():
                copy.wait_send()

        own, copy = par_copy(target)

        @pl.when(jnp.logical_not(own))
        def _():
            copy.wait_send()

        @pl.when(target != a)
        def _():
            rs_copy(target).wait_send()

        return carry

    lax.fori_loop(0, nx, drain, 0)


def shards(offsets, charges, counts, cl_up, cl_down, ct_up, ct_down):
    nx = lax.axis_size("gx")
    ny = lax.axis_size("gy")
    points = sphere_points(256)
    unit = np.zeros((8, 256), np.float32)
    unit[:3] = points
    unit_t = np.zeros((256, 8), np.float32)
    unit_t[:, :3] = points.T
    vmem = pl.BlockSpec(memory_space=pltpu.VMEM)
    dma = pltpu.SemaphoreType.DMA
    return pl.pallas_call(
        functools.partial(body, nx, ny),
        out_shape=jax.ShapeDtypeStruct(charges.shape, F32),
        in_specs=[pl.BlockSpec(memory_space=pl.ANY)] * 9,
        out_specs=vmem,
        scratch_shapes=[
            pltpu.SMEM(counts.shape, jnp.int32),
            pltpu.VMEM(offsets.shape, F32),
            pltpu.VMEM(charges.shape, F32),
            pltpu.VMEM(unit.shape, F32),
            pltpu.VMEM(unit_t.shape, F32),
            pltpu.VMEM((256, 256), F32),
            pltpu.VMEM((256, 256), F32),
            pltpu.VMEM((256, 256), F32),
            pltpu.VMEM((256, 256), F32),
            dma((9,)),
            pltpu.VMEM((4, 4, 16, 128), F32),
            pltpu.VMEM((4, 256, 256), F32),
            pltpu.VMEM((16, 128, 256), F32),
            pltpu.VMEM((16, 128, 256), F32),
            pltpu.VMEM((8, 256, 256), BF16),
            pltpu.VMEM((8, 256, 256), BF16),
            pltpu.VMEM((2, 8, 256), F32),
            pltpu.VMEM((nx, 2, 8, 256), F32),
            pltpu.VMEM((2, 256), F32),
            pltpu.VMEM((nx, 2, 256), F32),
            pltpu.VMEM((nx, 3, 8, 256), F32),
            pltpu.VMEM((nx, 3, 8, 256), F32),
            pltpu.VMEM((2, 8 * nx, 256), F32),
            pltpu.VMEM((2, nx, 256), F32),
            pltpu.VMEM((7, 256, 256), BF16),
            pltpu.VMEM((7, 256, 256), BF16),
            pltpu.VMEM((6, 8 * nx, 256), BF16),
            pltpu.VMEM((6, 8 * nx, 256), BF16),
            pltpu.VMEM((16, 128, 128), F32),
            pltpu.VMEM((3, 16, 128, 32), BF16),
            pltpu.VMEM((512, 128), F32),
            pltpu.VMEM((4, 32, 512), BF16),
            pltpu.VMEM((4, 2, 32, 512), BF16),
            pltpu.VMEM((4, 2, 32, 256), BF16),
            pltpu.VMEM((4, 8, 512), F32),
            pltpu.VMEM((4, 2, 8, 512), F32),
            pltpu.VMEM((4, 2, 8, 256), F32),
            dma((8,)),
            dma((8,)),
            dma((nx, 2)),
            dma((nx, 2)),
            dma((nx,)),
            dma((nx,)),
            dma((nx,)),
            dma((nx,)),
        ],
        compiler_params=pltpu.CompilerParams(
            has_side_effects=True, collective_id=0, vmem_limit_bytes=56 * 1024 * 1024
        ),
        name="multipole",
    )(counts, offsets, charges, jnp.asarray(unit), jnp.asarray(unit_t), cl_up, cl_down, ct_up, ct_down)


def solution(mesh):
    return jax.shard_map(
        shards,
        mesh=mesh,
        in_specs=(
            P(None, "gx", "gy", None, None),
            P("gx", "gy", None, None),
            P("gx", "gy", None),
            P(),
            P(),
            P(),
            P(),
        ),
        out_specs=P("gx", "gy", None, None),
        check_vma=False,
    )
```

```python
import functools

import jax
import jax.numpy as jnp
import numpy as np
from jax import lax
from jax.experimental import pallas as pl
from jax.experimental.pallas import tpu as pltpu
from jax.sharding import PartitionSpec as P

SOFT = 0.0004
F32 = jnp.float32
BF16 = jnp.bfloat16
HIGHEST = lax.Precision.HIGHEST
MESH = pl.DeviceIdType.MESH
SIDES = [(sx, sy) for sx in (-1, 0, 1) for sy in (-1, 0, 1) if (sx, sy) != (0, 0)]


def sphere_points(count):
    middle = np.arange(count).astype(np.float32) + np.float32(0.5)
    height = (np.float32(1.0) - np.float32(2.0) * middle / np.float32(count)).astype(np.float32)
    radial = np.sqrt(np.maximum(np.float32(1.0) - height * height, np.float32(0.0)))
    turn = (middle * np.float32(2.399963229728653)).astype(np.float32)
    cos = np.cos(turn.astype(np.float64)).astype(np.float32)
    sin = np.sin(turn.astype(np.float64)).astype(np.float32)
    return np.stack([radial * cos, radial * sin, height]).astype(np.float32)


def split(value):
    high = value.astype(BF16)
    low = (value - high.astype(F32)).astype(BF16)
    return high, low


def pieces(value):
    first = value.astype(BF16).astype(F32)
    rest = value - first
    second = rest.astype(BF16).astype(F32)
    return first, second, rest - second


def bdot(a, b):
    return jnp.dot(a, b, preferred_element_type=F32)


def dot_t(a, b):
    return lax.dot_general(
        a, b, (((1,), (1,)), ((), ())), precision=HIGHEST, preferred_element_type=F32
    )


def leaf_task(a):
    return a // 2 - 3, a % 2


def body(
    nx,
    ny,
    counts_hbm,
    off_hbm,
    chg_hbm,
    u_hbm,
    ut_hbm,
    cl_up_hbm,
    cl_down_hbm,
    ct_up_hbm,
    ct_down_hbm,
    out_ref,
    counts_ref,
    off_ref,
    chg_ref,
    u_ref,
    ut_ref,
    cl_up,
    cl_down,
    ct_up,
    ct_down,
    in_sem,
    halo,
    tables,
    k_leaf,
    k_parent,
    up_hi,
    up_lo,
    leaf_send,
    leaf_recv,
    par_send,
    par_recv,
    rs_send,
    rs_recv,
    shifted,
    par_ring,
    m_hi,
    m_lo,
    l_three,
    m_three,
    lines,
    near_acc,
    near_lhs,
    feat,
    bank_own,
    bank_x,
    bank_y,
    w_own,
    w_x,
    w_y,
    halo_ssem,
    halo_rsem,
    leaf_ssem,
    leaf_rsem,
    par_ssem,
    par_rsem,
    rs_ssem,
    rs_rsem,
):
    a = lax.axis_index("gx")
    b = lax.axis_index("gy")
    lane128 = lax.broadcasted_iota(jnp.int32, (4, 128), 1)

    fetches = [
        pltpu.make_async_copy(src, dst, in_sem.at[index])
        for index, (src, dst) in enumerate(
            (
                (counts_hbm, counts_ref),
                (off_hbm, off_ref),
                (chg_hbm, chg_ref),
                (u_hbm, u_ref),
                (ut_hbm, ut_ref),
                (cl_up_hbm, cl_up),
                (ct_up_hbm, ct_up),
                (cl_down_hbm, cl_down),
                (ct_down_hbm, ct_down),
            )
        )
    ]
    for fetch in fetches:
        fetch.start()

    barrier = pltpu.get_barrier_semaphore()

    def hello(to_a, to_b):
        pl.semaphore_signal(barrier, inc=1, device_id=(to_a, to_b), device_id_type=MESH)

    def hello_row(step, carry):
        hello(lax.rem(a + step, nx), b)
        return carry

    lax.fori_loop(1, nx, hello_row, 0)
    for sx, sy in SIDES:
        hello(lax.rem(a + sx + nx, nx), lax.rem(b + sy + ny, ny))
    task_dy, _ = leaf_task(a)
    leaf_row = jnp.where(task_dy > 0, 1, -1)
    far_b = lax.rem(b + a - nx // 2 + ny, ny)

    def hello_far(step, carry):
        to_a = lax.rem(a + step, nx)

        @pl.when((a < 14) & (task_dy != 0))
        def _():
            hello(to_a, lax.rem(b + leaf_row + ny, ny))

        @pl.when((to_a != a) | (far_b != b))
        def _():
            hello(to_a, far_b)

        return carry

    lax.fori_loop(0, nx, hello_far, 0)
    for fetch in fetches[:5]:
        fetch.wait()

    for px in range(2):
        for py in range(2):
            cell = halo.at[1 + px, 1 + py]
            for comp in range(3):
                cell[4 * comp : 4 * comp + 4, :] = off_ref[comp, px, py]
            for k in range(4):
                row = chg_ref[px, py, k : k + 1, :]
                cell[12 + k : 13 + k, :] = jnp.where(
                    lane128[0:1] < counts_ref[px, py, k], row, 0.0
                )

    def halo_copy(index):
        sx, sy = SIDES[index]
        src_x = pl.ds(1, 2) if sx == 0 else pl.ds(2 if sx == 1 else 1, 1)
        src_y = pl.ds(1, 2) if sy == 0 else pl.ds(2 if sy == 1 else 1, 1)
        dst_x = pl.ds(1, 2) if sx == 0 else pl.ds(0 if sx == 1 else 3, 1)
        dst_y = pl.ds(1, 2) if sy == 0 else pl.ds(0 if sy == 1 else 3, 1)
        return pltpu.make_async_remote_copy(
            src_ref=halo.at[src_x, src_y],
            dst_ref=halo.at[dst_x, dst_y],
            send_sem=halo_ssem.at[index],
            recv_sem=halo_rsem.at[index],
            device_id=(lax.rem(a + sx + nx, nx), lax.rem(b + sy + ny, ny)),
            device_id_type=MESH,
        )

    for chunk in range(8):
        rows = pl.ds(32 * chunk, 32)
        total = jnp.zeros((32, 256), F32)
        for comp in range(3):
            diff = 0.9 * (u_ref[comp : comp + 1, :] - ut_ref[rows, comp : comp + 1])
            tables[1 + comp, rows, :] = -2.0 * diff
            total = total + diff * diff
            if comp == 0:
                for dx in (-3, -2, -1, 1, 2, 3):
                    lines[dx + 3, rows, :] = (-2.0 * dx) * diff + float(dx * dx)
        tables[0, rows, :] = total

    def child_chunk(chunk, carry):
        rows = pl.ds(pl.multiple_of(32 * chunk, 32), 32)
        base = jnp.full((32, 256), 0.1875 + SOFT / 4, F32)
        half = []
        for comp in range(3):
            diff = 1.8 * u_ref[comp : comp + 1, :] - 0.45 * ut_ref[rows, comp : comp + 1]
            base = base + diff * diff
            half.append(0.5 * diff)
        for child in range(8):
            value = base
            for comp, bit in enumerate((child // 4, child // 2 % 2, child % 2)):
                value = value + half[comp] if bit == 0 else value - half[comp]
            high, low = split(lax.rsqrt(value))
            up_hi[child, rows, :] = high
            up_lo[child, rows, :] = low
        return carry

    lax.fori_loop(0, 8, child_chunk, 0)

    centre = [0.5 + 1.8 * u_ref[comp : comp + 1, :] for comp in range(3)]
    checks = []
    for px in range(2):
        for py in range(2):
            turned = jnp.transpose(halo[1 + px, 1 + py])
            for k in range(4):
                box = (px * 2 + py) * 4 + k
                total = jnp.full((128, 256), SOFT, F32)
                for comp in range(3):
                    diff = centre[comp] - turned[:, 4 * comp + k : 4 * comp + k + 1]
                    total = total + diff * diff
                kernel = lax.rsqrt(total)
                k_leaf[box] = kernel
                weight = turned[:, 12 + k : 13 + k]
                checks.append(jnp.sum(kernel * weight, axis=0, keepdims=True))
    leaf_check = jnp.concatenate(checks, axis=0)
    fetches[5].wait()
    leaf_eq = dot_t(leaf_check, cl_up[...])
    for px in range(2):
        for py in range(2):
            first = (px * 2 + py) * 4
            leaf_send[py, 4 * px : 4 * px + 4, :] = leaf_eq[first : first + 4, :]

    eq_hi, eq_lo = split(leaf_eq)
    both = jnp.concatenate([eq_hi, eq_lo], axis=0)
    row16 = lax.broadcasted_iota(jnp.int32, (16, 256), 0)
    rows_sum = jnp.zeros((16, 256), F32)
    for child in range(8):
        first = bdot(both, up_hi[child])
        term = first[:16] + first[16:] + bdot(eq_hi, up_lo[child])
        mine = ((row16 // 4) == (child // 2)) & ((row16 % 2) == (child % 2))
        rows_sum = jnp.where(mine, term, rows_sum)
    upper = (row16 % 4) >= 2
    check0 = 0.5 * jnp.sum(jnp.where(upper, 0.0, rows_sum), axis=0, keepdims=True)
    check1 = 0.5 * jnp.sum(jnp.where(upper, rows_sum, 0.0), axis=0, keepdims=True)
    row8 = lax.broadcasted_iota(jnp.int32, (8, 256), 0)
    parent_check = jnp.where(row8 == 0, check0, jnp.where(row8 == 1, check1, 0.0))
    fetches[6].wait()
    par_send[...] = dot_t(parent_check, ct_up[...])[0:2]

    def source_rows(x, y, z):
        rows = []
        for value in (x, y, z):
            q1, q2, q3 = pieces(value)
            rows += [q1, q2, q1, q2, q3, q1]
        n1, n2, n3 = pieces((x * x + y * y) + (z * z + SOFT))
        one = jnp.ones_like(x)
        return rows + [n1, n2, n3, one, one, one]

    def target_rows(x, y, z):
        rows = []
        for value in (x, y, z):
            p1, p2, p3 = [-2.0 * part for part in pieces(value)]
            rows += [p1, p1, p2, p2, p1, p3]
        one = jnp.ones_like(x)
        n1, n2, n3 = pieces((x * x + y * y) + z * z)
        return rows + [one, one, one, n1, n2, n3]

    box_row = lax.broadcasted_iota(jnp.int32, (16, 128), 0)
    own_x, own_y, own_z, own_w = [
        jnp.concatenate(
            [halo[1 + px, 1 + py, 4 * comp : 4 * comp + 4, :] for px in (0, 1) for py in (0, 1)],
            axis=0,
        )
        for comp in range(4)
    ]
    own_x = own_x + ((box_row // 8) - 1).astype(F32)
    own_y = own_y + ((box_row // 4 % 2) - 1).astype(F32)
    own_z = own_z - 0.5
    feat[pl.ds(384, 128), :] = jnp.zeros((128, 128), F32)
    for index, value in enumerate(source_rows(own_x, own_y, own_z)):
        feat[16 * index : 16 * index + 16, :] = value
    for column in range(4):
        for layer in range(4):
            block = feat[pl.ds(4 * column + layer, 32, stride=16), :]
            bank_own[layer, :, 128 * column : 128 * column + 128] = block.astype(BF16)
            row = own_w[4 * column + layer : 4 * column + layer + 1, :]
            w_own[layer, 0:1, 128 * column : 128 * column + 128] = row
    for turn in range(3):
        for index, value in enumerate(target_rows(own_x, own_y, own_z - float(turn - 1))):
            feat[16 * index : 16 * index + 16, :] = value
        for box in range(16):
            block = feat[pl.ds(box, 32, stride=16), :]
            near_lhs[turn, box] = jnp.transpose(block).astype(BF16)

    lane512 = lax.broadcasted_iota(jnp.int32, (128, 512), 1)
    row512 = lax.broadcasted_iota(jnp.int32, (128, 512), 0)

    def fold(value):
        total = value[:, 0:128]
        for first in range(128, value.shape[1], 128):
            total = total + value[:, first : first + 128]
        return total

    def near_own(turn):
        low = max(0, 1 - turn)

        def step(layer, carry):
            source = layer + turn - 1
            for column in range(4):
                box = 4 * column + layer
                kernel = lax.rsqrt(bdot(near_lhs[turn, box], bank_own[source]))
                if turn == 1:
                    kernel = jnp.where(lane512 == row512 + 128 * column, 0.0, kernel)
                value = fold(kernel * w_own[source, 0:1, :])
                near_acc[box] = value if turn == 1 else near_acc[box] + value
            return carry

        lax.fori_loop(low, low + 4 - abs(turn - 1), step, 0)

    def near_halo(turn):
        low = max(0, 1 - turn)

        def step(layer, carry):
            source = layer + turn - 1
            for column in range(4):
                box = 4 * column + layer
                px = column // 2
                py = column % 2
                lanes = pl.ds(128 * py, 384)
                lhs = near_lhs[turn, box]
                value = lax.rsqrt(bdot(lhs, bank_x[source, px, :, lanes]))
                value = fold(value * w_x[source, px, 0:1, lanes])
                other = lax.rsqrt(bdot(lhs, bank_y[source, py]))
                other = fold(other * w_y[source, py, 0:1, :])
                near_acc[box] = near_acc[box] + (value + other)
            return carry

        lax.fori_loop(low, low + 4 - abs(turn - 1), step, 0)

    def leaf_route(target, py):
        dy, _ = leaf_task(target)
        src = py + dy
        valid = (target < 14) & (src >= -2) & (src <= 3)
        row = (src + 4) // 2 - 2
        return valid, row, (src + 4) % 2

    def leaf_copy(target, py):
        valid, row, src_py = leaf_route(target, py)
        to_b = lax.rem(b - row + ny, ny)
        copy = pltpu.make_async_remote_copy(
            src_ref=leaf_send.at[src_py],
            dst_ref=leaf_recv.at[a, py],
            send_sem=leaf_ssem.at[target, py],
            recv_sem=leaf_rsem.at[a, py],
            device_id=(target, to_b),
            device_id_type=MESH,
        )
        self_copy = (target == a) & (to_b == b)
        return valid, self_copy, src_py, copy

    def leaf_start(target, carry):
        for py in range(2):
            valid, self_copy, src_py, copy = leaf_copy(target, py)

            @pl.when(valid & jnp.logical_not(self_copy))
            def _():
                copy.start()

            @pl.when(valid & self_copy)
            def _():
                leaf_recv[a, py] = leaf_send[src_py]

        return carry

    def par_copy(target):
        to_b = lax.rem(b - target + nx // 2 + ny, ny)
        copy = pltpu.make_async_remote_copy(
            src_ref=par_send,
            dst_ref=par_recv.at[a],
            send_sem=par_ssem.at[target],
            recv_sem=par_rsem.at[a],
            device_id=(target, to_b),
            device_id_type=MESH,
        )
        return (target == a) & (to_b == b), copy

    def par_start(target, carry):
        self_copy, copy = par_copy(target)

        @pl.when(jnp.logical_not(self_copy))
        def _():
            copy.start()

        @pl.when(self_copy)
        def _():
            par_recv[a] = par_send[...]

        return carry

    for px in range(2):
        for py in range(2):
            turned = jnp.transpose(halo[1 + px, 1 + py])
            for k in range(4):
                box = (px * 2 + py) * 4 + k
                total = jnp.full((128, 256), SOFT / 4, F32)
                for comp, bit in enumerate((px, py, k % 2)):
                    place = 0.5 * turned[:, 4 * comp + k : 4 * comp + k + 1] + 0.5 * bit
                    diff = centre[comp] - place
                    total = total + diff * diff
                k_parent[box] = lax.rsqrt(total)

    pl.semaphore_wait(barrier, (nx - 1) + 8 + 12 + jnp.where(a == nx // 2, nx - 1, nx))
    lax.fori_loop(0, nx, par_start, 0)
    lax.fori_loop(0, nx, leaf_start, 0)
    for index in range(8):
        halo_copy(index).start()

    for turn in (1, 0, 2):
        near_own(turn)

    def par_wait(source, carry):
        from_b = lax.rem(b + a - nx // 2 + ny, ny)
        self_copy = (source == a) & (from_b == b)
        arrived = pltpu.make_async_remote_copy(
            src_ref=par_send,
            dst_ref=par_recv.at[source],
            send_sem=par_ssem.at[source],
            recv_sem=par_rsem.at[source],
            device_id=(lax.rem(a + 1, nx), b),
            device_id_type=MESH,
        )

        @pl.when(jnp.logical_not(self_copy))
        def _():
            arrived.wait_recv()

        return carry

    lax.fori_loop(0, nx, par_wait, 0)
    for source in range(nx):
        for layer in range(2):
            par_ring[layer, source : source + 1, :] = par_recv[source, layer : layer + 1, :]

    oy = a - nx // 2
    oy_f = oy.astype(F32)

    for chunk in range(8):
        rows = pl.ds(32 * chunk, 32)
        lines[7, rows, :] = tables[0, rows, :] + (
            oy_f * tables[2, rows, :] + (oy_f * oy_f + SOFT / 4)
        )

    def far_offset(index, first_slot, acc0, acc1):
        ox = index - nx // 2
        ox_f = ox.astype(F32)
        keep = (ox > 1) | (ox < -1) | (oy > 1) | (oy < -1)
        for chunk in range(8):
            rows = pl.ds(32 * chunk, 32)
            flat = lines[7, rows, :] + (ox_f * tables[1, rows, :] + ox_f * ox_f)
            tall = flat + 1.0
            lift = tables[3, rows, :]
            for slot, value in enumerate((tall - lift, flat, tall + lift)):
                high, low = split(lax.rsqrt(value))
                m_hi[first_slot + slot, rows, :] = high
                m_lo[first_slot + slot, rows, :] = low
        turn = lax.rem(nx + nx // 2 - index, nx)
        p0h, p0l = split(jnp.where(keep, pltpu.roll(par_ring[0], turn, 0), 0.0))
        p1h, p1l = split(jnp.where(keep, pltpu.roll(par_ring[1], turn, 0), 0.0))
        same = bdot(jnp.concatenate([p0h, p1h, p0l, p1l], axis=0), m_hi[first_slot + 1])
        same2 = bdot(jnp.concatenate([p0h, p1h], axis=0), m_lo[first_slot + 1])
        up = bdot(jnp.concatenate([p1h, p1l], axis=0), m_hi[first_slot + 2])
        up2 = bdot(p1h, m_lo[first_slot + 2])
        down = bdot(jnp.concatenate([p0h, p0l], axis=0), m_hi[first_slot])
        down2 = bdot(p0h, m_lo[first_slot])
        acc0 = acc0 + ((same[0:16] + up[0:16]) + (same[32:48] + same2[0:16] + up[16:32] + up2))
        acc1 = acc1 + (
            (same[16:32] + down[0:16]) + (same[48:64] + same2[16:32] + down[16:32] + down2)
        )
        return acc0, acc1

    def far_step(index, carry):
        carry = far_offset(2 * index, 0, *carry)
        return far_offset(2 * index + 1, 3, *carry)

    zero16 = jnp.zeros((16, 256), F32)
    far0, far1 = lax.fori_loop(0, nx // 2, far_step, (zero16, zero16))
    for target in range(nx):
        rs_send[target, 2] = jnp.where(
            row8 == 0,
            0.5 * far0[target : target + 1, :],
            jnp.where(row8 == 1, 0.5 * far1[target : target + 1, :], 0.0),
        )

    dy, half_z = leaf_task(a)

    def leaf_wait(source, carry):
        for py in range(2):
            valid, row, src_py = leaf_route(a, py)
            self_copy = (source == a) & (row == 0)
            arrived = pltpu.make_async_remote_copy(
                src_ref=leaf_send.at[0],
                dst_ref=leaf_recv.at[source, py],
                send_sem=leaf_ssem.at[source, py],
                recv_sem=leaf_rsem.at[source, py],
                device_id=(lax.rem(a + 1, nx), b),
                device_id_type=MESH,
            )

            @pl.when(valid & jnp.logical_not(self_copy))
            def _():
                arrived.wait_recv()

        return carry

    lax.fori_loop(0, nx, leaf_wait, 0)

    @pl.when(dy == 3)
    def _():
        leaf_recv[:, 1] = jnp.zeros((nx, 8, 256), F32)

    @pl.when(dy == -3)
    def _():
        leaf_recv[:, 0] = jnp.zeros((nx, 8, 256), F32)

    for target in range(nx):
        rs_send[target, 0] = jnp.zeros((8, 256), F32)
        rs_send[target, 1] = jnp.zeros((8, 256), F32)

    @pl.when(a < 14)
    def _():
        for source in range(nx):
            low_py = leaf_recv[source, 0]
            high_py = leaf_recv[source, 1]
            first = row8 < 4
            shifted[0, 8 * source : 8 * source + 8, :] = jnp.where(
                first, low_py, pltpu.roll(high_py, 4, 0)
            )
            shifted[1, 8 * source : 8 * source + 8, :] = jnp.where(
                first, pltpu.roll(low_py, 4, 0), high_py
            )
        dy_f = dy.astype(F32)
        row128 = lax.broadcasted_iota(jnp.int32, (128, 256), 0) % 4

        def leaf_step(step, carry):
            dz = jnp.where(half_z == 0, step - 3, step + 1)

            @pl.when(dz <= 3)
            def _():
                dz_f = dz.astype(F32)
                beside = (dy >= -1) & (dy <= 1) & (dz >= -1) & (dz <= 1)
                inside = (row128 + dz >= 0) & (row128 + dz <= 3)
                turn = lax.rem(128 - dz, 128)
                for sx in range(2):
                    moved = jnp.where(inside, pltpu.roll(shifted[sx], turn, 0), 0.0)
                    for block in (-1, 0, 1):
                        if block == -1:
                            placed = jnp.concatenate([moved[120:], moved[:120]], axis=0)
                        elif block == 1:
                            placed = jnp.concatenate([moved[8:], moved[:8]], axis=0)
                        else:
                            placed = moved
                        slot = 2 * block + sx + 2
                        high, low = split(placed)
                        l_three[slot, :, 0:256] = high
                        l_three[slot, :, 256:512] = low
                        l_three[slot, :, 512:768] = high
                const = dy_f * dy_f + dz_f * dz_f + SOFT
                for chunk in range(8):
                    rows = pl.ds(32 * chunk, 32)
                    base = tables[0, rows, :] + dy_f * tables[2, rows, :]
                    lines[7, rows, :] = base + (dz_f * tables[3, rows, :] + const)
                totals = [rs_send[:, px].reshape(8 * nx, 256) for px in range(2)]
                for matrix in range(7):
                    dx = matrix - 3
                    for chunk in range(8):
                        rows = pl.ds(32 * chunk, 32)
                        value = lines[7, rows, :]
                        if dx:
                            value = value + lines[matrix, rows, :]
                        kernel = lax.rsqrt(value)
                        if abs(dx) <= 1:
                            kernel = jnp.where(beside, 0.0, kernel)
                        high, low = split(kernel)
                        m_three[matrix, 32 * chunk : 32 * chunk + 32, :] = high
                        m_three[matrix, 256 + 32 * chunk : 288 + 32 * chunk, :] = high
                        m_three[matrix, 512 + 32 * chunk : 544 + 32 * chunk, :] = low
                    for px in range(2):
                        slot = matrix - 1 + px
                        if 0 <= slot < 6:
                            totals[px] = totals[px] + bdot(l_three[slot], m_three[matrix])
                for px in range(2):
                    rs_send[:, px] = totals[px].reshape(nx, 8, 256)

            return carry

        lax.fori_loop(0, 4, leaf_step, 0)

    def rs_copy(target):
        return pltpu.make_async_remote_copy(
            src_ref=rs_send.at[target],
            dst_ref=rs_recv.at[a],
            send_sem=rs_ssem.at[target],
            recv_sem=rs_rsem.at[a],
            device_id=(target, b),
            device_id_type=MESH,
        )

    def rs_start(step, carry):
        rs_copy(lax.rem(a + step, nx)).start()
        return carry

    lax.fori_loop(1, nx, rs_start, 0)
    rs_recv[a] = rs_send[a]

    for index in range(8):
        halo_copy(7 - index).wait_recv()
    for strip in range(4):
        if strip < 2:
            cells = [(3 * strip, fy) for fy in range(4)]
        else:
            cells = [(1, 3 * (strip - 2)), (2, 3 * (strip - 2))]
        side_x, side_y, side_z, side_w = [
            jnp.concatenate(
                [halo[fx, fy, 4 * comp : 4 * comp + 4, :] for fx, fy in cells], axis=0
            )
            for comp in range(4)
        ]
        size = 4 * len(cells)
        place = lax.broadcasted_iota(jnp.int32, (size, 128), 0) // 4
        if strip < 2:
            side_x = side_x + float(3 * strip - 2)
            side_y = side_y + (place - 2).astype(F32)
        else:
            side_x = side_x + (place - 1).astype(F32)
            side_y = side_y + float(3 * (strip - 2) - 2)
        for index, value in enumerate(source_rows(side_x, side_y, side_z - 0.5)):
            feat[size * index : size * index + size, :] = value
        feat[pl.ds(24 * size, 8 * size), :] = jnp.zeros((8 * size, 128), F32)
        for cell in range(len(cells)):
            for layer in range(4):
                block = feat[pl.ds(4 * cell + layer, 32, stride=size), :].astype(BF16)
                row = side_w[4 * cell + layer : 4 * cell + layer + 1, :]
                if strip < 2:
                    bank_x[layer, strip, :, 128 * cell : 128 * cell + 128] = block
                    w_x[layer, strip, 0:1, 128 * cell : 128 * cell + 128] = row
                else:
                    bank_y[layer, strip - 2, :, 128 * cell : 128 * cell + 128] = block
                    w_y[layer, strip - 2, 0:1, 128 * cell : 128 * cell + 128] = row
    for turn in (1, 0, 2):
        near_halo(turn)

    def rs_wait(step, carry):
        source = lax.rem(a + step, nx)
        pltpu.make_async_remote_copy(
            src_ref=rs_send.at[source],
            dst_ref=rs_recv.at[source],
            send_sem=rs_ssem.at[source],
            recv_sem=rs_rsem.at[source],
            device_id=(source, b),
            device_id_type=MESH,
        ).wait_recv()
        return carry

    lax.fori_loop(1, nx, rs_wait, 0)
    sums = [jnp.zeros((8, 256), F32) for _ in range(3)]
    for source in range(nx):
        for part in range(3):
            sums[part] = sums[part] + rs_recv[source, part]

    fetches[7].wait()
    fetches[8].wait()
    leaf_local = dot_t(jnp.concatenate([sums[0], sums[1]], axis=0), cl_down[...])
    parent_local = 0.5 * dot_t(sums[2], ct_down[...])
    lanes = lax.broadcasted_iota(jnp.int32, (128, 128), 1)
    columns = jnp.zeros((128, 128), F32)
    for box in range(16):
        layer = (box % 4) // 2
        value = k_leaf[box] * leaf_local[box : box + 1, :]
        value = value + k_parent[box] * parent_local[layer : layer + 1, :]
        value = value[:, :128] + value[:, 128:] + near_acc[box]
        column = jnp.sum(value, axis=1, keepdims=True)
        columns = jnp.where(lanes == box, column, columns)
    flipped = jnp.transpose(columns)
    for px in range(2):
        for py in range(2):
            for k in range(4):
                box = (px * 2 + py) * 4 + k
                row = flipped[box : box + 1, :]
                out_ref[px, py, k : k + 1, :] = jnp.where(
                    lane128[0:1] < counts_ref[px, py, k], row, 0.0
                )

    for index in range(8):
        halo_copy(index).wait_send()

    def drain(target, carry):
        for py in range(2):
            valid, self_copy, _, copy = leaf_copy(target, py)

            @pl.when(valid & jnp.logical_not(self_copy))
            def _():
                copy.wait_send()

        own, copy = par_copy(target)

        @pl.when(jnp.logical_not(own))
        def _():
            copy.wait_send()

        @pl.when(target != a)
        def _():
            rs_copy(target).wait_send()

        return carry

    lax.fori_loop(0, nx, drain, 0)


def shards(offsets, charges, counts, cl_up, cl_down, ct_up, ct_down):
    nx = lax.axis_size("gx")
    ny = lax.axis_size("gy")
    points = sphere_points(256)
    unit = np.zeros((8, 256), np.float32)
    unit[:3] = points
    unit_t = np.zeros((256, 8), np.float32)
    unit_t[:, :3] = points.T
    vmem = pl.BlockSpec(memory_space=pltpu.VMEM)
    dma = pltpu.SemaphoreType.DMA
    return pl.pallas_call(
        functools.partial(body, nx, ny),
        out_shape=jax.ShapeDtypeStruct(charges.shape, F32),
        in_specs=[pl.BlockSpec(memory_space=pl.ANY)] * 9,
        out_specs=vmem,
        scratch_shapes=[
            pltpu.SMEM(counts.shape, jnp.int32),
            pltpu.VMEM(offsets.shape, F32),
            pltpu.VMEM(charges.shape, F32),
            pltpu.VMEM(unit.shape, F32),
            pltpu.VMEM(unit_t.shape, F32),
            pltpu.VMEM((256, 256), F32),
            pltpu.VMEM((256, 256), F32),
            pltpu.VMEM((256, 256), F32),
            pltpu.VMEM((256, 256), F32),
            dma((9,)),
            pltpu.VMEM((4, 4, 16, 128), F32),
            pltpu.VMEM((4, 256, 256), F32),
            pltpu.VMEM((16, 128, 256), F32),
            pltpu.VMEM((16, 128, 256), F32),
            pltpu.VMEM((8, 256, 256), BF16),
            pltpu.VMEM((8, 256, 256), BF16),
            pltpu.VMEM((2, 8, 256), F32),
            pltpu.VMEM((nx, 2, 8, 256), F32),
            pltpu.VMEM((2, 256), F32),
            pltpu.VMEM((nx, 2, 256), F32),
            pltpu.VMEM((nx, 3, 8, 256), F32),
            pltpu.VMEM((nx, 3, 8, 256), F32),
            pltpu.VMEM((2, 8 * nx, 256), F32),
            pltpu.VMEM((2, nx, 256), F32),
            pltpu.VMEM((6, 256, 256), BF16),
            pltpu.VMEM((6, 256, 256), BF16),
            pltpu.VMEM((6, 8 * nx, 768), BF16),
            pltpu.VMEM((7, 768, 256), BF16),
            pltpu.VMEM((8, 256, 256), F32),
            pltpu.VMEM((16, 128, 128), F32),
            pltpu.VMEM((3, 16, 128, 32), BF16),
            pltpu.VMEM((512, 128), F32),
            pltpu.VMEM((4, 32, 512), BF16),
            pltpu.VMEM((4, 2, 32, 512), BF16),
            pltpu.VMEM((4, 2, 32, 256), BF16),
            pltpu.VMEM((4, 8, 512), F32),
            pltpu.VMEM((4, 2, 8, 512), F32),
            pltpu.VMEM((4, 2, 8, 256), F32),
            dma((8,)),
            dma((8,)),
            dma((nx, 2)),
            dma((nx, 2)),
            dma((nx,)),
            dma((nx,)),
            dma((nx,)),
            dma((nx,)),
        ],
        compiler_params=pltpu.CompilerParams(
            has_side_effects=True, collective_id=0, vmem_limit_bytes=56 * 1024 * 1024
        ),
        name="multipole",
    )(counts, offsets, charges, jnp.asarray(unit), jnp.asarray(unit_t), cl_up, cl_down, ct_up, ct_down)


def solution(mesh):
    return jax.shard_map(
        shards,
        mesh=mesh,
        in_specs=(
            P(None, "gx", "gy", None, None),
            P("gx", "gy", None, None),
            P("gx", "gy", None),
            P(),
            P(),
            P(),
            P(),
        ),
        out_specs=P("gx", "gy", None, None),
        check_vma=False,
    )
```

```python
import functools

import jax
import jax.numpy as jnp
import numpy as np
from jax import lax
from jax.experimental import pallas as pl
from jax.experimental.pallas import tpu as pltpu
from jax.sharding import PartitionSpec as P

SOFT = 0.0004
F32 = jnp.float32
BF16 = jnp.bfloat16
MESH = pl.DeviceIdType.MESH
SIDES = [(sx, sy) for sx in (-1, 0, 1) for sy in (-1, 0, 1) if (sx, sy) != (0, 0)]


def sphere_points(count):
    middle = np.arange(count).astype(np.float32) + np.float32(0.5)
    height = (np.float32(1.0) - np.float32(2.0) * middle / np.float32(count)).astype(np.float32)
    radial = np.sqrt(np.maximum(np.float32(1.0) - height * height, np.float32(0.0)))
    turn = (middle * np.float32(2.399963229728653)).astype(np.float32)
    cos = np.cos(turn.astype(np.float64)).astype(np.float32)
    sin = np.sin(turn.astype(np.float64)).astype(np.float32)
    return np.stack([radial * cos, radial * sin, height]).astype(np.float32)


def split(value):
    high = value.astype(BF16)
    low = (value - high.astype(F32)).astype(BF16)
    return high, low


def pieces(value):
    first = value.astype(BF16).astype(F32)
    rest = value - first
    second = rest.astype(BF16).astype(F32)
    return first, second, rest - second


def bdot(a, b):
    return jnp.dot(a, b, preferred_element_type=F32)


def wrap(value, size):
    if size & (size - 1) == 0:
        return value & (size - 1)
    return lax.rem(value + size, size)


def leaf_task(a):
    return a // 2 - 3, a % 2


def body(
    nx,
    ny,
    counts_hbm,
    off_hbm,
    chg_hbm,
    u_hbm,
    ut_hbm,
    cl_up_hbm,
    cl_down_hbm,
    ct_up_hbm,
    ct_down_hbm,
    out_ref,
    counts_ref,
    off_ref,
    chg_ref,
    u_ref,
    ut_ref,
    cl_up,
    cl_down,
    ct_up,
    ct_down,
    in_sem,
    halo,
    tables,
    k_leaf,
    k_parent,
    up_hi,
    up_lo,
    leaf_send,
    leaf_recv,
    par_send,
    par_recv,
    rs_send,
    rs_recv,
    shifted,
    par_ring,
    m_hi,
    m_lo,
    l_three,
    m_three,
    lines,
    near_acc,
    op_hi,
    op_lo,
    near_lhs,
    feat,
    bank_own,
    bank_x,
    bank_y,
    w_own,
    w_x,
    w_y,
    halo_ssem,
    halo_rsem,
    leaf_ssem,
    leaf_rsem,
    par_ssem,
    par_rsem,
    rs_ssem,
    rs_rsem,
):
    a = lax.axis_index("gx")
    b = lax.axis_index("gy")
    lane128 = lax.broadcasted_iota(jnp.int32, (4, 128), 1)

    barrier = pltpu.get_barrier_semaphore()

    def hello(to_a, to_b):
        pl.semaphore_signal(barrier, inc=1, device_id=(to_a, to_b), device_id_type=MESH)

    def hello_row(step, carry):
        hello(wrap(a + step, nx), b)
        return carry

    lax.fori_loop(1, nx, hello_row, 0)
    for sx, sy in SIDES:
        hello(wrap(a + sx, nx), wrap(b + sy, ny))
    task_dy, _ = leaf_task(a)
    leaf_row = jnp.where(task_dy > 0, 1, -1)
    far_b = wrap(b + a - nx // 2, ny)
    leaf_b = wrap(b + leaf_row, ny)

    def hello_far(step, carry):
        to_a = wrap(a + step, nx)

        @pl.when((a < 14) & (task_dy != 0))
        def _():
            hello(to_a, leaf_b)

        @pl.when((to_a != a) | (far_b != b))
        def _():
            hello(to_a, far_b)

        return carry

    lax.fori_loop(0, nx, hello_far, 0)
    fetches = [
        pltpu.make_async_copy(src, dst, in_sem.at[index])
        for index, (src, dst) in enumerate(
            (
                (counts_hbm, counts_ref),
                (off_hbm, off_ref),
                (chg_hbm, chg_ref),
                (u_hbm, u_ref),
                (ut_hbm, ut_ref),
                (cl_up_hbm, cl_up),
                (ct_up_hbm, ct_up),
                (cl_down_hbm, cl_down),
                (ct_down_hbm, ct_down),
            )
        )
    ]
    for fetch in fetches:
        fetch.start()
    for fetch in fetches[:5]:
        fetch.wait()

    for px in range(2):
        for py in range(2):
            cell = halo.at[1 + px, 1 + py]
            for comp in range(3):
                cell[4 * comp : 4 * comp + 4, :] = off_ref[comp, px, py]
            for k in range(4):
                row = chg_ref[px, py, k : k + 1, :]
                cell[12 + k : 13 + k, :] = jnp.where(
                    lane128[0:1] < counts_ref[px, py, k], row, 0.0
                )

    def halo_copy(index):
        sx, sy = SIDES[index]
        src_x = pl.ds(1, 2) if sx == 0 else pl.ds(2 if sx == 1 else 1, 1)
        src_y = pl.ds(1, 2) if sy == 0 else pl.ds(2 if sy == 1 else 1, 1)
        dst_x = pl.ds(1, 2) if sx == 0 else pl.ds(0 if sx == 1 else 3, 1)
        dst_y = pl.ds(1, 2) if sy == 0 else pl.ds(0 if sy == 1 else 3, 1)
        return pltpu.make_async_remote_copy(
            src_ref=halo.at[src_x, src_y],
            dst_ref=halo.at[dst_x, dst_y],
            send_sem=halo_ssem.at[index],
            recv_sem=halo_rsem.at[index],
            device_id=(wrap(a + sx, nx), wrap(b + sy, ny)),
            device_id_type=MESH,
        )

    def child_chunk(chunk, carry):
        rows = pl.ds(pl.multiple_of(32 * chunk, 32), 32)
        base = jnp.full((32, 256), 0.1875 + SOFT / 4, F32)
        half = []
        for comp in range(3):
            diff = 1.8 * u_ref[comp : comp + 1, :] - 0.45 * ut_ref[rows, comp : comp + 1]
            base = base + diff * diff
            half.append(0.5 * diff)
        for child in range(8):
            value = base
            for comp, bit in enumerate((child // 4, child // 2 % 2, child % 2)):
                value = value + half[comp] if bit == 0 else value - half[comp]
            high, low = split(lax.rsqrt(value))
            up_hi[child, rows, :] = high
            up_lo[child, rows, :] = low
        return carry

    lax.fori_loop(0, 8, child_chunk, 0)

    def prepare(matrix, slot):
        high, low = split(jnp.transpose(matrix[...]))
        op_hi[slot] = high
        op_lo[slot] = low

    def apply(rows, slot):
        if rows.shape[0] < 16:
            rows = jnp.concatenate([rows, jnp.zeros((16 - rows.shape[0], 256), F32)], axis=0)
        high, low = split(rows)
        first = bdot(jnp.concatenate([high, low], axis=0), op_hi[slot])
        count = rows.shape[0]
        return first[:count] + (first[count:] + bdot(high, op_lo[slot]))

    centre = [0.5 + 1.8 * u_ref[comp : comp + 1, :] for comp in range(3)]
    checks = []
    for px in range(2):
        for py in range(2):
            turned = jnp.transpose(halo[1 + px, 1 + py])
            for k in range(4):
                box = (px * 2 + py) * 4 + k
                total = jnp.full((128, 256), SOFT, F32)
                for comp in range(3):
                    diff = centre[comp] - turned[:, 4 * comp + k : 4 * comp + k + 1]
                    total = total + diff * diff
                kernel = lax.rsqrt(total)
                k_leaf[box] = kernel
                weight = turned[:, 12 + k : 13 + k]
                checks.append(jnp.sum(kernel * weight, axis=0, keepdims=True))
    leaf_check = jnp.concatenate(checks, axis=0)
    fetches[5].wait()
    fetches[6].wait()
    prepare(cl_up, 0)
    prepare(ct_up, 1)
    leaf_eq = apply(leaf_check, 0)
    for px in range(2):
        for py in range(2):
            first = (px * 2 + py) * 4
            leaf_send[py, 4 * px : 4 * px + 4, :] = leaf_eq[first : first + 4, :]

    eq_hi, eq_lo = split(leaf_eq)
    both = jnp.concatenate([eq_hi, eq_lo], axis=0)
    row16 = lax.broadcasted_iota(jnp.int32, (16, 256), 0)
    rows_sum = jnp.zeros((16, 256), F32)
    for child in range(8):
        first = bdot(both, up_hi[child])
        term = first[:16] + first[16:] + bdot(eq_hi, up_lo[child])
        mine = ((row16 // 4) == (child // 2)) & ((row16 % 2) == (child % 2))
        rows_sum = jnp.where(mine, term, rows_sum)
    upper = (row16 % 4) >= 2
    check0 = 0.5 * jnp.sum(jnp.where(upper, 0.0, rows_sum), axis=0, keepdims=True)
    check1 = 0.5 * jnp.sum(jnp.where(upper, rows_sum, 0.0), axis=0, keepdims=True)
    row8 = lax.broadcasted_iota(jnp.int32, (8, 256), 0)
    parent_check = jnp.where(row8 == 0, check0, jnp.where(row8 == 1, check1, 0.0))
    par_send[...] = apply(parent_check, 1)[0:2]

    def leaf_route(target, py):
        dy, _ = leaf_task(target)
        src = py + dy
        valid = (target < 14) & (src >= -2) & (src <= 3)
        row = (src + 4) // 2 - 2
        return valid, row, (src + 4) % 2

    def leaf_copies():
        for target in range(min(nx, 14)):
            for py in range(2):
                valid, row, src_py = leaf_route(target, py)
                if not valid:
                    continue
                copy = pltpu.make_async_remote_copy(
                    src_ref=leaf_send.at[src_py],
                    dst_ref=leaf_recv.at[a, py],
                    send_sem=leaf_ssem.at[target, py],
                    recv_sem=leaf_rsem.at[a, py],
                    device_id=(target, wrap(b - row, ny)),
                    device_id_type=MESH,
                )
                yield target, py, row, src_py, copy

    def leaf_start():
        for target, py, row, src_py, copy in leaf_copies():
            if row:
                copy.start()
                continue

            @pl.when(target != a)
            def _():
                copy.start()

            @pl.when(target == a)
            def _():
                leaf_recv[a, py] = leaf_send[src_py]

    def leaf_drain():
        for target, py, row, src_py, copy in leaf_copies():
            if row:
                copy.wait_send()
                continue

            @pl.when(target != a)
            def _():
                copy.wait_send()

    def par_copy(target):
        to_b = wrap(b - target + nx // 2, ny)
        copy = pltpu.make_async_remote_copy(
            src_ref=par_send,
            dst_ref=par_recv.at[a],
            send_sem=par_ssem.at[target],
            recv_sem=par_rsem.at[a],
            device_id=(target, to_b),
            device_id_type=MESH,
        )
        return (target == a) & (to_b == b), copy

    def par_start(target, carry):
        self_copy, copy = par_copy(target)

        @pl.when(jnp.logical_not(self_copy))
        def _():
            copy.start()

        @pl.when(self_copy)
        def _():
            par_recv[a] = par_send[...]

        return carry

    pl.semaphore_wait(barrier, (nx - 1) + 8 + 12 + jnp.where(a == nx // 2, nx - 1, nx))
    lax.fori_loop(0, nx, par_start, 0)
    leaf_start()
    for index in range(8):
        halo_copy(index).start()

    for chunk in range(8):
        rows = pl.ds(32 * chunk, 32)
        total = jnp.zeros((32, 256), F32)
        for comp in range(3):
            diff = 0.9 * (u_ref[comp : comp + 1, :] - ut_ref[rows, comp : comp + 1])
            tables[1 + comp, rows, :] = -2.0 * diff
            total = total + diff * diff
            if comp == 0:
                for dx in (-3, -2, -1, 1, 2, 3):
                    lines[dx + 3, rows, :] = (-2.0 * dx) * diff + float(dx * dx)
        tables[0, rows, :] = total

    def source_rows(x, y, z):
        rows = []
        for value in (x, y, z):
            q1, q2, q3 = pieces(value)
            rows += [q1, q2, q1, q2, q3, q1]
        n1, n2, n3 = pieces((x * x + y * y) + (z * z + SOFT))
        one = jnp.ones_like(x)
        return rows + [n1, n2, n3, one, one, one]

    def target_rows(x, y, z):
        rows = []
        for value in (x, y, z):
            p1, p2, p3 = [-2.0 * part for part in pieces(value)]
            rows += [p1, p1, p2, p2, p1, p3]
        one = jnp.ones_like(x)
        n1, n2, n3 = pieces((x * x + y * y) + z * z)
        return rows + [one, one, one, n1, n2, n3]

    box_row = lax.broadcasted_iota(jnp.int32, (16, 128), 0)
    own_x, own_y, own_z, own_w = [
        jnp.concatenate(
            [halo[1 + px, 1 + py, 4 * comp : 4 * comp + 4, :] for px in (0, 1) for py in (0, 1)],
            axis=0,
        )
        for comp in range(4)
    ]
    own_x = own_x + ((box_row // 8) - 1).astype(F32)
    own_y = own_y + ((box_row // 4 % 2) - 1).astype(F32)
    own_z = own_z - 0.5
    feat[pl.ds(384, 128), :] = jnp.zeros((128, 128), F32)
    for index, value in enumerate(source_rows(own_x, own_y, own_z)):
        feat[16 * index : 16 * index + 16, :] = value
    for column in range(4):
        for layer in range(4):
            block = feat[pl.ds(4 * column + layer, 32, stride=16), :]
            bank_own[layer, :, 128 * column : 128 * column + 128] = block.astype(BF16)
            row = own_w[4 * column + layer : 4 * column + layer + 1, :]
            w_own[layer, 0:1, 128 * column : 128 * column + 128] = row
    for turn in range(3):
        for index, value in enumerate(target_rows(own_x, own_y, own_z - float(turn - 1))):
            feat[16 * index : 16 * index + 16, :] = value
        for box in range(16):
            block = feat[pl.ds(box, 32, stride=16), :]
            near_lhs[turn, box] = jnp.transpose(block).astype(BF16)

    lane512 = lax.broadcasted_iota(jnp.int32, (128, 512), 1)
    row512 = lax.broadcasted_iota(jnp.int32, (128, 512), 0)

    def fold(value):
        total = value[:, 0:128]
        for first in range(128, value.shape[1], 128):
            total = total + value[:, first : first + 128]
        return total

    def near_own(turn):
        low = max(0, 1 - turn)

        def step(layer, carry):
            source = layer + turn - 1
            for column in range(4):
                box = 4 * column + layer
                kernel = lax.rsqrt(bdot(near_lhs[turn, box], bank_own[source]))
                if turn == 1:
                    kernel = jnp.where(lane512 == row512 + 128 * column, 0.0, kernel)
                value = fold(kernel * w_own[source, 0:1, :])
                near_acc[box] = value if turn == 1 else near_acc[box] + value
            return carry

        lax.fori_loop(low, low + 4 - abs(turn - 1), step, 0)

    def near_halo(turn):
        low = max(0, 1 - turn)

        def step(layer, carry):
            source = layer + turn - 1
            for column in range(4):
                box = 4 * column + layer
                px = column // 2
                py = column % 2
                lanes = pl.ds(128 * py, 384)
                lhs = near_lhs[turn, box]
                value = lax.rsqrt(bdot(lhs, bank_x[source, px, :, lanes]))
                value = fold(value * w_x[source, px, 0:1, lanes])
                other = lax.rsqrt(bdot(lhs, bank_y[source, py]))
                other = fold(other * w_y[source, py, 0:1, :])
                near_acc[box] = near_acc[box] + (value + other)
            return carry

        lax.fori_loop(low, low + 4 - abs(turn - 1), step, 0)

    for turn in (1, 0, 2):
        near_own(turn)

    fetches[7].wait()
    fetches[8].wait()
    prepare(cl_down, 2)
    prepare(ct_down, 3)

    for px in range(2):
        for py in range(2):
            turned = jnp.transpose(halo[1 + px, 1 + py])
            for k in range(4):
                box = (px * 2 + py) * 4 + k
                total = jnp.full((128, 256), SOFT / 4, F32)
                for comp, bit in enumerate((px, py, k % 2)):
                    place = 0.5 * turned[:, 4 * comp + k : 4 * comp + k + 1] + 0.5 * bit
                    diff = centre[comp] - place
                    total = total + diff * diff
                k_parent[box] = lax.rsqrt(total)

    def par_wait(source, carry):
        self_copy = (source == a) & (far_b == b)
        arrived = pltpu.make_async_remote_copy(
            src_ref=par_send,
            dst_ref=par_recv.at[source],
            send_sem=par_ssem.at[source],
            recv_sem=par_rsem.at[source],
            device_id=(wrap(a + 1, nx), b),
            device_id_type=MESH,
        )

        @pl.when(jnp.logical_not(self_copy))
        def _():
            arrived.wait_recv()

        return carry

    lax.fori_loop(0, nx, par_wait, 0)
    for source in range(nx):
        for layer in range(2):
            par_ring[layer, source : source + 1, :] = par_recv[source, layer : layer + 1, :]

    oy = a - nx // 2
    oy_f = oy.astype(F32)

    for chunk in range(8):
        rows = pl.ds(32 * chunk, 32)
        lines[7, rows, :] = tables[0, rows, :] + (
            oy_f * tables[2, rows, :] + (oy_f * oy_f + SOFT / 4)
        )

    def far_offset(index, first_slot, acc0, acc1):
        ox = index - nx // 2
        ox_f = ox.astype(F32)
        keep = (ox > 1) | (ox < -1) | (oy > 1) | (oy < -1)
        for chunk in range(8):
            rows = pl.ds(32 * chunk, 32)
            flat = lines[7, rows, :] + (ox_f * tables[1, rows, :] + ox_f * ox_f)
            tall = flat + 1.0
            lift = tables[3, rows, :]
            for slot, value in enumerate((tall - lift, flat, tall + lift)):
                high, low = split(lax.rsqrt(value))
                m_hi[first_slot + slot, rows, :] = high
                m_lo[first_slot + slot, rows, :] = low
        turn = wrap(nx + nx // 2 - index, nx)
        p0h, p0l = split(jnp.where(keep, pltpu.roll(par_ring[0], turn, 0), 0.0))
        p1h, p1l = split(jnp.where(keep, pltpu.roll(par_ring[1], turn, 0), 0.0))
        same = bdot(jnp.concatenate([p0h, p1h, p0l, p1l], axis=0), m_hi[first_slot + 1])
        same2 = bdot(jnp.concatenate([p0h, p1h], axis=0), m_lo[first_slot + 1])
        up = bdot(jnp.concatenate([p1h, p1l], axis=0), m_hi[first_slot + 2])
        up2 = bdot(p1h, m_lo[first_slot + 2])
        down = bdot(jnp.concatenate([p0h, p0l], axis=0), m_hi[first_slot])
        down2 = bdot(p0h, m_lo[first_slot])
        acc0 = acc0 + ((same[0:16] + up[0:16]) + (same[32:48] + same2[0:16] + up[16:32] + up2))
        acc1 = acc1 + (
            (same[16:32] + down[0:16]) + (same[48:64] + same2[16:32] + down[16:32] + down2)
        )
        return acc0, acc1

    def far_step(index, carry):
        carry = far_offset(2 * index, 0, *carry)
        return far_offset(2 * index + 1, 3, *carry)

    zero16 = jnp.zeros((16, 256), F32)
    far0, far1 = lax.fori_loop(0, nx // 2, far_step, (zero16, zero16))
    for target in range(nx):
        rs_send[target, 2] = jnp.where(
            row8 == 0,
            0.5 * far0[target : target + 1, :],
            jnp.where(row8 == 1, 0.5 * far1[target : target + 1, :], 0.0),
        )

    dy, half_z = leaf_task(a)

    routes = [leaf_route(a, py) for py in range(2)]

    def leaf_wait(source, carry):
        for py in range(2):
            valid, row, _ = routes[py]
            arrived = pltpu.make_async_remote_copy(
                src_ref=leaf_send.at[0],
                dst_ref=leaf_recv.at[source, py],
                send_sem=leaf_ssem.at[source, py],
                recv_sem=leaf_rsem.at[source, py],
                device_id=(wrap(a + 1, nx), b),
                device_id_type=MESH,
            )

            @pl.when(valid & ((source != a) | (row != 0)))
            def _():
                arrived.wait_recv()

        return carry

    lax.fori_loop(0, nx, leaf_wait, 0)

    @pl.when(dy == 3)
    def _():
        leaf_recv[:, 1] = jnp.zeros((nx, 8, 256), F32)

    @pl.when(dy == -3)
    def _():
        leaf_recv[:, 0] = jnp.zeros((nx, 8, 256), F32)

    for target in range(nx):
        rs_send[target, 0] = jnp.zeros((8, 256), F32)
        rs_send[target, 1] = jnp.zeros((8, 256), F32)

    @pl.when(a < 14)
    def _():
        for source in range(nx):
            low_py = leaf_recv[source, 0]
            high_py = leaf_recv[source, 1]
            first = row8 < 4
            shifted[0, 8 * source : 8 * source + 8, :] = jnp.where(
                first, low_py, pltpu.roll(high_py, 4, 0)
            )
            shifted[1, 8 * source : 8 * source + 8, :] = jnp.where(
                first, pltpu.roll(low_py, 4, 0), high_py
            )
        dy_f = dy.astype(F32)
        row128 = lax.broadcasted_iota(jnp.int32, (128, 256), 0) % 4

        def leaf_step(step, carry):
            dz = jnp.where(half_z == 0, step - 3, step + 1)

            @pl.when(dz <= 3)
            def _():
                dz_f = dz.astype(F32)
                beside = (dy >= -1) & (dy <= 1) & (dz >= -1) & (dz <= 1)
                inside = (row128 + dz >= 0) & (row128 + dz <= 3)
                turn = lax.rem(128 - dz, 128)
                for sx in range(2):
                    moved = jnp.where(inside, pltpu.roll(shifted[sx], turn, 0), 0.0)
                    for block in (-1, 0, 1):
                        if block == -1:
                            placed = jnp.concatenate([moved[120:], moved[:120]], axis=0)
                        elif block == 1:
                            placed = jnp.concatenate([moved[8:], moved[:8]], axis=0)
                        else:
                            placed = moved
                        slot = 2 * block + sx + 2
                        high, low = split(placed)
                        l_three[slot, :, 0:256] = high
                        l_three[slot, :, 256:512] = low
                        l_three[slot, :, 512:768] = high
                const = dy_f * dy_f + dz_f * dz_f + SOFT
                for chunk in range(8):
                    rows = pl.ds(32 * chunk, 32)
                    base = tables[0, rows, :] + dy_f * tables[2, rows, :]
                    lines[7, rows, :] = base + (dz_f * tables[3, rows, :] + const)
                totals = [rs_send[:, px].reshape(8 * nx, 256) for px in range(2)]
                for matrix in range(7):
                    dx = matrix - 3
                    for chunk in range(8):
                        rows = pl.ds(32 * chunk, 32)
                        value = lines[7, rows, :]
                        if dx:
                            value = value + lines[matrix, rows, :]
                        kernel = lax.rsqrt(value)
                        if abs(dx) <= 1:
                            kernel = jnp.where(beside, 0.0, kernel)
                        high, low = split(kernel)
                        m_three[matrix, 32 * chunk : 32 * chunk + 32, :] = high
                        m_three[matrix, 256 + 32 * chunk : 288 + 32 * chunk, :] = high
                        m_three[matrix, 512 + 32 * chunk : 544 + 32 * chunk, :] = low
                    for px in range(2):
                        slot = matrix - 1 + px
                        if 0 <= slot < 6:
                            totals[px] = totals[px] + bdot(l_three[slot], m_three[matrix])
                for px in range(2):
                    rs_send[:, px] = totals[px].reshape(nx, 8, 256)

            return carry

        lax.fori_loop(0, 4, leaf_step, 0)

    def rs_copy(target):
        return pltpu.make_async_remote_copy(
            src_ref=rs_send.at[target],
            dst_ref=rs_recv.at[a],
            send_sem=rs_ssem.at[target],
            recv_sem=rs_rsem.at[a],
            device_id=(target, b),
            device_id_type=MESH,
        )

    def rs_start(step, carry):
        rs_copy(wrap(a + step, nx)).start()
        return carry

    lax.fori_loop(1, nx, rs_start, 0)
    rs_recv[a] = rs_send[a]

    for index in range(8):
        halo_copy(7 - index).wait_recv()
    for strip in range(4):
        if strip < 2:
            cells = [(3 * strip, fy) for fy in range(4)]
        else:
            cells = [(1, 3 * (strip - 2)), (2, 3 * (strip - 2))]
        side_x, side_y, side_z, side_w = [
            jnp.concatenate(
                [halo[fx, fy, 4 * comp : 4 * comp + 4, :] for fx, fy in cells], axis=0
            )
            for comp in range(4)
        ]
        size = 4 * len(cells)
        place = lax.broadcasted_iota(jnp.int32, (size, 128), 0) // 4
        if strip < 2:
            side_x = side_x + float(3 * strip - 2)
            side_y = side_y + (place - 2).astype(F32)
        else:
            side_x = side_x + (place - 1).astype(F32)
            side_y = side_y + float(3 * (strip - 2) - 2)
        for index, value in enumerate(source_rows(side_x, side_y, side_z - 0.5)):
            feat[size * index : size * index + size, :] = value
        feat[pl.ds(24 * size, 8 * size), :] = jnp.zeros((8 * size, 128), F32)
        for cell in range(len(cells)):
            for layer in range(4):
                block = feat[pl.ds(4 * cell + layer, 32, stride=size), :].astype(BF16)
                row = side_w[4 * cell + layer : 4 * cell + layer + 1, :]
                if strip < 2:
                    bank_x[layer, strip, :, 128 * cell : 128 * cell + 128] = block
                    w_x[layer, strip, 0:1, 128 * cell : 128 * cell + 128] = row
                else:
                    bank_y[layer, strip - 2, :, 128 * cell : 128 * cell + 128] = block
                    w_y[layer, strip - 2, 0:1, 128 * cell : 128 * cell + 128] = row
    for turn in (1, 0, 2):
        near_halo(turn)

    for index in range(8):
        halo_copy(index).wait_send()
    leaf_drain()

    def drain(target, carry):
        own, copy = par_copy(target)

        @pl.when(jnp.logical_not(own))
        def _():
            copy.wait_send()

        @pl.when(target != a)
        def _():
            rs_copy(target).wait_send()

        return carry

    lax.fori_loop(0, nx, drain, 0)

    def rs_wait(step, carry):
        source = wrap(a + step, nx)
        pltpu.make_async_remote_copy(
            src_ref=rs_send.at[source],
            dst_ref=rs_recv.at[source],
            send_sem=rs_ssem.at[source],
            recv_sem=rs_rsem.at[source],
            device_id=(source, b),
            device_id_type=MESH,
        ).wait_recv()
        return carry

    lax.fori_loop(1, nx, rs_wait, 0)
    sums = [jnp.zeros((8, 256), F32) for _ in range(3)]
    for source in range(nx):
        for part in range(3):
            sums[part] = sums[part] + rs_recv[source, part]

    leaf_local = apply(jnp.concatenate([sums[0], sums[1]], axis=0), 2)
    parent_local = 0.5 * apply(sums[2], 3)
    lanes = lax.broadcasted_iota(jnp.int32, (128, 128), 1)
    columns = jnp.zeros((128, 128), F32)
    for box in range(16):
        layer = (box % 4) // 2
        value = k_leaf[box] * leaf_local[box : box + 1, :]
        value = value + k_parent[box] * parent_local[layer : layer + 1, :]
        value = value[:, :128] + value[:, 128:] + near_acc[box]
        column = jnp.sum(value, axis=1, keepdims=True)
        columns = jnp.where(lanes == box, column, columns)
    flipped = jnp.transpose(columns)
    for px in range(2):
        for py in range(2):
            for k in range(4):
                box = (px * 2 + py) * 4 + k
                row = flipped[box : box + 1, :]
                out_ref[px, py, k : k + 1, :] = jnp.where(
                    lane128[0:1] < counts_ref[px, py, k], row, 0.0
                )


def shards(offsets, charges, counts, cl_up, cl_down, ct_up, ct_down):
    nx = lax.axis_size("gx")
    ny = lax.axis_size("gy")
    points = sphere_points(256)
    unit = np.zeros((8, 256), np.float32)
    unit[:3] = points
    unit_t = np.zeros((256, 8), np.float32)
    unit_t[:, :3] = points.T
    vmem = pl.BlockSpec(memory_space=pltpu.VMEM)
    dma = pltpu.SemaphoreType.DMA
    return pl.pallas_call(
        functools.partial(body, nx, ny),
        out_shape=jax.ShapeDtypeStruct(charges.shape, F32),
        in_specs=[pl.BlockSpec(memory_space=pl.ANY)] * 9,
        out_specs=vmem,
        scratch_shapes=[
            pltpu.SMEM(counts.shape, jnp.int32),
            pltpu.VMEM(offsets.shape, F32),
            pltpu.VMEM(charges.shape, F32),
            pltpu.VMEM(unit.shape, F32),
            pltpu.VMEM(unit_t.shape, F32),
            pltpu.VMEM((256, 256), F32),
            pltpu.VMEM((256, 256), F32),
            pltpu.VMEM((256, 256), F32),
            pltpu.VMEM((256, 256), F32),
            dma((9,)),
            pltpu.VMEM((4, 4, 16, 128), F32),
            pltpu.VMEM((4, 256, 256), F32),
            pltpu.VMEM((16, 128, 256), F32),
            pltpu.VMEM((16, 128, 256), F32),
            pltpu.VMEM((8, 256, 256), BF16),
            pltpu.VMEM((8, 256, 256), BF16),
            pltpu.VMEM((2, 8, 256), F32),
            pltpu.VMEM((nx, 2, 8, 256), F32),
            pltpu.VMEM((2, 256), F32),
            pltpu.VMEM((nx, 2, 256), F32),
            pltpu.VMEM((nx, 3, 8, 256), F32),
            pltpu.VMEM((nx, 3, 8, 256), F32),
            pltpu.VMEM((2, 8 * nx, 256), F32),
            pltpu.VMEM((2, nx, 256), F32),
            pltpu.VMEM((6, 256, 256), BF16),
            pltpu.VMEM((6, 256, 256), BF16),
            pltpu.VMEM((6, 8 * nx, 768), BF16),
            pltpu.VMEM((7, 768, 256), BF16),
            pltpu.VMEM((8, 256, 256), F32),
            pltpu.VMEM((16, 128, 128), F32),
            pltpu.VMEM((4, 256, 256), BF16),
            pltpu.VMEM((4, 256, 256), BF16),
            pltpu.VMEM((3, 16, 128, 32), BF16),
            pltpu.VMEM((512, 128), F32),
            pltpu.VMEM((4, 32, 512), BF16),
            pltpu.VMEM((4, 2, 32, 512), BF16),
            pltpu.VMEM((4, 2, 32, 256), BF16),
            pltpu.VMEM((4, 8, 512), F32),
            pltpu.VMEM((4, 2, 8, 512), F32),
            pltpu.VMEM((4, 2, 8, 256), F32),
            dma((8,)),
            dma((8,)),
            dma((nx, 2)),
            dma((nx, 2)),
            dma((nx,)),
            dma((nx,)),
            dma((nx,)),
            dma((nx,)),
        ],
        compiler_params=pltpu.CompilerParams(
            has_side_effects=True, collective_id=0, vmem_limit_bytes=56 * 1024 * 1024
        ),
        name="multipole",
    )(counts, offsets, charges, jnp.asarray(unit), jnp.asarray(unit_t), cl_up, cl_down, ct_up, ct_down)


def solution(mesh):
    return jax.shard_map(
        shards,
        mesh=mesh,
        in_specs=(
            P(None, "gx", "gy", None, None),
            P("gx", "gy", None, None),
            P("gx", "gy", None),
            P(),
            P(),
            P(),
            P(),
        ),
        out_specs=P("gx", "gy", None, None),
        check_vma=False,
    )
```

```python
import functools

import jax
import jax.numpy as jnp
import numpy as np
from jax import lax
from jax.experimental import pallas as pl
from jax.experimental.pallas import tpu as pltpu
from jax.sharding import PartitionSpec as P

SOFT = 0.0004
F32 = jnp.float32
BF16 = jnp.bfloat16
MESH = pl.DeviceIdType.MESH
SIDES = [(sx, sy) for sx in (-1, 0, 1) for sy in (-1, 0, 1) if (sx, sy) != (0, 0)]


def sphere_points(count):
    middle = np.arange(count).astype(np.float32) + np.float32(0.5)
    height = (np.float32(1.0) - np.float32(2.0) * middle / np.float32(count)).astype(np.float32)
    radial = np.sqrt(np.maximum(np.float32(1.0) - height * height, np.float32(0.0)))
    turn = (middle * np.float32(2.399963229728653)).astype(np.float32)
    cos = np.cos(turn.astype(np.float64)).astype(np.float32)
    sin = np.sin(turn.astype(np.float64)).astype(np.float32)
    return np.stack([radial * cos, radial * sin, height]).astype(np.float32)


def split(value):
    high = value.astype(BF16)
    low = (value - high.astype(F32)).astype(BF16)
    return high, low


def pieces(value):
    first = value.astype(BF16).astype(F32)
    rest = value - first
    second = rest.astype(BF16).astype(F32)
    return first, second, rest - second


def bdot(a, b):
    return jnp.dot(a, b, preferred_element_type=F32)


def wrap(value, size):
    if size & (size - 1) == 0:
        return value & (size - 1)
    return lax.rem(value + size, size)


def leaf_task(a):
    return a // 2 - 3, a % 2


def body(
    nx,
    ny,
    counts_hbm,
    off_hbm,
    chg_hbm,
    u_hbm,
    ut_hbm,
    cl_up_hbm,
    cl_down_hbm,
    ct_up_hbm,
    ct_down_hbm,
    out_ref,
    counts_ref,
    off_ref,
    chg_ref,
    u_ref,
    ut_ref,
    cl_up,
    cl_down,
    ct_up,
    ct_down,
    in_sem,
    halo,
    tables,
    k_leaf,
    k_parent,
    up_hi,
    up_lo,
    leaf_send,
    leaf_recv,
    par_send,
    par_recv,
    rs_send,
    rs_recv,
    shifted,
    par_ring,
    m_hi,
    m_lo,
    l_three,
    m_three,
    lines,
    near_acc,
    op_hi,
    op_lo,
    near_lhs,
    feat,
    bank_own,
    bank_x,
    bank_y,
    w_own,
    w_x,
    w_y,
    halo_ssem,
    halo_rsem,
    leaf_ssem,
    leaf_rsem,
    par_ssem,
    par_rsem,
    rs_ssem,
    rs_rsem,
):
    a = lax.axis_index("gx")
    b = lax.axis_index("gy")
    lane128 = lax.broadcasted_iota(jnp.int32, (4, 128), 1)

    fetches = [
        pltpu.make_async_copy(src, dst, in_sem.at[index])
        for index, (src, dst) in enumerate(
            (
                (counts_hbm, counts_ref),
                (off_hbm, off_ref),
                (chg_hbm, chg_ref),
                (u_hbm, u_ref),
                (ut_hbm, ut_ref),
                (cl_up_hbm, cl_up),
                (ct_up_hbm, ct_up),
                (cl_down_hbm, cl_down),
                (ct_down_hbm, ct_down),
            )
        )
    ]
    for fetch in fetches:
        fetch.start()

    barrier = pltpu.get_barrier_semaphore()

    def hello(to_a, to_b):
        pl.semaphore_signal(barrier, inc=1, device_id=(to_a, to_b), device_id_type=MESH)

    for sx, sy in SIDES:
        hello(wrap(a + sx, nx), wrap(b + sy, ny))
    for step in range(1, nx):
        hello(wrap(a + step, nx), b)
    task_dy, _ = leaf_task(a)
    leaf_row = jnp.where(task_dy > 0, 1, -1)
    far_b = wrap(b + a - nx // 2, ny)
    leaf_b = wrap(b + leaf_row, ny)

    @pl.when((a < 14) & (task_dy != 0))
    def _():
        for to_a in range(nx):
            hello(to_a, leaf_b)

    for to_a in range(nx):
        if to_a != nx // 2:
            hello(to_a, far_b)

    @pl.when(a != nx // 2)
    def _():
        hello(nx // 2, far_b)

    for fetch in fetches[:5]:
        fetch.wait()

    for px in range(2):
        for py in range(2):
            cell = halo.at[1 + px, 1 + py]
            for comp in range(3):
                cell[4 * comp : 4 * comp + 4, :] = off_ref[comp, px, py]
            for k in range(4):
                row = chg_ref[px, py, k : k + 1, :]
                cell[12 + k : 13 + k, :] = jnp.where(
                    lane128[0:1] < counts_ref[px, py, k], row, 0.0
                )

    def halo_copy(index):
        sx, sy = SIDES[index]
        src_x = pl.ds(1, 2) if sx == 0 else pl.ds(2 if sx == 1 else 1, 1)
        src_y = pl.ds(1, 2) if sy == 0 else pl.ds(2 if sy == 1 else 1, 1)
        dst_x = pl.ds(1, 2) if sx == 0 else pl.ds(0 if sx == 1 else 3, 1)
        dst_y = pl.ds(1, 2) if sy == 0 else pl.ds(0 if sy == 1 else 3, 1)
        return pltpu.make_async_remote_copy(
            src_ref=halo.at[src_x, src_y],
            dst_ref=halo.at[dst_x, dst_y],
            send_sem=halo_ssem.at[index],
            recv_sem=halo_rsem.at[index],
            device_id=(wrap(a + sx, nx), wrap(b + sy, ny)),
            device_id_type=MESH,
        )

    def child_chunk(chunk, carry):
        rows = pl.ds(pl.multiple_of(32 * chunk, 32), 32)
        base = jnp.full((32, 256), 0.1875 + SOFT / 4, F32)
        half = []
        for comp in range(3):
            diff = 1.8 * u_ref[comp : comp + 1, :] - 0.45 * ut_ref[rows, comp : comp + 1]
            base = base + diff * diff
            half.append(0.5 * diff)
        for child in range(8):
            value = base
            for comp, bit in enumerate((child // 4, child // 2 % 2, child % 2)):
                value = value + half[comp] if bit == 0 else value - half[comp]
            high, low = split(lax.rsqrt(value))
            up_hi[child, rows, :] = high
            up_lo[child, rows, :] = low
        return carry

    lax.fori_loop(0, 8, child_chunk, 0)

    def prepare(matrix, slot):
        high, low = split(jnp.transpose(matrix[...]))
        op_hi[slot] = high
        op_lo[slot] = low

    def apply(rows, slot):
        if rows.shape[0] < 16:
            rows = jnp.concatenate([rows, jnp.zeros((16 - rows.shape[0], 256), F32)], axis=0)
        high, low = split(rows)
        first = bdot(jnp.concatenate([high, low], axis=0), op_hi[slot])
        count = rows.shape[0]
        return first[:count] + (first[count:] + bdot(high, op_lo[slot]))

    centre = [0.5 + 1.8 * u_ref[comp : comp + 1, :] for comp in range(3)]
    checks = []
    for px in range(2):
        for py in range(2):
            turned = jnp.transpose(halo[1 + px, 1 + py])
            for k in range(4):
                box = (px * 2 + py) * 4 + k
                total = jnp.full((128, 256), SOFT, F32)
                for comp in range(3):
                    diff = centre[comp] - turned[:, 4 * comp + k : 4 * comp + k + 1]
                    total = total + diff * diff
                kernel = lax.rsqrt(total)
                k_leaf[box] = kernel
                weight = turned[:, 12 + k : 13 + k]
                checks.append(jnp.sum(kernel * weight, axis=0, keepdims=True))
    leaf_check = jnp.concatenate(checks, axis=0)
    fetches[5].wait()
    fetches[6].wait()
    prepare(cl_up, 0)
    prepare(ct_up, 1)
    leaf_eq = apply(leaf_check, 0)
    for px in range(2):
        for py in range(2):
            first = (px * 2 + py) * 4
            leaf_send[py, 4 * px : 4 * px + 4, :] = leaf_eq[first : first + 4, :]

    eq_hi, eq_lo = split(leaf_eq)
    both = jnp.concatenate([eq_hi, eq_lo], axis=0)
    row16 = lax.broadcasted_iota(jnp.int32, (16, 256), 0)
    rows_sum = jnp.zeros((16, 256), F32)
    for child in range(8):
        first = bdot(both, up_hi[child])
        term = first[:16] + first[16:] + bdot(eq_hi, up_lo[child])
        mine = ((row16 // 4) == (child // 2)) & ((row16 % 2) == (child % 2))
        rows_sum = jnp.where(mine, term, rows_sum)
    upper = (row16 % 4) >= 2
    check0 = 0.5 * jnp.sum(jnp.where(upper, 0.0, rows_sum), axis=0, keepdims=True)
    check1 = 0.5 * jnp.sum(jnp.where(upper, rows_sum, 0.0), axis=0, keepdims=True)
    row8 = lax.broadcasted_iota(jnp.int32, (8, 256), 0)
    parent_check = jnp.where(row8 == 0, check0, jnp.where(row8 == 1, check1, 0.0))
    par_send[...] = apply(parent_check, 1)[0:2]

    def leaf_route(target, py):
        dy, _ = leaf_task(target)
        src = py + dy
        valid = (target < 14) & (src >= -2) & (src <= 3)
        row = (src + 4) // 2 - 2
        return valid, row, (src + 4) % 2

    def leaf_copies():
        for target in range(min(nx, 14)):
            for py in range(2):
                valid, row, src_py = leaf_route(target, py)
                if not valid:
                    continue
                copy = pltpu.make_async_remote_copy(
                    src_ref=leaf_send.at[src_py],
                    dst_ref=leaf_recv.at[a, py],
                    send_sem=leaf_ssem.at[target, py],
                    recv_sem=leaf_rsem.at[a, py],
                    device_id=(target, wrap(b - row, ny)),
                    device_id_type=MESH,
                )
                yield target, py, row, src_py, copy

    def leaf_start():
        for target, py, row, src_py, copy in leaf_copies():
            if row:
                copy.start()
                continue

            @pl.when(target != a)
            def _():
                copy.start()

            @pl.when(target == a)
            def _():
                leaf_recv[a, py] = leaf_send[src_py]

    def leaf_drain():
        for target, py, row, src_py, copy in leaf_copies():
            if row:
                copy.wait_send()
                continue

            @pl.when(target != a)
            def _():
                copy.wait_send()

    def par_copy(target):
        to_b = wrap(b - target + nx // 2, ny)
        copy = pltpu.make_async_remote_copy(
            src_ref=par_send,
            dst_ref=par_recv.at[a],
            send_sem=par_ssem.at[target],
            recv_sem=par_rsem.at[a],
            device_id=(target, to_b),
            device_id_type=MESH,
        )
        return copy

    def par_start():
        for target in range(nx):
            if target != nx // 2:
                par_copy(target).start()

        @pl.when(a != nx // 2)
        def _():
            par_copy(nx // 2).start()

        @pl.when(a == nx // 2)
        def _():
            par_recv[a] = par_send[...]

    pl.semaphore_wait(barrier, (nx - 1) + 8 + 12 + jnp.where(a == nx // 2, nx - 1, nx))
    par_start()
    leaf_start()
    for index in range(8):
        halo_copy(index).start()

    for chunk in range(8):
        rows = pl.ds(32 * chunk, 32)
        total = jnp.zeros((32, 256), F32)
        for comp in range(3):
            diff = 0.9 * (u_ref[comp : comp + 1, :] - ut_ref[rows, comp : comp + 1])
            tables[1 + comp, rows, :] = -2.0 * diff
            total = total + diff * diff
            if comp == 0:
                for dx in (-3, -2, -1, 1, 2, 3):
                    lines[dx + 3, rows, :] = (-2.0 * dx) * diff + float(dx * dx)
        tables[0, rows, :] = total

    def source_rows(x, y, z):
        rows = []
        for value in (x, y, z):
            q1, q2, q3 = pieces(value)
            rows += [q1, q2, q1, q2, q3, q1]
        n1, n2, n3 = pieces((x * x + y * y) + (z * z + SOFT))
        one = jnp.ones_like(x)
        return rows + [n1, n2, n3, one, one, one]

    def target_rows(x, y, z):
        rows = []
        for value in (x, y, z):
            p1, p2, p3 = [-2.0 * part for part in pieces(value)]
            rows += [p1, p1, p2, p2, p1, p3]
        one = jnp.ones_like(x)
        n1, n2, n3 = pieces((x * x + y * y) + z * z)
        return rows + [one, one, one, n1, n2, n3]

    box_row = lax.broadcasted_iota(jnp.int32, (16, 128), 0)
    own_x, own_y, own_z, own_w = [
        jnp.concatenate(
            [halo[1 + px, 1 + py, 4 * comp : 4 * comp + 4, :] for px in (0, 1) for py in (0, 1)],
            axis=0,
        )
        for comp in range(4)
    ]
    own_x = own_x + ((box_row // 8) - 1).astype(F32)
    own_y = own_y + ((box_row // 4 % 2) - 1).astype(F32)
    own_z = own_z - 0.5
    feat[pl.ds(384, 128), :] = jnp.zeros((128, 128), F32)
    for index, value in enumerate(source_rows(own_x, own_y, own_z)):
        feat[16 * index : 16 * index + 16, :] = value
    for column in range(4):
        for layer in range(4):
            block = feat[pl.ds(4 * column + layer, 32, stride=16), :]
            bank_own[layer, :, 128 * column : 128 * column + 128] = block.astype(BF16)
            row = own_w[4 * column + layer : 4 * column + layer + 1, :]
            w_own[layer, 0:1, 128 * column : 128 * column + 128] = row
    for turn in range(3):
        for index, value in enumerate(target_rows(own_x, own_y, own_z - float(turn - 1))):
            feat[16 * index : 16 * index + 16, :] = value
        for box in range(16):
            block = feat[pl.ds(box, 32, stride=16), :]
            near_lhs[turn, box] = jnp.transpose(block).astype(BF16)

    lane512 = lax.broadcasted_iota(jnp.int32, (128, 512), 1)
    row512 = lax.broadcasted_iota(jnp.int32, (128, 512), 0)

    def fold(value):
        total = value[:, 0:128]
        for first in range(128, value.shape[1], 128):
            total = total + value[:, first : first + 128]
        return total

    def near_own(turn):
        low = max(0, 1 - turn)

        def step(layer, carry):
            source = layer + turn - 1
            for column in range(4):
                box = 4 * column + layer
                kernel = lax.rsqrt(bdot(near_lhs[turn, box], bank_own[source]))
                if turn == 1:
                    kernel = jnp.where(lane512 == row512 + 128 * column, 0.0, kernel)
                value = fold(kernel * w_own[source, 0:1, :])
                near_acc[box] = value if turn == 1 else near_acc[box] + value
            return carry

        lax.fori_loop(low, low + 4 - abs(turn - 1), step, 0)

    def near_halo(turn):
        low = max(0, 1 - turn)

        def step(layer, carry):
            source = layer + turn - 1
            for column in range(4):
                box = 4 * column + layer
                px = column // 2
                py = column % 2
                lanes = pl.ds(128 * py, 384)
                lhs = near_lhs[turn, box]
                value = lax.rsqrt(bdot(lhs, bank_x[source, px, :, lanes]))
                value = fold(value * w_x[source, px, 0:1, lanes])
                other = lax.rsqrt(bdot(lhs, bank_y[source, py]))
                other = fold(other * w_y[source, py, 0:1, :])
                near_acc[box] = near_acc[box] + (value + other)
            return carry

        lax.fori_loop(low, low + 4 - abs(turn - 1), step, 0)

    for turn in (1, 0, 2):
        near_own(turn)

    fetches[7].wait()
    fetches[8].wait()
    prepare(cl_down, 2)
    prepare(ct_down, 3)

    for px in range(2):
        for py in range(2):
            turned = jnp.transpose(halo[1 + px, 1 + py])
            for k in range(4):
                box = (px * 2 + py) * 4 + k
                total = jnp.full((128, 256), SOFT / 4, F32)
                for comp, bit in enumerate((px, py, k % 2)):
                    place = 0.5 * turned[:, 4 * comp + k : 4 * comp + k + 1] + 0.5 * bit
                    diff = centre[comp] - place
                    total = total + diff * diff
                k_parent[box] = lax.rsqrt(total)

    def par_wait(source, carry):
        self_copy = (source == a) & (far_b == b)
        arrived = pltpu.make_async_remote_copy(
            src_ref=par_send,
            dst_ref=par_recv.at[source],
            send_sem=par_ssem.at[source],
            recv_sem=par_rsem.at[source],
            device_id=(wrap(a + 1, nx), b),
            device_id_type=MESH,
        )

        @pl.when(jnp.logical_not(self_copy))
        def _():
            arrived.wait_recv()

        return carry

    lax.fori_loop(0, nx, par_wait, 0)
    for source in range(nx):
        for layer in range(2):
            par_ring[layer, source : source + 1, :] = par_recv[source, layer : layer + 1, :]

    oy = a - nx // 2
    oy_f = oy.astype(F32)

    for chunk in range(8):
        rows = pl.ds(32 * chunk, 32)
        lines[7, rows, :] = tables[0, rows, :] + (
            oy_f * tables[2, rows, :] + (oy_f * oy_f + SOFT / 4)
        )

    def far_offset(index, first_slot, acc0, acc1):
        ox = index - nx // 2
        ox_f = ox.astype(F32)
        keep = (ox > 1) | (ox < -1) | (oy > 1) | (oy < -1)
        for chunk in range(8):
            rows = pl.ds(32 * chunk, 32)
            flat = lines[7, rows, :] + (ox_f * tables[1, rows, :] + ox_f * ox_f)
            tall = flat + 1.0
            lift = tables[3, rows, :]
            for slot, value in enumerate((tall - lift, flat, tall + lift)):
                high, low = split(lax.rsqrt(value))
                m_hi[first_slot + slot, rows, :] = high
                m_lo[first_slot + slot, rows, :] = low
        turn = wrap(nx + nx // 2 - index, nx)
        p0h, p0l = split(jnp.where(keep, pltpu.roll(par_ring[0], turn, 0), 0.0))
        p1h, p1l = split(jnp.where(keep, pltpu.roll(par_ring[1], turn, 0), 0.0))
        same = bdot(jnp.concatenate([p0h, p1h, p0l, p1l], axis=0), m_hi[first_slot + 1])
        same2 = bdot(jnp.concatenate([p0h, p1h], axis=0), m_lo[first_slot + 1])
        up = bdot(jnp.concatenate([p1h, p1l], axis=0), m_hi[first_slot + 2])
        up2 = bdot(p1h, m_lo[first_slot + 2])
        down = bdot(jnp.concatenate([p0h, p0l], axis=0), m_hi[first_slot])
        down2 = bdot(p0h, m_lo[first_slot])
        acc0 = acc0 + ((same[0:16] + up[0:16]) + (same[32:48] + same2[0:16] + up[16:32] + up2))
        acc1 = acc1 + (
            (same[16:32] + down[0:16]) + (same[48:64] + same2[16:32] + down[16:32] + down2)
        )
        return acc0, acc1

    def far_step(index, carry):
        carry = far_offset(2 * index, 0, *carry)
        return far_offset(2 * index + 1, 3, *carry)

    zero16 = jnp.zeros((16, 256), F32)
    far0, far1 = lax.fori_loop(0, nx // 2, far_step, (zero16, zero16))
    for target in range(nx):
        rs_send[target, 2] = jnp.where(
            row8 == 0,
            0.5 * far0[target : target + 1, :],
            jnp.where(row8 == 1, 0.5 * far1[target : target + 1, :], 0.0),
        )

    dy, half_z = leaf_task(a)

    routes = [leaf_route(a, py) for py in range(2)]

    def leaf_wait(source, carry):
        for py in range(2):
            valid, row, _ = routes[py]
            arrived = pltpu.make_async_remote_copy(
                src_ref=leaf_send.at[0],
                dst_ref=leaf_recv.at[source, py],
                send_sem=leaf_ssem.at[source, py],
                recv_sem=leaf_rsem.at[source, py],
                device_id=(wrap(a + 1, nx), b),
                device_id_type=MESH,
            )

            @pl.when(valid & ((source != a) | (row != 0)))
            def _():
                arrived.wait_recv()

        return carry

    lax.fori_loop(0, nx, leaf_wait, 0)

    @pl.when(dy == 3)
    def _():
        leaf_recv[:, 1] = jnp.zeros((nx, 8, 256), F32)

    @pl.when(dy == -3)
    def _():
        leaf_recv[:, 0] = jnp.zeros((nx, 8, 256), F32)

    for target in range(nx):
        rs_send[target, 0] = jnp.zeros((8, 256), F32)
        rs_send[target, 1] = jnp.zeros((8, 256), F32)

    @pl.when(a < 14)
    def _():
        for source in range(nx):
            low_py = leaf_recv[source, 0]
            high_py = leaf_recv[source, 1]
            first = row8 < 4
            shifted[0, 8 * source : 8 * source + 8, :] = jnp.where(
                first, low_py, pltpu.roll(high_py, 4, 0)
            )
            shifted[1, 8 * source : 8 * source + 8, :] = jnp.where(
                first, pltpu.roll(low_py, 4, 0), high_py
            )
        dy_f = dy.astype(F32)
        row128 = lax.broadcasted_iota(jnp.int32, (128, 256), 0) % 4

        def leaf_step(step, carry):
            dz = jnp.where(half_z == 0, step - 3, step + 1)

            @pl.when(dz <= 3)
            def _():
                dz_f = dz.astype(F32)
                beside = (dy >= -1) & (dy <= 1) & (dz >= -1) & (dz <= 1)
                inside = (row128 + dz >= 0) & (row128 + dz <= 3)
                turn = lax.rem(128 - dz, 128)
                for sx in range(2):
                    moved = jnp.where(inside, pltpu.roll(shifted[sx], turn, 0), 0.0)
                    for block in (-1, 0, 1):
                        if block == -1:
                            placed = jnp.concatenate([moved[120:], moved[:120]], axis=0)
                        elif block == 1:
                            placed = jnp.concatenate([moved[8:], moved[:8]], axis=0)
                        else:
                            placed = moved
                        slot = 2 * block + sx + 2
                        high, low = split(placed)
                        l_three[slot, :, 0:256] = high
                        l_three[slot, :, 256:512] = low
                        l_three[slot, :, 512:768] = high
                const = dy_f * dy_f + dz_f * dz_f + SOFT
                for chunk in range(8):
                    rows = pl.ds(32 * chunk, 32)
                    base = tables[0, rows, :] + dy_f * tables[2, rows, :]
                    lines[7, rows, :] = base + (dz_f * tables[3, rows, :] + const)
                totals = [rs_send[:, px].reshape(8 * nx, 256) for px in range(2)]
                for matrix in range(7):
                    dx = matrix - 3
                    for chunk in range(8):
                        rows = pl.ds(32 * chunk, 32)
                        value = lines[7, rows, :]
                        if dx:
                            value = value + lines[matrix, rows, :]
                        kernel = lax.rsqrt(value)
                        if abs(dx) <= 1:
                            kernel = jnp.where(beside, 0.0, kernel)
                        high, low = split(kernel)
                        m_three[matrix, 32 * chunk : 32 * chunk + 32, :] = high
                        m_three[matrix, 256 + 32 * chunk : 288 + 32 * chunk, :] = high
                        m_three[matrix, 512 + 32 * chunk : 544 + 32 * chunk, :] = low
                    for px in range(2):
                        slot = matrix - 1 + px
                        if 0 <= slot < 6:
                            totals[px] = totals[px] + bdot(l_three[slot], m_three[matrix])
                for px in range(2):
                    rs_send[:, px] = totals[px].reshape(nx, 8, 256)

            return carry

        lax.fori_loop(0, 4, leaf_step, 0)

    def rs_copy(target):
        return pltpu.make_async_remote_copy(
            src_ref=rs_send.at[target],
            dst_ref=rs_recv.at[a],
            send_sem=rs_ssem.at[target],
            recv_sem=rs_rsem.at[a],
            device_id=(target, b),
            device_id_type=MESH,
        )

    for step in range(1, nx):
        rs_copy(wrap(a + step, nx)).start()
    rs_recv[a] = rs_send[a]

    for index in range(8):
        halo_copy(7 - index).wait_recv()
    for strip in range(4):
        if strip < 2:
            cells = [(3 * strip, fy) for fy in range(4)]
        else:
            cells = [(1, 3 * (strip - 2)), (2, 3 * (strip - 2))]
        side_x, side_y, side_z, side_w = [
            jnp.concatenate(
                [halo[fx, fy, 4 * comp : 4 * comp + 4, :] for fx, fy in cells], axis=0
            )
            for comp in range(4)
        ]
        size = 4 * len(cells)
        place = lax.broadcasted_iota(jnp.int32, (size, 128), 0) // 4
        if strip < 2:
            side_x = side_x + float(3 * strip - 2)
            side_y = side_y + (place - 2).astype(F32)
        else:
            side_x = side_x + (place - 1).astype(F32)
            side_y = side_y + float(3 * (strip - 2) - 2)
        for index, value in enumerate(source_rows(side_x, side_y, side_z - 0.5)):
            feat[size * index : size * index + size, :] = value
        feat[pl.ds(24 * size, 8 * size), :] = jnp.zeros((8 * size, 128), F32)
        for cell in range(len(cells)):
            for layer in range(4):
                block = feat[pl.ds(4 * cell + layer, 32, stride=size), :].astype(BF16)
                row = side_w[4 * cell + layer : 4 * cell + layer + 1, :]
                if strip < 2:
                    bank_x[layer, strip, :, 128 * cell : 128 * cell + 128] = block
                    w_x[layer, strip, 0:1, 128 * cell : 128 * cell + 128] = row
                else:
                    bank_y[layer, strip - 2, :, 128 * cell : 128 * cell + 128] = block
                    w_y[layer, strip - 2, 0:1, 128 * cell : 128 * cell + 128] = row
    for turn in (1, 0, 2):
        near_halo(turn)

    for index in range(8):
        halo_copy(index).wait_send()
    leaf_drain()

    def drain(target, carry):
        @pl.when((target != nx // 2) | (a != nx // 2))
        def _():
            par_copy(target).wait_send()

        @pl.when(target != a)
        def _():
            rs_copy(target).wait_send()

        return carry

    lax.fori_loop(0, nx, drain, 0)

    def rs_wait(step, carry):
        source = wrap(a + step, nx)
        pltpu.make_async_remote_copy(
            src_ref=rs_send.at[source],
            dst_ref=rs_recv.at[source],
            send_sem=rs_ssem.at[source],
            recv_sem=rs_rsem.at[source],
            device_id=(source, b),
            device_id_type=MESH,
        ).wait_recv()
        return carry

    lax.fori_loop(1, nx, rs_wait, 0)
    sums = [jnp.zeros((8, 256), F32) for _ in range(3)]
    for source in range(nx):
        for part in range(3):
            sums[part] = sums[part] + rs_recv[source, part]

    leaf_local = apply(jnp.concatenate([sums[0], sums[1]], axis=0), 2)
    parent_local = 0.5 * apply(sums[2], 3)
    lanes = lax.broadcasted_iota(jnp.int32, (128, 128), 1)
    columns = jnp.zeros((128, 128), F32)
    for box in range(16):
        layer = (box % 4) // 2
        value = k_leaf[box] * leaf_local[box : box + 1, :]
        value = value + k_parent[box] * parent_local[layer : layer + 1, :]
        value = value[:, :128] + value[:, 128:] + near_acc[box]
        column = jnp.sum(value, axis=1, keepdims=True)
        columns = jnp.where(lanes == box, column, columns)
    flipped = jnp.transpose(columns)
    for px in range(2):
        for py in range(2):
            for k in range(4):
                box = (px * 2 + py) * 4 + k
                row = flipped[box : box + 1, :]
                out_ref[px, py, k : k + 1, :] = jnp.where(
                    lane128[0:1] < counts_ref[px, py, k], row, 0.0
                )


def shards(offsets, charges, counts, cl_up, cl_down, ct_up, ct_down):
    nx = lax.axis_size("gx")
    ny = lax.axis_size("gy")
    points = sphere_points(256)
    unit = np.zeros((8, 256), np.float32)
    unit[:3] = points
    unit_t = np.zeros((256, 8), np.float32)
    unit_t[:, :3] = points.T
    vmem = pl.BlockSpec(memory_space=pltpu.VMEM)
    dma = pltpu.SemaphoreType.DMA
    return pl.pallas_call(
        functools.partial(body, nx, ny),
        out_shape=jax.ShapeDtypeStruct(charges.shape, F32),
        in_specs=[pl.BlockSpec(memory_space=pl.ANY)] * 9,
        out_specs=vmem,
        scratch_shapes=[
            pltpu.SMEM(counts.shape, jnp.int32),
            pltpu.VMEM(offsets.shape, F32),
            pltpu.VMEM(charges.shape, F32),
            pltpu.VMEM(unit.shape, F32),
            pltpu.VMEM(unit_t.shape, F32),
            pltpu.VMEM((256, 256), F32),
            pltpu.VMEM((256, 256), F32),
            pltpu.VMEM((256, 256), F32),
            pltpu.VMEM((256, 256), F32),
            dma((9,)),
            pltpu.VMEM((4, 4, 16, 128), F32),
            pltpu.VMEM((4, 256, 256), F32),
            pltpu.VMEM((16, 128, 256), F32),
            pltpu.VMEM((16, 128, 256), F32),
            pltpu.VMEM((8, 256, 256), BF16),
            pltpu.VMEM((8, 256, 256), BF16),
            pltpu.VMEM((2, 8, 256), F32),
            pltpu.VMEM((nx, 2, 8, 256), F32),
            pltpu.VMEM((2, 256), F32),
            pltpu.VMEM((nx, 2, 256), F32),
            pltpu.VMEM((nx, 3, 8, 256), F32),
            pltpu.VMEM((nx, 3, 8, 256), F32),
            pltpu.VMEM((2, 8 * nx, 256), F32),
            pltpu.VMEM((2, nx, 256), F32),
            pltpu.VMEM((6, 256, 256), BF16),
            pltpu.VMEM((6, 256, 256), BF16),
            pltpu.VMEM((6, 8 * nx, 768), BF16),
            pltpu.VMEM((7, 768, 256), BF16),
            pltpu.VMEM((8, 256, 256), F32),
            pltpu.VMEM((16, 128, 128), F32),
            pltpu.VMEM((4, 256, 256), BF16),
            pltpu.VMEM((4, 256, 256), BF16),
            pltpu.VMEM((3, 16, 128, 32), BF16),
            pltpu.VMEM((512, 128), F32),
            pltpu.VMEM((4, 32, 512), BF16),
            pltpu.VMEM((4, 2, 32, 512), BF16),
            pltpu.VMEM((4, 2, 32, 256), BF16),
            pltpu.VMEM((4, 8, 512), F32),
            pltpu.VMEM((4, 2, 8, 512), F32),
            pltpu.VMEM((4, 2, 8, 256), F32),
            dma((8,)),
            dma((8,)),
            dma((nx, 2)),
            dma((nx, 2)),
            dma((nx,)),
            dma((nx,)),
            dma((nx,)),
            dma((nx,)),
        ],
        compiler_params=pltpu.CompilerParams(
            has_side_effects=True, collective_id=0, vmem_limit_bytes=56 * 1024 * 1024
        ),
        name="multipole",
    )(counts, offsets, charges, jnp.asarray(unit), jnp.asarray(unit_t), cl_up, cl_down, ct_up, ct_down)


def solution(mesh):
    return jax.shard_map(
        shards,
        mesh=mesh,
        in_specs=(
            P(None, "gx", "gy", None, None),
            P("gx", "gy", None, None),
            P("gx", "gy", None),
            P(),
            P(),
            P(),
            P(),
        ),
        out_specs=P("gx", "gy", None, None),
        check_vma=False,
    )
```
